32 devices in a mesh: section: 4 (over y, x), dp: 8 (over z, core).
Axes of the slice: x: 2, y: 2, z: 4, core: 2. Of those that a mesh axis runs over, the one named last changes fastest.
Arguments:
- inputs: bfloat16 [16, 512, 768], P('dp'), may hold values from -6 to 6
- evaluation_input: bfloat16 [16, 512, 768], P('dp'), may hold values from -6 to 6
- output_cotangent: bfloat16 [16, 512, 768], P('dp'), may hold values from -6 to 6
- packed_segment_lengths: int32 [16, 8], P('dp'), may hold values from 1 to 384, 512 in all within a row
- attention_in_weight: bfloat16 [4, 768, 2304], P('section', 'dp'), may hold values from -0.21875 to 0.21875
- attention_out_weight: bfloat16 [4, 768, 768], P('section', 'dp'), may hold values from -0.625 to 0.625
- feedforward_in_weight: bfloat16 [4, 768, 3072], P('section', 'dp'), may hold values from -0.21875 to 0.21875
- feedforward_out_weight: bfloat16 [4, 3072, 768], P('section', 'dp'), may hold values from -0.109375 to 0.109375
- adapter_down_weight: bfloat16 [4, 768, 16], P('section'), may hold values from -0.21875 to 0.21875
- adapter_up_weight: float32 [4, 2, 8, 768], P('section'), may hold values from -1 to 1
- projection_biases: float32 [4, 4, 768], P('section'), may hold values from -3 to 3
- feedforward_bias: float32 [4, 3072], P('section'), may hold values from -3 to 3
- layer_norm_gain: float32 [4, 2, 768], P('section'), may hold values from 0.5 to 1.5
- layer_norm_shift: float32 [4, 2, 768], P('section'), may hold values from -2 to 2
Outputs:
- activations: bfloat16 [4, 16, 512, 768], P('section', 'dp')
- input_grads: bfloat16 [4, 16, 512, 768], P('section', 'dp')
- adapter_grads: float32 [4, 2, 8, 768], P('section')
- joined_outputs: bfloat16 [4, 16, 512, 768], P('section', 'dp')
The draws below stay inside these ranges and needn't reach their ends.
Inputs may be any that keep to these rules, and one draw needn't show every extreme that they name: `packed_segment_lengths`: each row's 8 segment lengths sum to 512, and some row has a segment of exactly 384 tokens.
All inputs are finite; a program needn't handle non-finite values.
Results may differ from the reference program's by a relative error of at most 0.028.
Values may be sent and summed in bfloat16 or wider, within the bound.
No kernel may reach another device: no remote copies, remote signals or barrier semaphores. Data moves between devices by JAX's collectives and lax.ppermute only.
A program may use at most 128 MiB of HBM per device.

```python
import math
import jax
import jax.numpy as jnp
import numpy as np
from jax import lax

MODEL_WIDTH = 768
HEADS = 12
FF = 3072
ADAPTER_RANK = 8
SEQ = 512
NSEG = 8
MOSTSEG = 384
HEAD_DIM = 64
LAYER_COUNT = 4
ROWS = 16


def level_of(rng, dims, split, smallest, largest):
    factor_of = 1.0
    for dim, parts in split:
        heights = jax.random.uniform(jax.random.fold_in(jax.random.fold_in(rng, 6), dim), (parts,), jnp.float32, smallest / len(split), largest / len(split))
        factor_of = factor_of * jnp.repeat(jnp.exp(heights), dims[dim] // parts).reshape((-1,) + (1,) * (len(dims) - 1 - dim))
    return factor_of


def split_up(amount, total, limit, lean):
    portions = [(1 << 20) // math.isqrt(rank ** lean) + 1 for rank in range(2, amount + 1)]
    spare, counts = total - limit - (amount - 1), [1] * (amount - 1)
    while spare > 0:
        movable = [i for i in range(amount - 1) if counts[i] < limit]
        whole, budget = sum([portions[i] for i in movable]), spare
        for i in movable:
            more = min(limit - counts[i], max(1, budget * portions[i] // whole), spare)
            counts[i] = counts[i] + more
            spare = spare - more
    return np.array([limit] + counts)


def uneven_parts(key, amount, total, reach, skew):
    if amount == 2:
        one = jax.random.randint(key, (), max(1, total - reach), min(reach, total - 1) + 1)
        return jnp.stack([one, total - one])
    tallies = jnp.asarray(split_up(amount, total, reach, skew), jnp.int32)
    pairs = (amount - 1) // 2
    source_of, taker = tallies[1:1 + 2 * pairs:2], tallies[2:2 + 2 * pairs:2]
    room = jnp.minimum(source_of - 1, reach - taker)
    moved = jax.random.randint(jax.random.fold_in(key, 1), (pairs,), 0, 1 << 20) % (room + 1)
    tallies = tallies.at[1:1 + 2 * pairs:2].set(source_of - moved).at[2:2 + 2 * pairs:2].set(taker + moved)
    return tallies[jax.random.permutation(jax.random.fold_in(key, 2), amount)]


def centred(stream_key, shape, deviation, bound, cuts=(), kind=jnp.bfloat16):
    values = deviation * jax.random.normal(stream_key, shape, jnp.float32)
    if cuts:
        values = values * level_of(stream_key, shape, cuts, -0.22, 0.18)
    return jnp.clip(values, -bound, bound).astype(kind)


def setup_inputs(seed: int = 0) -> dict:
    seeds = jax.random.split(jax.random.key(seed), 15)
    return {
        "inputs": centred(seeds[0], (ROWS, SEQ, MODEL_WIDTH), 1.0, 6.0, ((0, 8),)),
        "evaluation_input": centred(seeds[1], (ROWS, SEQ, MODEL_WIDTH), 1.0, 6.0, ((0, 8),)),
        "output_cotangent": centred(seeds[2], (ROWS, SEQ, MODEL_WIDTH), 1.0, 6.0, ((0, 8),)),
        "packed_segment_lengths": jax.vmap(lambda own: uneven_parts(own, NSEG, SEQ, MOSTSEG, 2))(jax.random.split(seeds[3], ROWS)).reshape((ROWS, NSEG)).astype(jnp.int32),
        "attention_in_weight": centred(seeds[4], (LAYER_COUNT, MODEL_WIDTH, 3 * MODEL_WIDTH), MODEL_WIDTH ** -0.5, 0.21875, ((0, 4), (1, 8))),
        "attention_out_weight": centred(seeds[5], (LAYER_COUNT, MODEL_WIDTH, MODEL_WIDTH), (MODEL_WIDTH // 8) ** -0.5, 0.625, ((0, 4), (1, 8))),
        "feedforward_in_weight": centred(seeds[6], (LAYER_COUNT, MODEL_WIDTH, FF), MODEL_WIDTH ** -0.5, 0.21875, ((0, 4), (1, 8))),
        "feedforward_out_weight": centred(seeds[7], (LAYER_COUNT, FF, MODEL_WIDTH), FF ** -0.5, 0.109375, ((0, 4), (1, 8))),
        "adapter_down_weight": centred(seeds[8], (LAYER_COUNT, MODEL_WIDTH, 2 * ADAPTER_RANK), MODEL_WIDTH ** -0.5, 0.21875, ((0, 4),)),
        "adapter_up_weight": centred(seeds[9], (LAYER_COUNT, 2, ADAPTER_RANK, MODEL_WIDTH), (4 * ADAPTER_RANK) ** -0.5, 1.0, ((0, 4),), jnp.float32),
        "projection_biases": centred(seeds[10], (LAYER_COUNT, 4, MODEL_WIDTH), 0.5, 3.0, ((0, 4),), jnp.float32),
        "feedforward_bias": centred(seeds[11], (LAYER_COUNT, FF), 0.5, 3.0, ((0, 4),), jnp.float32),
        "layer_norm_gain": jnp.clip(1.0 + 0.1 * jax.random.normal(seeds[12], (LAYER_COUNT, 2, MODEL_WIDTH), jnp.float32), 0.5, 1.5),
        "layer_norm_shift": centred(seeds[13], (LAYER_COUNT, 2, MODEL_WIDTH), 0.3, 2.0, ((0, 4),), jnp.float32),
    }


@jax.custom_vjp
def low_rank_input(v):
    return lax.optimization_barrier(v.astype(jnp.bfloat16)).astype(jnp.float32)

@jax.custom_vjp
def low_rank_gradient(v):
    return v

def low_keep(v):
    return (low_rank_input(v), None)

def low_pass(kept, grad):
    return (grad,)

def back_keep(v):
    return (v, None)

def back_low(kept, grad):
    return (low_rank_input(grad),)
low_rank_input.defvjp(low_keep, low_pass)
low_rank_gradient.defvjp(back_keep, back_low)

def adapter_product(left, right):
    return jnp.matmul(left, right, precision=lax.Precision.HIGHEST)

def normalize(value, gain, shift):
    centered = value - lax.optimization_barrier(jnp.mean(value, axis=-1, keepdims=True))
    spread = lax.optimization_barrier(jnp.mean(centered * centered, axis=-1, keepdims=True))
    return centered * lax.rsqrt(spread + 1e-05) * gain + shift

def segment_labels(lengths):
    ends = jnp.cumsum(lengths, axis=-1)
    places = jnp.arange(SEQ, dtype=jnp.int32)
    return lax.optimization_barrier(jnp.sum((places[None, :, None] >= ends[:, None, :]).astype(jnp.int32), axis=-1))

def attend(query_rows, keys, value_rows, labels):
    scores = jnp.einsum('qhd,khd->hqk', query_rows, keys, precision=lax.Precision.HIGHEST) * HEAD_DIM ** (-0.5)
    scores = low_rank_gradient(scores)
    allowed = labels[:, None] == labels[None, :]
    scores = jnp.where(allowed[None], scores, -1e+30)
    top = lax.optimization_barrier(jnp.max(scores, axis=-1, keepdims=True))
    weights = jnp.exp(scores - top)
    shares = low_rank_input(weights / lax.optimization_barrier(jnp.sum(weights, axis=-1, keepdims=True)))
    return jnp.einsum('hqk,khd->qhd', shares, value_rows, precision=lax.Precision.HIGHEST)

def layer_number(hidden_state, labels, weights, adapter_pair):
    input_weight, w_out, w_up, w_down, bias_rows, ffn_shift, gains, shifts = weights
    length = hidden_state.shape[0]
    packed = adapter_product(hidden_state, input_weight)
    query_rows = packed[:, :MODEL_WIDTH] + bias_rows[0]
    value_rows = packed[:, 2 * MODEL_WIDTH:] + bias_rows[1]
    if adapter_pair is not None:
        adapter_down_slice, adapter_up_slice = adapter_pair
        down_matrix = low_rank_gradient(low_rank_input(adapter_product(hidden_state, adapter_down_slice)))
        query_rows = query_rows + 2.0 * adapter_product(down_matrix[:, :ADAPTER_RANK], low_rank_input(adapter_up_slice[0]))
        value_rows = value_rows + 2.0 * adapter_product(down_matrix[:, ADAPTER_RANK:], low_rank_input(adapter_up_slice[1]))
    query_rows = low_rank_gradient(low_rank_input(query_rows))
    keys = low_rank_gradient(low_rank_input(packed[:, MODEL_WIDTH:2 * MODEL_WIDTH]))
    value_rows = low_rank_gradient(low_rank_input(value_rows))
    split_shape = (length, HEADS, HEAD_DIM)
    mixed = jax.checkpoint(attend)(query_rows.reshape(split_shape), keys.reshape(split_shape), value_rows.reshape(split_shape), labels)
    mixed = low_rank_gradient(low_rank_input(mixed.reshape(length, MODEL_WIDTH)))
    attended = low_rank_gradient(adapter_product(mixed, w_out) + bias_rows[2])
    first = low_rank_input(normalize(hidden_state + attended, gains[0], shifts[0]))
    inner = low_rank_gradient(adapter_product(first, w_up) + ffn_shift)
    activated = low_rank_input(jax.nn.gelu(inner, approximate=False))
    branch = low_rank_gradient(adapter_product(activated, w_down) + bias_rows[3])
    return low_rank_input(normalize(first + branch, gains[1], shifts[1]))

def reference(inputs, evaluation_input, output_cotangent, packed_segment_lengths, attention_in_weight, attention_out_weight, feedforward_in_weight, feedforward_out_weight, adapter_down_weight, adapter_up_weight, projection_biases, feedforward_bias, layer_norm_gain, layer_norm_shift):
    labels = segment_labels(packed_segment_lengths)
    frozen_weights = []
    for layer_index in range(LAYER_COUNT):
        frozen_weights.append((attention_in_weight[layer_index].astype(jnp.float32), attention_out_weight[layer_index].astype(jnp.float32), feedforward_in_weight[layer_index].astype(jnp.float32), feedforward_out_weight[layer_index].astype(jnp.float32), projection_biases[layer_index], feedforward_bias[layer_index], layer_norm_gain[layer_index], layer_norm_shift[layer_index]))
    adapter_down_slice = adapter_down_weight.astype(jnp.float32)

    def network(start, segment_offsets, upper_blocks, row_segment_labels):
        hidden_state = start
        kept = []
        for layer_index in range(LAYER_COUNT):
            hidden_state = layer_number(low_rank_gradient(hidden_state + segment_offsets[layer_index]), row_segment_labels, frozen_weights[layer_index], (adapter_down_slice[layer_index], upper_blocks[layer_index]))
            kept.append(hidden_state)
        return (hidden_state, jnp.stack(kept))

    def train_row(total, row):
        start, cotangent, row_segment_labels = row
        segment_offsets = jnp.zeros((LAYER_COUNT,) + start.shape, jnp.float32)

        def tied_weights(shifted, upper_blocks):
            return network(start, shifted, upper_blocks, row_segment_labels)
        final_output, pullback_function, layer_outputs = jax.vjp(tied_weights, segment_offsets, adapter_up_weight, has_aux=True)
        d_offsets, d_uppers = pullback_function(cotangent)
        return (total + d_uppers, (layer_outputs, d_offsets))
    upper_start_index = jnp.zeros(adapter_up_weight.shape, jnp.float32)
    upper_total, (layer_outputs, d_offsets) = lax.scan(train_row, upper_start_index, (inputs.astype(jnp.float32), output_cotangent.astype(jnp.float32), labels))
    merged_matrix = []
    for layer_index in range(LAYER_COUNT):
        input_weight = frozen_weights[layer_index][0]
        query_columns = low_rank_input(input_weight[:, :MODEL_WIDTH] + 2.0 * adapter_product(adapter_down_slice[layer_index][:, :ADAPTER_RANK], adapter_up_weight[layer_index, 0]))
        value_columns = low_rank_input(input_weight[:, 2 * MODEL_WIDTH:] + 2.0 * adapter_product(adapter_down_slice[layer_index][:, ADAPTER_RANK:], adapter_up_weight[layer_index, 1]))
        merged_matrix.append((jnp.concatenate([query_columns, input_weight[:, MODEL_WIDTH:2 * MODEL_WIDTH], value_columns], axis=1),) + frozen_weights[layer_index][1:])

    def eval_row(carry, row):
        hidden_state, row_segment_labels = row
        kept = []
        for layer_index in range(LAYER_COUNT):
            hidden_state = layer_number(hidden_state, row_segment_labels, merged_matrix[layer_index], None)
            kept.append(hidden_state)
        return (carry, jnp.stack(kept))
    counter = jnp.zeros((), jnp.int32)
    _, joined = lax.scan(eval_row, counter, (evaluation_input.astype(jnp.float32), labels))
    return (jnp.swapaxes(layer_outputs, 0, 1).astype(jnp.bfloat16), jnp.swapaxes(d_offsets, 0, 1).astype(jnp.bfloat16), upper_total, jnp.swapaxes(joined, 0, 1).astype(jnp.bfloat16))
```

```python
import functools

import jax
import jax.numpy as jnp
import numpy as np
from jax import lax
from jax.experimental import pallas as pl
from jax.experimental.pallas import tpu as pltpu
from jax.sharding import PartitionSpec as P

HEADS = 12
norm_eps = 1e-05
masked_score = -1e30
BF = jnp.bfloat16
F32 = jnp.float32
AXES = ("section", "dp")
SHARDS = 8
RING = (0, 1, 3, 2)
PARAM_ROWS = 32
VMEM_BYTES = 60 << 20
PLACES = 9
PARITY, STAGE, OWN_SHARD = 8, 9, 10
RATE_FIRST, RATE_SECOND = 12, 13


def dot(left, right, left_dim=1, right_dim=0):
    return lax.dot_general(
        left, right, (((left_dim,), (right_dim,)), ((), ())), preferred_element_type=F32
    )


def centre_and_scale(value):
    centered = value - jnp.mean(value, axis=-1, keepdims=True)
    spread = jnp.mean(centered * centered, axis=-1, keepdims=True)
    rate = lax.rsqrt(spread + norm_eps)
    return centered * rate, rate


def norm_backward(normal, rate, gain, cotangent):
    q = gain * cotangent
    along = jnp.mean(q * normal, axis=-1, keepdims=True)
    return (q - jnp.mean(q, axis=-1, keepdims=True) - normal * along) * rate


def pack_kernel(
    scal, w_in, w_out, w_up, w_down, down_t, up, biases, inner_bias, gains, shifts, part_a, part_b, mine, rows
):
    depth, width = w_out.shape
    rank = up.shape[1]
    mine[0:4, :] = biases[...]
    for block in range(4):
        mine[4 + block : 5 + block, :] = inner_bias[:, block * width : (block + 1) * width]
    mine[8:10, :] = gains[...]
    mine[10:12, :] = shifts[...]
    down_t32 = down_t[...].astype(F32)
    mine[12:28, :] = down_t32
    mine[28:32, :] = jnp.zeros((4, width), F32)
    rows[:, 0 : 2 * rank] = down_t32.T
    a = rows[pl.ds(pl.multiple_of(scal[OWN_SHARD] * depth, 8), depth), 0 : 2 * rank]
    for block in range(3):
        piece = w_in[:, block * width : (block + 1) * width]
        if block != 1:
            side = block // 2
            extra = a[:, side * rank : side * rank + 1] * up[side, 0:1, :]
            for i in range(1, rank):
                extra = extra + a[:, side * rank + i : side * rank + i + 1] * up[side, i : i + 1, :]
            piece = (piece.astype(F32) + 2.0 * extra).astype(BF)
        part_a[block * depth : (block + 1) * depth, :] = piece
    part_a[3 * depth : 4 * depth, :] = w_out[...]
    for block in range(4):
        piece = w_up[:, block * width : (block + 1) * width]
        if block < 2:
            part_a[(4 + block) * depth : (5 + block) * depth, :] = piece
        else:
            part_b[(block - 2) * depth : (block - 1) * depth, :] = piece
    part_b[2 * depth : 6 * depth, :] = w_down[...]


def pack(scal, w_in, w_out, w_up, w_down, down_t, up, biases, inner_bias, gains, shifts):
    depth, width = w_out.shape
    shape = jax.ShapeDtypeStruct
    part = shape((6 * depth, width), BF)
    smem = pl.BlockSpec(memory_space=pltpu.SMEM)
    vmem = pl.BlockSpec(memory_space=pltpu.VMEM)
    return pl.pallas_call(
        pack_kernel,
        out_shape=(part, part, shape((PARAM_ROWS, width), F32)),
        in_specs=[smem] + [vmem] * 10,
        out_specs=(vmem, vmem, vmem),
        scratch_shapes=[pltpu.VMEM((width, 128), F32)],
        compiler_params=pltpu.CompilerParams(vmem_limit_bytes=VMEM_BYTES),
        name="pack",
    )(scal, w_in, w_out, w_up, w_down, down_t, up, biases, inner_bias, gains, shifts)


def piece_of(pieces, parity, l, step, side, half):
    if step < 3:
        base = 0 if parity == l else 12
        return pieces[base + (step * 2 + side) * 2 + half]
    if l == 0:
        return pieces[24 + (0 if half == parity else 2) + side]
    return pieces[28 + side * 2 + half]


def block_view(w, l, place):
    width = w.shape[2]
    return w.at[l, pl.ds(place * width, (4 if place == 8 else 1) * width)]


def start_block(scal, pieces, w, sem, l, place):
    depth, width = w.shape[2] // 8, w.shape[2]
    half, block = (0, place) if place < 6 else (1, place - 6)
    rows = 4 * depth if place == 8 else depth
    for parity in range(2):

        @pl.when(scal[PARITY] == parity)
        def _():
            for i in range(8):
                source = piece_of(pieces, parity, l, i // 2, i % 2, half)
                at = pl.multiple_of(place * width + rows * scal[i], 16)
                pltpu.make_async_copy(
                    source.at[pl.ds(block * depth, rows)], w.at[l, pl.ds(at, rows)], sem.at[l, place]
                ).start()


def wait_block(w, sem, l, place):
    view = block_view(w, l, place)
    pltpu.make_async_copy(view, view, sem.at[l, place]).wait()


def take_params(scal, mine, theirs, prm):
    prm[scal[PARITY]] = mine[...]
    prm[1 - scal[PARITY]] = theirs[...]


def label_lanes(lens, row, length):
    places = lax.broadcasted_iota(jnp.int32, (length, 1), 0)
    label = jnp.zeros((length, 1), jnp.int32)
    end = jnp.int32(0)
    segments = lens.shape[1]
    for j in range(segments):
        end = end + lens[row, j]
        label = label + (places >= end).astype(jnp.int32)
    lane = lax.broadcasted_iota(jnp.int32, (1, 128), 1) % 64
    same = label == lane
    used = lane <= segments
    query_lanes = jnp.where(same, 1.0, 0.0).astype(BF)
    key_lanes = jnp.where(same | ~used, 0.0, masked_score).astype(BF)
    return query_lanes, key_lanes


def forward_layer(l, lens_lanes, x, w, prm, act, state, ready, after):
    length, width = x.shape[1:]
    quads = width // 256
    lane = lax.broadcasted_iota(jnp.int32, (1, 128), 1)
    value = x[l]
    for place in range(4):
        ready(place)
    after("begin")
    attended = None
    if state is not None:
        qkv, shares, mixed_out, n, gp, r = state
        rates = jnp.zeros((length, 128), F32)
    for quad in range(quads):
        cols = slice(256 * quad, 256 * quad + 256)
        query = (dot(value, w[l, 0:width, cols]) + prm[l, 0:1, cols]).astype(BF)
        keys = dot(value, w[l, width : 2 * width, cols]).astype(BF)
        values = (dot(value, w[l, 2 * width : 3 * width, cols]) + prm[l, 1:2, cols]).astype(BF)
        if state is not None:
            qkv[0, :, cols] = query
            qkv[1, :, cols] = keys
            qkv[2, :, cols] = values
        query_lanes, key_lanes = lens_lanes[0], lens_lanes[1]
        joined = []
        for pair in range(2):
            lanes = slice(128 * pair, 128 * pair + 128)
            scaled = query[:, lanes] * BF(0.125)
            parts = []
            for head in range(2):
                mine = (lane < 64) == (head == 0)
                scores = dot(
                    jnp.where(mine, scaled, query_lanes), jnp.where(mine, keys[:, lanes], key_lanes), 1, 1
                )
                top = jnp.max(scores, axis=1, keepdims=True)
                weights = jnp.exp(scores - top)
                share = weights.astype(BF)
                over = 1.0 / jnp.sum(weights, axis=1, keepdims=True)
                if state is not None:
                    which = quad * 4 + pair * 2 + head
                    shares[which] = share
                    rates = jnp.where(lane == which, over, rates)
                parts.append(dot(share, values[:, lanes]) * over)
            joined.append(jnp.where(lane < 64, parts[0], parts[1]).astype(BF))
        mixed = jnp.concatenate(joined, axis=1)
        if state is not None:
            mixed_out[:, cols] = mixed
        term = dot(mixed, w[l, pl.ds(3 * width + 256 * quad, 256), :])
        attended = term if attended is None else attended + term
        after(quad)
    after("attended")
    summed = value.astype(F32) + (attended + prm[l, 2:3, :])
    normal, rate_first = centre_and_scale(summed)
    first = (normal * prm[l, 8:9, :] + prm[l, 10:11, :]).astype(BF)
    if state is not None:
        n[0] = normal.astype(BF)
    for block in range(4):
        ready(4 + block)
        inner = dot(first, w[l, pl.ds((4 + block) * width, width), :]) + prm[l, 4 + block : 5 + block, :]
        below = 0.5 + 0.5 * lax.erf(inner * (2**-0.5))
        act[block] = (inner * below).astype(BF)
        if state is not None:
            bell = jnp.exp(-0.5 * inner * inner) * 0.3989422804014327
            gp[block] = (below + inner * bell).astype(BF)
        after(("inner", block))
    ready(8)
    branch = None
    for block in range(4):
        term = dot(act[block], w[l, pl.ds((8 + block) * width, width), :])
        branch = term if branch is None else branch + term
    closing = first.astype(F32) + (branch + prm[l, 3:4, :])
    normal, rate_second = centre_and_scale(closing)
    if state is not None:
        n[1] = normal.astype(BF)
        rates = jnp.where(lane == RATE_FIRST, rate_first, rates)
        r[...] = jnp.where(lane == RATE_SECOND, rate_second, rates)
    x[l + 1] = (normal * prm[l, 9:10, :] + prm[l, 11:12, :]).astype(BF)
    after("end")


def backward_layer(l, c_in, c_out, x, w, prm, d_qkv, d_up, state, ready, have, spent, after):
    qkv, shares, mixed, n, gp, r = state
    length, width = x.shape[1:]
    quads = width // 256
    lane = lax.broadcasted_iota(jnp.int32, (1, 128), 1)
    for part in ("n", "r", "gp"):
        have(part)
    ready(8)
    rates = r[...]
    rate_first = rates[:, RATE_FIRST : RATE_FIRST + 1]
    rate_second = rates[:, RATE_SECOND : RATE_SECOND + 1]
    d_closing = norm_backward(n[1].astype(F32), rate_second, prm[l, 9:10, :], c_in[...].astype(F32))
    d_branch = d_closing.astype(BF)
    total = d_closing
    for block in range(4):
        ready(4 + block)
        d_active = dot(d_branch, w[l, pl.ds((8 + block) * width, width), :], 1, 1)
        d_inner = (d_active * gp[block].astype(F32)).astype(BF)
        total = total + dot(d_inner, w[l, pl.ds((4 + block) * width, width), :], 1, 1)
        after(("inner", block))
    spent("gp")
    d_summed = norm_backward(n[0].astype(F32), rate_first, prm[l, 8:9, :], total)
    spent("n")
    ready(3)
    d_mixed = dot(d_summed.astype(BF), w[l, 3 * width : 4 * width, :], 1, 1).astype(BF)
    have("mixed")
    have("qkv")
    for quad in range(quads):
        have(quad)
        for pair in range(2):
            lanes = slice(256 * quad + 128 * pair, 256 * quad + 128 * pair + 128)
            query, keys, values = qkv[0, :, lanes], qkv[1, :, lanes], qkv[2, :, lanes]
            out_rows = d_mixed[:, lanes].astype(F32)
            along = out_rows * mixed[:, lanes].astype(F32)
            query_t = query.T
            d_query, d_keys, d_values = [], [], []
            for head in range(2):
                mine = (lane < 64) == (head == 0)
                which = quad * 4 + pair * 2 + head
                over = rates[:, which : which + 1]
                share = shares[which]
                scaled = jnp.where(mine, out_rows * over, 0.0).astype(BF)
                row_sum = jnp.sum(jnp.where(mine, along, 0.0), axis=1, keepdims=True) * over
                d_score = (share.astype(F32) * (dot(scaled, values, 1, 1) - row_sum)).astype(BF)
                rows = slice(64 * head, 64 * head + 64)
                d_query.append(dot(d_score, keys))
                d_keys.append(dot(query_t[rows], d_score))
                d_values.append(dot(scaled.T[rows], share))
            d_qkv[0, :, lanes] = (jnp.where(lane < 64, d_query[0], d_query[1]) * 0.125).astype(BF)
            d_qkv[1, :, lanes] = (jnp.concatenate(d_keys, axis=0) * 0.125).astype(BF).T
            d_qkv[2, :, lanes] = jnp.concatenate(d_values, axis=0).astype(BF).T
        spent(quad)
        after(quad)
    for part in ("r", "mixed", "qkv"):
        spent(part)
    have("x")
    down = dot(x[l], prm[l, 12:28, :].astype(BF), 1, 1).astype(BF)
    rank = down.shape[1] // 2
    d_up[l, 0:rank, :] = 2.0 * dot(down, d_qkv[0], 0, 0)[0:rank]
    d_up[l, rank : 2 * rank, :] = 2.0 * dot(down, d_qkv[2], 0, 0)[rank:]
    total = d_summed
    for kind in range(3):
        ready(kind)
        total = total + dot(d_qkv[kind], w[l, kind * width : (kind + 1) * width, :], 1, 1)
    c_out[...] = total.astype(BF)


def state_shapes(length, width):
    return [
        ((3, length, width), BF),
        ((HEADS, length, length), BF),
        ((length, width), BF),
        ((2, length, width), BF),
        ((4, length, width), BF),
        ((length, 128), F32),
    ]


def state_copy(state, kept, sem, l, part, load):
    if isinstance(part, int):
        inside, outside = state[1].at[pl.ds(4 * part, 4)], kept[1].at[l, pl.ds(4 * part, 4)]
        which = 5 + part
    else:
        i = {"qkv": 0, "mixed": 2, "n": 3, "gp": 4, "r": 5}[part]
        inside, outside = state[i], kept[i].at[l]
        which = {0: 0, 2: 1, 3: 2, 4: 3, 5: 4}[i]
    ends = (outside, inside) if load else (inside, outside)
    return pltpu.make_async_copy(*ends, sem.at[which])


EARLY_PARTS = ("qkv", "mixed", 0, 1, 2)
LATE_PARTS = ("n", "gp", "r")


def save_calls(state, kept, sem, l):
    def after(point):
        if point == "begin":

            @pl.when(l > 0)
            def _():
                for part in EARLY_PARTS:
                    state_copy(state, kept, sem, 0, part, False).wait()

        if point == "attended":

            @pl.when(l > 0)
            def _():
                for part in LATE_PARTS:
                    state_copy(state, kept, sem, 0, part, False).wait()

    return after


def first_kernel(scal, lens, source, mine, theirs, *refs):
    pieces, refs = refs[:32], refs[32:]
    w_all, out_first, out_second = refs[:3]
    kept, refs = refs[3:9], refs[9:]
    x, w, prm, lanes, act, wsem, osem, xsem, hsem, ssem = refs[:10]
    state = refs[10:]
    parity, stage = scal[PARITY], scal[STAGE]

    def out_copy(l, place):
        return pltpu.make_async_copy(block_view(w, l, place), block_view(w_all, l, place), osem.at[l, place])

    for place in range(4):
        start_block(scal, pieces, w, wsem, 0, place)

    @pl.when(stage != 0)
    def _():
        for l in range(2):
            for place in range(PLACES):
                if l or place > 3:
                    start_block(scal, pieces, w, wsem, l, place)
        for l in range(2):
            for place in range(PLACES):
                wait_block(w, wsem, l, place)
                out_copy(l, place).start()

    @pl.when(stage == 0)
    def _():
        fresh = pltpu.make_async_copy(source.at[parity], x.at[0], xsem)
        fresh.start()
        take_params(scal, mine, theirs, prm)
        query_lanes, key_lanes = label_lanes(lens, parity, x.shape[1])
        lanes[0] = query_lanes
        lanes[1] = key_lanes
        fresh.wait()

        def layer(l, carry):
            def ready(place):
                wait_block(w, wsem, l, place)
                out_copy(l, place).start()

            waits = save_calls(state, kept, ssem, l)

            def ahead(places, own):
                for i in range(2):
                    if own or i == 0:

                        @pl.when(l == i)
                        def _():
                            for place in places:
                                start_block(scal, pieces, w, wsem, i if own else 1, place)

            def after(point):
                waits(point)
                if point == 0:
                    ahead((4, 5), True)
                if point == 1:
                    ahead((6, 7), True)
                if point == 2:
                    ahead((8,), True)
                if point == "attended":
                    for part in EARLY_PARTS:
                        state_copy(state, kept, ssem, l, part, False).start()
                if isinstance(point, tuple):
                    ahead((point[1],), False)
                if point == "end":
                    for part in LATE_PARTS:
                        state_copy(state, kept, ssem, l, part, False).start()

            forward_layer(l, lanes, x, w, prm, act, state, ready, after)
            return carry

        lax.fori_loop(0, 2, layer, 0)
        outs = [
            pltpu.make_async_copy(x.at[1], out_first, hsem.at[0]),
            pltpu.make_async_copy(x.at[2], out_second, hsem.at[1]),
        ]
        for copy in outs:
            copy.start()
        for part in EARLY_PARTS + LATE_PARTS:
            state_copy(state, kept, ssem, 1, part, False).wait()
        for copy in outs:
            copy.wait()

    for l in range(2):
        for place in range(PLACES):
            out_copy(l, place).wait()


def load_weights(w_all, w, wsem, l, places):
    for place in places:
        pltpu.make_async_copy(block_view(w_all, l, place), block_view(w, l, place), wsem.at[l, place]).start()


def load_ahead(w_all, w, wsem, l, point):
    own = {"begin": (4,), 0: (5, 6), 1: (7,), 2: (8,)}.get(point, ())
    load_weights(w_all, w, wsem, l, own)
    if isinstance(point, tuple):

        @pl.when(l == 0)
        def _():
            load_weights(w_all, w, wsem, 1, (point[1],))


def middle_kernel(scal, lens, source, arrived, cotangent, early_first, early_second, mine, theirs, w_all, *refs):
    hop_up, hop_down, acts, acts_other, second, second_other, d_up = refs[:7]
    kept, refs = refs[7:13], refs[13:]
    x, w, prm, lanes, act, c, wsem, xsem, hsem, ssem = refs[:10]
    state = refs[10:]
    parity, stage = scal[PARITY], scal[STAGE]
    load_weights(w_all, w, wsem, 0, range(4))
    d_up[...] = jnp.zeros(d_up.shape, F32)
    take_params(scal, mine, theirs, prm)
    query_lanes, key_lanes = label_lanes(lens, parity, x.shape[1])
    lanes[0] = query_lanes
    lanes[1] = key_lanes

    def placed(first, last, own, other, at):
        for p in range(2):

            @pl.when(parity == p)
            def _():
                ends = (first, last) if p == 0 else (last, first)
                pltpu.make_async_copy(ends[0], own.at[p], hsem.at[at]).start()
                pltpu.make_async_copy(ends[1], other, hsem.at[at + 1]).start()

    def placed_wait(own, other, at):
        pltpu.make_async_copy(own.at[0], own.at[0], hsem.at[at]).wait()
        pltpu.make_async_copy(other, other, hsem.at[at + 1]).wait()

    def both(copies):
        for copy in copies:
            copy.start()
        for copy in copies:
            copy.wait()

    @pl.when(stage == 0)
    def _():
        both(
            [
                pltpu.make_async_copy(source.at[parity], x.at[0], xsem.at[0]),
                pltpu.make_async_copy(early_first, c.at[0], xsem.at[1]),
                pltpu.make_async_copy(early_second, c.at[1], xsem.at[2]),
            ]
        )
        placed(c.at[0], c.at[1], acts, acts_other, 0)

    @pl.when(stage != 0)
    def _():
        both(
            [
                pltpu.make_async_copy(arrived, x.at[0], xsem.at[0]),
                pltpu.make_async_copy(cotangent.at[parity], c.at[0], xsem.at[1]),
            ]
        )

    def layer(l, carry):
        def ready(place):
            wait_block(w, wsem, l, place)

        waits = save_calls(state, kept, ssem, l)

        def after(point):
            waits(point)
            load_ahead(w_all, w, wsem, l, point)
            if point in ("attended", "end"):

                @pl.when(l == 0)
                def _():
                    for part in EARLY_PARTS if point == "attended" else LATE_PARTS:
                        state_copy(state, kept, ssem, 0, part, False).start()

        forward_layer(l, lanes, x, w, prm, act, state, ready, after)
        return carry

    lax.fori_loop(0, 2, layer, 0)

    @pl.when(stage == 0)
    def _():
        up = pltpu.make_async_copy(x.at[2], hop_up, xsem.at[0])
        up.start()
        placed(x.at[1], x.at[2], second, second_other, 2)
        up.wait()

    @pl.when(stage != 0)
    def _():
        placed(x.at[1], x.at[2], acts, acts_other, 0)

        def gradient(i, carry):
            l = 1 - i

            def have(part):
                if part != "x":

                    @pl.when(i > 0)
                    def _():
                        state_copy(state, kept, ssem, 0, part, True).wait()

            def spent(part):
                @pl.when(i == 0)
                def _():
                    state_copy(state, kept, ssem, 0, part, True).start()

            backward_layer(
                l, c.at[i], c.at[1 - i], x, w, prm, act, d_up, state, lambda place: None, have, spent, lambda point: None
            )
            return carry

        lax.fori_loop(0, 2, gradient, 0)
        down = pltpu.make_async_copy(c.at[0], hop_down, xsem.at[0])
        down.start()
        placed(c.at[0], c.at[1], second, second_other, 2)
        down.wait()

    placed_wait(acts, acts_other, 0)
    placed_wait(second, second_other, 2)


def last_kernel(scal, lens, source, arrived_up, arrived_down, early_first, second, mine, theirs, w_all, *refs):
    kept, refs = refs[:6], refs[6:]
    joined, grads, other, d_up = refs[:4]
    x, w, prm, lanes, act, c, wsem, xsem, hsem, ssem = refs[4:14]
    state = refs[14:]
    parity, stage = scal[PARITY], scal[STAGE]
    take_params(scal, mine, theirs, prm)
    d_up[...] = jnp.zeros(d_up.shape, F32)

    def carry_in(room):
        return pltpu.make_async_copy(second.at[parity], room, hsem.at[3])

    def carry_out(room, earlier):
        return pltpu.make_async_copy(room, earlier.at[parity], hsem.at[2])

    def finish(first, last, own):
        for p in range(2):

            @pl.when(parity == p)
            def _():
                ends = (first, last) if p == 0 else (last, first)
                copies = [
                    pltpu.make_async_copy(ends[1], other, hsem.at[1]),
                    pltpu.make_async_copy(ends[0], own.at[p], hsem.at[0]),
                ]
                for copy in copies:
                    copy.start()
                for copy in copies:
                    copy.wait()

    @pl.when(stage == 0)
    def _():
        def load(l, part):
            return state_copy(state, kept, ssem, l, part, True)

        cot = pltpu.make_async_copy(arrived_down, c.at[0], xsem.at[0])
        start_x = pltpu.make_async_copy(source.at[parity], x.at[0], xsem.at[1])
        middle_x = pltpu.make_async_copy(early_first, x.at[1], xsem.at[2])
        cot.start()
        for part in ("n", "r"):
            load(1, part).start()
        load_weights(w_all, w, wsem, 1, (8,))
        load(1, "gp").start()
        load_weights(w_all, w, wsem, 1, (4, 5))
        cot.wait()

        def gradient(i, carry):
            l = 1 - i

            def have(part):
                if part != "x":
                    load(0, part).wait()
                    return

                @pl.when(i == 0)
                def _():
                    start_x.wait()
                    middle_x.wait()

            def spent(part):
                @pl.when(i == 0)
                def _():
                    load(0, part).start()

            def ready(place):
                wait_block(w, wsem, l, place)

            def after(point):
                key = point[1] if isinstance(point, tuple) else point + 4
                load_weights(w_all, w, wsem, l, ((6,), (7,), (3,), (), (0,), (1, 2), ())[key])

                @pl.when(i == 0)
                def _():
                    for part in (("mixed",), ("qkv",), (0,), (1,), (2,), (), ())[key]:
                        load(1, part).start()
                    if key == 4:
                        carry_in(x.at[2]).start()
                        start_x.start()
                        middle_x.start()
                    if key == 5:
                        load_weights(w_all, w, wsem, 0, (8,))
                        carry_in(x.at[2]).wait()
                        carry_out(x.at[2], joined).start()
                    if key == 6:
                        load_weights(w_all, w, wsem, 0, (4, 5))

            backward_layer(l, c.at[i], c.at[1 - i], x, w, prm, act, d_up, state, ready, have, spent, after)
            return carry

        lax.fori_loop(0, 2, gradient, 0)
        finish(c.at[0], c.at[1], grads)
        carry_out(x.at[2], joined).wait()

    @pl.when(stage != 0)
    def _():
        load_weights(w_all, w, wsem, 0, range(4))
        query_lanes, key_lanes = label_lanes(lens, parity, x.shape[1])
        lanes[0] = query_lanes
        lanes[1] = key_lanes
        copy = pltpu.make_async_copy(arrived_up, x.at[0], xsem.at[0])
        copy.start()
        copy.wait()
        carry_in(c.at[0]).start()
        carry_in(c.at[0]).wait()
        carry_out(c.at[0], grads).start()

        def layer(l, carry):
            forward_layer(
                l,
                lanes,
                x,
                w,
                prm,
                act,
                None,
                lambda place: wait_block(w, wsem, l, place),
                lambda point: load_ahead(w_all, w, wsem, l, point),
            )
            return carry

        lax.fori_loop(0, 2, layer, 0)
        finish(x.at[1], x.at[2], joined)
        carry_out(c.at[0], grads).wait()


def common_scratch(length, width, rows, extra):
    return (
        [
            pltpu.VMEM((3, length, width), BF),
            pltpu.VMEM((2, 12 * width, width), BF),
            pltpu.VMEM((2, PARAM_ROWS, width), F32),
            pltpu.VMEM((2, length, 128), BF),
            pltpu.VMEM((4, length, width), BF),
        ]
        + extra
        + [
            pltpu.SemaphoreType.DMA((3,)),
            pltpu.SemaphoreType.DMA((4,)),
            pltpu.SemaphoreType.DMA((8,)),
        ]
        + [pltpu.VMEM(dims, kind) for dims, kind in state_shapes(length, width)]
    )


def layers_cost(length, width, forwards, backwards):
    dense = 2 * length * width * width * 12
    heads = 2 * length * length * width
    return pl.CostEstimate(
        flops=2 * (forwards * (dense + 2 * heads) + backwards * (dense + 5 * heads)),
        bytes_accessed=2 * 12 * width * width * 2,
        transcendentals=0,
    )


def run_first(scal, lens, source, mine, theirs, pieces):
    _, length, width = source.shape
    shape = jax.ShapeDtypeStruct
    anywhere = pl.BlockSpec(memory_space=pl.ANY)
    smem = pl.BlockSpec(memory_space=pltpu.SMEM)
    vmem = pl.BlockSpec(memory_space=pltpu.VMEM)
    row = shape((length, width), BF)
    outs = [shape((2, 12 * width, width), BF), row, row]
    outs += [shape((2,) + dims, kind) for dims, kind in state_shapes(length, width)]
    scratch = common_scratch(
        length, width, 2, [pltpu.SemaphoreType.DMA((2, PLACES)), pltpu.SemaphoreType.DMA((2, PLACES))]
    )
    scratch[7] = pltpu.SemaphoreType.DMA
    return pl.pallas_call(
        first_kernel,
        out_shape=outs,
        in_specs=[smem, smem, anywhere, vmem, vmem] + [anywhere] * 32,
        out_specs=[anywhere] * len(outs),
        scratch_shapes=scratch,
        compiler_params=pltpu.CompilerParams(vmem_limit_bytes=VMEM_BYTES),
        cost_estimate=layers_cost(length, width, 1, 0),
        name="first",
    )(scal, lens, source, mine, theirs, *pieces)


def run_middle(scal, lens, source, arrived, cotangent, early_first, early_second, mine, theirs, w_all):
    _, length, width = source.shape
    shape = jax.ShapeDtypeStruct
    anywhere = pl.BlockSpec(memory_space=pl.ANY)
    smem = pl.BlockSpec(memory_space=pltpu.SMEM)
    vmem = pl.BlockSpec(memory_space=pltpu.VMEM)
    row, rows = shape((length, width), BF), shape((2, length, width), BF)
    outs = [row, row, rows, row, rows, row, shape((2, 16, width), F32)]
    outs += [shape((1,) + dims, kind) for dims, kind in state_shapes(length, width)]
    return pl.pallas_call(
        middle_kernel,
        out_shape=outs,
        in_specs=[smem, smem] + [anywhere] * 5 + [vmem, vmem, anywhere],
        out_specs=[anywhere] * 6 + [vmem] + [anywhere] * 6,
        scratch_shapes=common_scratch(
            length,
            width,
            2,
            [pltpu.VMEM((2, length, width), BF), pltpu.SemaphoreType.DMA((2, PLACES))],
        ),
        compiler_params=pltpu.CompilerParams(vmem_limit_bytes=VMEM_BYTES),
        cost_estimate=layers_cost(length, width, 1, 1),
        name="middle",
    )(scal, lens, source, arrived, cotangent, early_first, early_second, mine, theirs, w_all)


def run_last(scal, lens, source, arrived_up, arrived_down, early_first, second, mine, theirs, w_all, kept):
    _, length, width = source.shape
    shape = jax.ShapeDtypeStruct
    anywhere = pl.BlockSpec(memory_space=pl.ANY)
    smem = pl.BlockSpec(memory_space=pltpu.SMEM)
    vmem = pl.BlockSpec(memory_space=pltpu.VMEM)
    row, rows = shape((length, width), BF), shape((2, length, width), BF)
    return pl.pallas_call(
        last_kernel,
        out_shape=[rows, rows, row, shape((2, 16, width), F32)],
        in_specs=[smem, smem] + [anywhere] * 5 + [vmem, vmem] + [anywhere] * 7,
        out_specs=[anywhere] * 3 + [vmem],
        scratch_shapes=common_scratch(
            length,
            width,
            2,
            [pltpu.VMEM((2, length, width), BF), pltpu.SemaphoreType.DMA((2, PLACES))],
        ),
        compiler_params=pltpu.CompilerParams(vmem_limit_bytes=VMEM_BYTES),
        cost_estimate=layers_cost(length, width, 0, 1),
        name="last",
    )(scal, lens, source, arrived_up, arrived_down, early_first, second, mine, theirs, w_all, *kept)


def tables(sections, copies):
    group = copies // SHARDS
    out = np.zeros((sections * copies, 12), np.int32)
    for s in range(sections):
        for d in range(copies):
            shard = d // group
            place, side = RING.index(shard // 2), shard % 2
            row = out[s * copies + d]
            for step in range(4):
                node = RING[(place - step) % 4]
                row[2 * step], row[2 * step + 1] = 2 * node + side, 2 * node + 1 - side
            row[PARITY], row[STAGE], row[OWN_SHARD] = s % 2, s // 2, shard
    return out


def body(
    inputs,
    evaluation_input,
    output_cotangent,
    packed_segment_lengths,
    attention_in_weight,
    attention_out_weight,
    feedforward_in_weight,
    feedforward_out_weight,
    adapter_down_weight,
    adapter_up_weight,
    projection_biases,
    feedforward_bias,
    layer_norm_gain,
    layer_norm_shift,
):
    sections, copies = lax.axis_size("section"), lax.axis_size("dp")
    group = copies // SHARDS
    section, place = lax.axis_index("section"), lax.axis_index("dp")
    even = section % 2 == 0
    scal = lax.dynamic_index_in_dim(
        jnp.asarray(tables(sections, copies)), section * copies + place, 0, keepdims=False
    )

    def permuted(array, move):
        pairs = []
        for s in range(sections):
            for d in range(copies):
                target = move(s, d // group)
                if target is not None:
                    pairs.append((s * copies + d, target[0] * copies + target[1] * group + d % group))
        return lax.ppermute(array, AXES, pairs)

    ring_next = {RING[i]: RING[(i + 1) % 4] for i in range(4)}
    ring_last = {RING[i]: RING[i - 1] for i in range(4)}
    along = lambda s, q: (s, ring_next[q // 2] * 2 + q % 2)
    against = lambda s, q: (s, ring_last[q // 2] * 2 + q % 2)
    other_side = lambda s, q: (s, q ^ 1)
    partner = lambda s, q: (s ^ 1, q)
    upward = lambda s, q: (s + 2, q) if s < 2 else None
    downward = lambda s, q: (s - 2, q) if s >= 2 else None

    w_in, w_out, w_up, w_down = (
        attention_in_weight[0],
        attention_out_weight[0],
        feedforward_in_weight[0],
        feedforward_out_weight[0],
    )
    if group > 1:
        groups = [[q * group + i for i in range(group)] for q in range(SHARDS)]
        w_in, w_out, w_up, w_down = (
            lax.all_gather(piece, "dp", axis=0, tiled=True, axis_index_groups=groups)
            for piece in (w_in, w_out, w_up, w_down)
        )
    part_a, part_b, mine = pack(
        scal,
        w_in,
        w_out,
        w_up,
        w_down,
        adapter_down_weight[0].T,
        adapter_up_weight[0],
        projection_biases[0],
        feedforward_bias,
        layer_norm_gain[0],
        layer_norm_shift[0],
    )

    def held_back(array, until):
        return lax.optimization_barrier((array, until))[0]

    r0 = [part_a, part_b]
    x0, r1 = [None, None], [None, None]
    for half in range(2):
        x0[half] = permuted(r0[half], partner)
        r1[half] = permuted(r0[half], along)
    x1, r2 = [None, None], [None, None]
    for half in range(2):
        x1[half] = permuted(held_back(r1[half], x0[half]), partner)
        r2[half] = permuted(r1[half], along)
    z_first = permuted(held_back(jnp.where(even, r0[0], x0[1]), r2[0]), against)
    x2, z_second = [None, None], [None, None]
    for half in range(2):
        x2[half] = permuted(held_back(r2[half], x1[half]), partner)
        second_layer = jnp.where(even, x0[half], r0[half])
        z_second[half] = permuted(held_back(second_layer, z_first if half else r2[1]), against)
    x_first = permuted(held_back(z_first, x2[0]), partner)
    theirs = permuted(held_back(mine, r1[0]), partner)

    def swapped(halves):
        return halves + [permuted(half, other_side) for half in halves]

    pieces = []
    for halves in (r0, r1, r2, x0, x1, x2, [z_first], [x_first], z_second):
        pieces += swapped(halves)

    lens = packed_segment_lengths
    w_all, early_first, early_second, *kept = run_first(scal, lens, inputs, mine, theirs, pieces)
    arrived = permuted(early_second, upward)
    hop_up, hop_down, acts, acts_other, second, second_other, d_up_late, *_ = run_middle(
        scal,
        lens,
        evaluation_input,
        arrived,
        output_cotangent,
        early_first,
        early_second,
        mine,
        theirs,
        w_all,
    )
    arrived_down = permuted(hop_down, downward)
    arrived_up = permuted(hop_up, upward)
    acts_row = permuted(acts_other, partner)
    second_row = permuted(second_other, partner)
    joined, grads, last_other, d_up_early = run_last(
        scal, lens, inputs, arrived_up, arrived_down, early_first, second, mine, theirs, w_all, kept
    )
    last_other, d_up_early, acts_row, second_row = lax.optimization_barrier(
        (last_other, d_up_early, acts_row, second_row)
    )
    last_row = permuted(last_other, partner)
    early = section < 2
    row = 1 - section % 2

    def settled(rows, arrived_row):
        return lax.dynamic_update_slice(rows, arrived_row[None], (row, 0, 0))[None]

    activations = settled(acts, acts_row)
    joined = settled(joined, jnp.where(early, second_row, last_row))
    grads = settled(grads, jnp.where(early, last_row, second_row))

    total = jnp.where(early, d_up_early, d_up_late)
    step = 1
    while step < copies:
        total = total + lax.ppermute(total, "dp", [(d, d ^ step) for d in range(copies)])
        step *= 2
    total = jnp.where(even, total[0], total[1]) + permuted(jnp.where(even, total[1], total[0]), partner)
    total = total.reshape((1, 2, total.shape[0] // 2, total.shape[1]))
    return (activations, grads, total, joined)


def solution(mesh):
    in_specs = (
        P("dp", None, None),
        P("dp", None, None),
        P("dp", None, None),
        P("dp", None),
        P("section", "dp", None),
        P("section", "dp", None),
        P("section", "dp", None),
        P("section", "dp", None),
        P("section", None, None),
        P("section", None, None, None),
        P("section", None, None),
        P("section", None),
        P("section", None, None),
        P("section", None, None),
    )
    out_specs = (
        P("section", "dp", None, None),
        P("section", "dp", None, None),
        P("section", None, None, None),
        P("section", "dp", None, None),
    )
    return jax.shard_map(body, mesh=mesh, in_specs=in_specs, out_specs=out_specs, check_vma=False)
```

```python
import functools

import jax
import jax.numpy as jnp
import numpy as np
from jax import lax
from jax.experimental import pallas as pl
from jax.experimental.pallas import tpu as pltpu
from jax.sharding import PartitionSpec as P

HEADS = 12
norm_eps = 1e-05
masked_score = -1e30
BF = jnp.bfloat16
F32 = jnp.float32
AXES = ("section", "dp")
SHARDS = 8
RING = (0, 1, 3, 2)
PARAM_ROWS = 32
VMEM_BYTES = 62 << 20
PLACES = 9
PARITY, STAGE, OWN_SHARD = 8, 9, 10
RATE_FIRST, RATE_SECOND = 12, 13


def dot(left, right, left_dim=1, right_dim=0):
    return lax.dot_general(
        left, right, (((left_dim,), (right_dim,)), ((), ())), preferred_element_type=F32
    )


def centre_and_scale(value):
    centered = value - jnp.mean(value, axis=-1, keepdims=True)
    spread = jnp.mean(centered * centered, axis=-1, keepdims=True)
    rate = lax.rsqrt(spread + norm_eps)
    return centered * rate, rate


def norm_backward(normal, rate, gain, cotangent):
    q = gain * cotangent
    along = jnp.mean(q * normal, axis=-1, keepdims=True)
    return (q - jnp.mean(q, axis=-1, keepdims=True) - normal * along) * rate


def pack_kernel(
    scal, w_in, w_out, w_up, w_down, down_t, up, biases, inner_bias, gains, shifts, part_a, part_b, mine, rows
):
    depth, width = w_out.shape
    rank = up.shape[1]
    mine[0:4, :] = biases[...]
    for block in range(4):
        mine[4 + block : 5 + block, :] = inner_bias[:, block * width : (block + 1) * width]
    mine[8:10, :] = gains[...]
    mine[10:12, :] = shifts[...]
    down_t32 = down_t[...].astype(F32)
    mine[12:28, :] = down_t32
    mine[28:32, :] = jnp.zeros((4, width), F32)
    rows[:, 0 : 2 * rank] = down_t32.T
    a = rows[pl.ds(pl.multiple_of(scal[OWN_SHARD] * depth, 8), depth), 0 : 2 * rank]
    for block in range(3):
        piece = w_in[:, block * width : (block + 1) * width]
        if block != 1:
            side = block // 2
            extra = a[:, side * rank : side * rank + 1] * up[side, 0:1, :]
            for i in range(1, rank):
                extra = extra + a[:, side * rank + i : side * rank + i + 1] * up[side, i : i + 1, :]
            piece = (piece.astype(F32) + 2.0 * extra).astype(BF)
        part_a[block * depth : (block + 1) * depth, :] = piece
    part_a[3 * depth : 4 * depth, :] = w_out[...]
    for block in range(4):
        piece = w_up[:, block * width : (block + 1) * width]
        if block < 2:
            part_a[(4 + block) * depth : (5 + block) * depth, :] = piece
        else:
            part_b[(block - 2) * depth : (block - 1) * depth, :] = piece
    part_b[2 * depth : 6 * depth, :] = w_down[...]


def pack(scal, w_in, w_out, w_up, w_down, down_t, up, biases, inner_bias, gains, shifts):
    depth, width = w_out.shape
    shape = jax.ShapeDtypeStruct
    part = shape((6 * depth, width), BF)
    smem = pl.BlockSpec(memory_space=pltpu.SMEM)
    vmem = pl.BlockSpec(memory_space=pltpu.VMEM)
    return pl.pallas_call(
        pack_kernel,
        out_shape=(part, part, shape((PARAM_ROWS, width), F32)),
        in_specs=[smem] + [vmem] * 10,
        out_specs=(vmem, vmem, vmem),
        scratch_shapes=[pltpu.VMEM((width, 128), F32)],
        compiler_params=pltpu.CompilerParams(vmem_limit_bytes=VMEM_BYTES),
        name="pack",
    )(scal, w_in, w_out, w_up, w_down, down_t, up, biases, inner_bias, gains, shifts)


def piece_of(pieces, parity, l, step, side, half):
    if step < 3:
        base = 0 if parity == l else 12
        return pieces[base + (step * 2 + side) * 2 + half]
    if l == 0:
        return pieces[24 + (0 if half == parity else 2) + side]
    return pieces[28 + side * 2 + half]


def block_view(w, l, place):
    width = w.shape[2]
    return w.at[l, pl.ds(place * width, (4 if place == 8 else 1) * width)]


def start_block(scal, pieces, w, sem, l, place):
    depth, width = w.shape[2] // 8, w.shape[2]
    half, block = (0, place) if place < 6 else (1, place - 6)
    rows = 4 * depth if place == 8 else depth
    for parity in range(2):

        @pl.when(scal[PARITY] == parity)
        def _():
            for i in range(8):
                source = piece_of(pieces, parity, l, i // 2, i % 2, half)
                at = pl.multiple_of(place * width + rows * scal[i], 16)
                pltpu.make_async_copy(
                    source.at[pl.ds(block * depth, rows)], w.at[l, pl.ds(at, rows)], sem.at[l, place]
                ).start()


def wait_block(w, sem, l, place):
    view = block_view(w, l, place)
    pltpu.make_async_copy(view, view, sem.at[l, place]).wait()


def take_params(scal, mine, theirs, prm):
    prm[scal[PARITY]] = mine[...]
    prm[1 - scal[PARITY]] = theirs[...]


def label_lanes(lens, row, length):
    places = lax.broadcasted_iota(jnp.int32, (length, 1), 0)
    label = jnp.zeros((length, 1), jnp.int32)
    end = jnp.int32(0)
    segments = lens.shape[1]
    for j in range(segments):
        end = end + lens[row, j]
        label = label + (places >= end).astype(jnp.int32)
    lane = lax.broadcasted_iota(jnp.int32, (1, 128), 1) % 64
    same = label == lane
    used = lane <= segments
    query_lanes = jnp.where(same, 1.0, 0.0).astype(BF)
    key_lanes = jnp.where(same | ~used, 0.0, masked_score).astype(BF)
    return query_lanes, key_lanes


def forward_layer(l, lens_lanes, x, w, prm, act, state, ready, after):
    length, width = x.shape[1:]
    quads = width // 256
    lane = lax.broadcasted_iota(jnp.int32, (1, 128), 1)
    value = x[l]
    for place in range(4):
        ready(place)
    after("begin")
    attended = None
    if state is not None:
        qkv, shares, mixed_out, n, gp, r = state
        rates = jnp.zeros((length, 128), F32)
    for quad in range(quads):
        cols = slice(256 * quad, 256 * quad + 256)
        query = (dot(value, w[l, 0:width, cols]) + prm[l, 0:1, cols]).astype(BF)
        keys = dot(value, w[l, width : 2 * width, cols]).astype(BF)
        values = (dot(value, w[l, 2 * width : 3 * width, cols]) + prm[l, 1:2, cols]).astype(BF)
        if state is not None:
            qkv[0, :, cols] = query
            qkv[1, :, cols] = keys
            qkv[2, :, cols] = values
        query_lanes, key_lanes = lens_lanes[0], lens_lanes[1]
        joined = []
        for pair in range(2):
            lanes = slice(128 * pair, 128 * pair + 128)
            scaled = query[:, lanes] * BF(0.125)
            parts = []
            for head in range(2):
                mine = (lane < 64) == (head == 0)
                scores = dot(
                    jnp.where(mine, scaled, query_lanes), jnp.where(mine, keys[:, lanes], key_lanes), 1, 1
                )
                top = jnp.max(scores, axis=1, keepdims=True)
                weights = jnp.exp(scores - top)
                share = weights.astype(BF)
                part = dot(share, jnp.where(mine, values[:, lanes], BF(1)))
                other = 64 - 64 * head
                over = 1.0 / part[:, other : other + 1]
                if state is not None:
                    which = quad * 4 + pair * 2 + head
                    shares[which] = share
                    rates = jnp.where(lane == which, over, rates)
                parts.append(part * over)
            joined.append(jnp.where(lane < 64, parts[0], parts[1]))
            if state is not None:
                mixed_out[:, 256 * quad + 128 * pair : 256 * quad + 128 * pair + 128] = joined[pair]
        mixed = jnp.concatenate(joined, axis=1).astype(BF)
        term = dot(mixed, w[l, pl.ds(3 * width + 256 * quad, 256), :])
        attended = term if attended is None else attended + term
        after(quad)
    after("attended")
    summed = value.astype(F32) + (attended + prm[l, 2:3, :])
    normal, rate_first = centre_and_scale(summed)
    first = (normal * prm[l, 8:9, :] + prm[l, 10:11, :]).astype(BF)
    if state is not None:
        n[0] = normal.astype(BF)
    for block in range(4):
        ready(4 + block)
        inner = dot(first, w[l, pl.ds((4 + block) * width, width), :]) + prm[l, 4 + block : 5 + block, :]
        below = 0.5 + 0.5 * lax.erf(inner * (2**-0.5))
        act[block] = (inner * below).astype(BF)
        if state is not None:
            bell = jnp.exp(-0.5 * inner * inner) * 0.3989422804014327
            gp[block] = (below + inner * bell).astype(BF)
        after(("inner", block))
    ready(8)
    branch = None
    for block in range(4):
        term = dot(act[block], w[l, pl.ds((8 + block) * width, width), :])
        branch = term if branch is None else branch + term
    closing = first.astype(F32) + (branch + prm[l, 3:4, :])
    normal, rate_second = centre_and_scale(closing)
    if state is not None:
        n[1] = normal.astype(BF)
        rates = jnp.where(lane == RATE_FIRST, rate_first, rates)
        r[...] = jnp.where(lane == RATE_SECOND, rate_second, rates)
    x[l + 1] = (normal * prm[l, 9:10, :] + prm[l, 11:12, :]).astype(BF)
    after("end")


def backward_layer(l, c_in, c_out, x, w, prm, d_qkv, d_up, state, ready, have, spent, after):
    qkv, shares, mixed, n, gp, r = state
    length, width = x.shape[1:]
    quads = width // 256
    lane = lax.broadcasted_iota(jnp.int32, (1, 128), 1)
    for part in ("n", "r", "gp"):
        have(part)
    ready(8)
    rates = r[...]
    rate_first = rates[:, RATE_FIRST : RATE_FIRST + 1]
    rate_second = rates[:, RATE_SECOND : RATE_SECOND + 1]
    d_closing = norm_backward(n[1].astype(F32), rate_second, prm[l, 9:10, :], c_in[...].astype(F32))
    d_branch = d_closing.astype(BF)
    total = d_closing
    for block in range(4):
        ready(4 + block)
        d_active = dot(d_branch, w[l, pl.ds((8 + block) * width, width), :], 1, 1)
        d_inner = (d_active * gp[block].astype(F32)).astype(BF)
        total = total + dot(d_inner, w[l, pl.ds((4 + block) * width, width), :], 1, 1)
        after(("inner", block))
    spent("gp")
    d_summed = norm_backward(n[0].astype(F32), rate_first, prm[l, 8:9, :], total)
    spent("n")
    ready(3)
    d_mixed = dot(d_summed.astype(BF), w[l, 3 * width : 4 * width, :], 1, 1).astype(BF)
    have("mixed")
    have("qkv")
    for quad in range(quads):
        have(quad)
        for pair in range(2):
            lanes = slice(256 * quad + 128 * pair, 256 * quad + 128 * pair + 128)
            query, keys, values = qkv[0, :, lanes], qkv[1, :, lanes], qkv[2, :, lanes]
            out_rows = d_mixed[:, lanes].astype(F32)
            mixed_rows = mixed[:, lanes]
            query_t = query.T
            d_query, d_keys, d_values = [], [], []
            for head in range(2):
                mine = (lane < 64) == (head == 0)
                which = quad * 4 + pair * 2 + head
                over = rates[:, which : which + 1]
                share = shares[which]
                scaled = jnp.where(mine, out_rows * over, 0.0).astype(BF)
                row_sum = jnp.sum(scaled.astype(F32) * mixed_rows, axis=1, keepdims=True)
                d_score = (share.astype(F32) * (dot(scaled, values, 1, 1) - row_sum)).astype(BF)
                rows = slice(64 * head, 64 * head + 64)
                d_query.append(dot(d_score, keys))
                d_keys.append(dot(query_t[rows], d_score))
                d_values.append(dot(scaled.T[rows], share))
            d_qkv[0, :, lanes] = (jnp.where(lane < 64, d_query[0], d_query[1]) * 0.125).astype(BF)
            d_qkv[1, :, lanes] = (jnp.concatenate(d_keys, axis=0) * 0.125).astype(BF).T
            d_qkv[2, :, lanes] = jnp.concatenate(d_values, axis=0).astype(BF).T
        spent(quad)
        after(quad)
    for part in ("r", "mixed", "qkv"):
        spent(part)
    have("x")
    down = dot(x[l], prm[l, 12:28, :].astype(BF), 1, 1).astype(BF)
    rank = down.shape[1] // 2
    d_up[l, 0:rank, :] = 2.0 * dot(down, d_qkv[0], 0, 0)[0:rank]
    d_up[l, rank : 2 * rank, :] = 2.0 * dot(down, d_qkv[2], 0, 0)[rank:]
    total = d_summed
    for kind in range(3):
        ready(kind)
        total = total + dot(d_qkv[kind], w[l, kind * width : (kind + 1) * width, :], 1, 1)
    c_out[...] = total.astype(BF)


def state_shapes(length, width):
    return [
        ((3, length, width), BF),
        ((HEADS, length, length), BF),
        ((length, width), F32),
        ((2, length, width), BF),
        ((4, length, width), BF),
        ((length, 128), F32),
    ]


def state_copy(state, kept, sem, l, part, load):
    if isinstance(part, int):
        inside, outside = state[1].at[pl.ds(4 * part, 4)], kept[1].at[l, pl.ds(4 * part, 4)]
        which = 5 + part
    else:
        i = {"qkv": 0, "mixed": 2, "n": 3, "gp": 4, "r": 5}[part]
        inside, outside = state[i], kept[i].at[l]
        which = {0: 0, 2: 1, 3: 2, 4: 3, 5: 4}[i]
    ends = (outside, inside) if load else (inside, outside)
    return pltpu.make_async_copy(*ends, sem.at[which])


EARLY_PARTS = ("qkv", "mixed", 0, 1, 2)
INNER_PARTS = ("gp",)
END_PARTS = ("n", "r")
BATCHES = {"attended": EARLY_PARTS, ("inner", 3): INNER_PARTS, "end": END_PARTS}


def save_calls(state, kept, sem, l):
    def after(point):
        if point == "begin":

            @pl.when(l > 0)
            def _():
                for part in EARLY_PARTS:
                    state_copy(state, kept, sem, 0, part, False).wait()

        if point == "attended":

            @pl.when(l > 0)
            def _():
                for part in INNER_PARTS + END_PARTS:
                    state_copy(state, kept, sem, 0, part, False).wait()

    return after


def first_kernel(scal, lens, source, mine, theirs, *refs):
    pieces, refs = refs[:32], refs[32:]
    w_all, out_first, out_second = refs[:3]
    kept, refs = refs[3:9], refs[9:]
    x, w, prm, lanes, act, wsem, osem, xsem, hsem, ssem = refs[:10]
    state = refs[10:]
    parity, stage = scal[PARITY], scal[STAGE]

    def out_copy(l, place):
        return pltpu.make_async_copy(block_view(w, l, place), block_view(w_all, l, place), osem.at[l, place])

    for place in range(4):
        start_block(scal, pieces, w, wsem, 0, place)

    @pl.when(stage != 0)
    def _():
        for l in range(2):
            for place in range(PLACES):
                if l or place > 3:
                    start_block(scal, pieces, w, wsem, l, place)
        for l in range(2):
            for place in range(PLACES):
                wait_block(w, wsem, l, place)
                out_copy(l, place).start()

    @pl.when(stage == 0)
    def _():
        fresh = pltpu.make_async_copy(source.at[parity], x.at[0], xsem)
        fresh.start()
        take_params(scal, mine, theirs, prm)
        query_lanes, key_lanes = label_lanes(lens, parity, x.shape[1])
        lanes[0] = query_lanes
        lanes[1] = key_lanes
        fresh.wait()

        def layer(l, carry):
            def ready(place):
                wait_block(w, wsem, l, place)
                out_copy(l, place).start()

            waits = save_calls(state, kept, ssem, l)

            def ahead(places, own):
                for i in range(2):
                    if own or i == 0:

                        @pl.when(l == i)
                        def _():
                            for place in places:
                                start_block(scal, pieces, w, wsem, i if own else 1, place)

            def after(point):
                waits(point)
                if point == 0:
                    ahead((4, 5), True)
                if point == 1:
                    ahead((6, 7), True)
                if point == 2:
                    ahead((8,), True)
                for part in BATCHES.get(point, ()):
                    state_copy(state, kept, ssem, l, part, False).start()
                if isinstance(point, tuple):
                    ahead((point[1],), False)

            forward_layer(l, lanes, x, w, prm, act, state, ready, after)
            return carry

        lax.fori_loop(0, 2, layer, 0)
        outs = [
            pltpu.make_async_copy(x.at[1], out_first, hsem.at[0]),
            pltpu.make_async_copy(x.at[2], out_second, hsem.at[1]),
        ]
        for copy in outs:
            copy.start()
        for part in EARLY_PARTS + INNER_PARTS + END_PARTS:
            state_copy(state, kept, ssem, 1, part, False).wait()
        for copy in outs:
            copy.wait()

    for l in range(2):
        for place in range(PLACES):
            out_copy(l, place).wait()


def load_weights(w_all, w, wsem, l, places):
    for place in places:
        pltpu.make_async_copy(block_view(w_all, l, place), block_view(w, l, place), wsem.at[l, place]).start()


def load_ahead(w_all, w, wsem, l, point):
    own = {"begin": (4,), 0: (5, 6), 1: (7,), 2: (8,)}.get(point, ())
    load_weights(w_all, w, wsem, l, own)
    if isinstance(point, tuple):

        @pl.when(l == 0)
        def _():
            load_weights(w_all, w, wsem, 1, (point[1],))


def middle_kernel(scal, lens, source, arrived, cotangent, early_first, early_second, mine, theirs, w_all, *refs):
    hop_up, hop_down, acts, acts_other, second, second_other, d_up = refs[:7]
    kept, refs = refs[7:13], refs[13:]
    x, w, prm, lanes, act, c, wsem, xsem, hsem, ssem = refs[:10]
    state = refs[10:]
    parity, stage = scal[PARITY], scal[STAGE]
    load_weights(w_all, w, wsem, 0, range(4))
    d_up[...] = jnp.zeros(d_up.shape, F32)
    take_params(scal, mine, theirs, prm)
    query_lanes, key_lanes = label_lanes(lens, parity, x.shape[1])
    lanes[0] = query_lanes
    lanes[1] = key_lanes

    def placed(first, last, own, other, at):
        for p in range(2):

            @pl.when(parity == p)
            def _():
                ends = (first, last) if p == 0 else (last, first)
                pltpu.make_async_copy(ends[0], own.at[p], hsem.at[at]).start()
                pltpu.make_async_copy(ends[1], other, hsem.at[at + 1]).start()

    def placed_wait(own, other, at):
        pltpu.make_async_copy(own.at[0], own.at[0], hsem.at[at]).wait()
        pltpu.make_async_copy(other, other, hsem.at[at + 1]).wait()

    def both(copies):
        for copy in copies:
            copy.start()
        for copy in copies:
            copy.wait()

    @pl.when(stage == 0)
    def _():
        both(
            [
                pltpu.make_async_copy(source.at[parity], x.at[0], xsem.at[0]),
                pltpu.make_async_copy(early_first, c.at[0], xsem.at[1]),
                pltpu.make_async_copy(early_second, c.at[1], xsem.at[2]),
            ]
        )
        placed(c.at[0], c.at[1], acts, acts_other, 0)

    @pl.when(stage != 0)
    def _():
        both(
            [
                pltpu.make_async_copy(arrived, x.at[0], xsem.at[0]),
                pltpu.make_async_copy(cotangent.at[parity], c.at[0], xsem.at[1]),
            ]
        )

    def layer(l, carry):
        def ready(place):
            wait_block(w, wsem, l, place)

        waits = save_calls(state, kept, ssem, l)

        def after(point):
            waits(point)
            load_ahead(w_all, w, wsem, l, point)
            if point in BATCHES:

                @pl.when(l == 0)
                def _():
                    for part in BATCHES[point]:
                        state_copy(state, kept, ssem, 0, part, False).start()

        forward_layer(l, lanes, x, w, prm, act, state, ready, after)
        return carry

    lax.fori_loop(0, 2, layer, 0)

    @pl.when(stage == 0)
    def _():
        up = pltpu.make_async_copy(x.at[2], hop_up, xsem.at[0])
        up.start()
        placed(x.at[1], x.at[2], second, second_other, 2)
        up.wait()

    @pl.when(stage != 0)
    def _():
        placed(x.at[1], x.at[2], acts, acts_other, 0)

        def gradient(i, carry):
            l = 1 - i

            def have(part):
                if part != "x":

                    @pl.when(i > 0)
                    def _():
                        state_copy(state, kept, ssem, 0, part, True).wait()

            def spent(part):
                @pl.when(i == 0)
                def _():
                    state_copy(state, kept, ssem, 0, part, True).start()

            backward_layer(
                l, c.at[i], c.at[1 - i], x, w, prm, act, d_up, state, lambda place: None, have, spent, lambda point: None
            )
            return carry

        lax.fori_loop(0, 2, gradient, 0)
        down = pltpu.make_async_copy(c.at[0], hop_down, xsem.at[0])
        down.start()
        placed(c.at[0], c.at[1], second, second_other, 2)
        down.wait()

    placed_wait(acts, acts_other, 0)
    placed_wait(second, second_other, 2)


def last_kernel(scal, lens, source, arrived_up, arrived_down, early_first, second, mine, theirs, w_all, *refs):
    kept, refs = refs[:6], refs[6:]
    joined, grads, other, d_up = refs[:4]
    x, w, prm, lanes, act, c, wsem, xsem, hsem, ssem = refs[4:14]
    state = refs[14:]
    parity, stage = scal[PARITY], scal[STAGE]
    take_params(scal, mine, theirs, prm)
    d_up[...] = jnp.zeros(d_up.shape, F32)

    def carry_in(room):
        return pltpu.make_async_copy(second.at[parity], room, hsem.at[3])

    def carry_out(room, earlier):
        return pltpu.make_async_copy(room, earlier.at[parity], hsem.at[2])

    def finish(first, last, own):
        for p in range(2):

            @pl.when(parity == p)
            def _():
                ends = (first, last) if p == 0 else (last, first)
                copies = [
                    pltpu.make_async_copy(ends[1], other, hsem.at[1]),
                    pltpu.make_async_copy(ends[0], own.at[p], hsem.at[0]),
                ]
                for copy in copies:
                    copy.start()
                for copy in copies:
                    copy.wait()

    @pl.when(stage == 0)
    def _():
        def load(l, part):
            return state_copy(state, kept, ssem, l, part, True)

        cot = pltpu.make_async_copy(arrived_down, c.at[0], xsem.at[0])
        start_x = pltpu.make_async_copy(source.at[parity], x.at[0], xsem.at[1])
        middle_x = pltpu.make_async_copy(early_first, x.at[1], xsem.at[2])
        cot.start()
        for part in ("n", "r"):
            load(1, part).start()
        load_weights(w_all, w, wsem, 1, (8,))
        load(1, "gp").start()
        load_weights(w_all, w, wsem, 1, (4, 5))
        cot.wait()

        def gradient(i, carry):
            l = 1 - i

            def have(part):
                if part != "x":
                    load(0, part).wait()
                    return

                @pl.when(i == 0)
                def _():
                    start_x.wait()
                    middle_x.wait()

            def spent(part):
                @pl.when(i == 0)
                def _():
                    load(0, part).start()

            def ready(place):
                wait_block(w, wsem, l, place)

            def after(point):
                key = point[1] if isinstance(point, tuple) else point + 4
                load_weights(w_all, w, wsem, l, ((6,), (7,), (3,), (), (0,), (1, 2), ())[key])

                @pl.when(i == 0)
                def _():
                    for part in (("mixed",), ("qkv",), (0,), (1,), (2,), (), ())[key]:
                        load(1, part).start()
                    if key == 4:
                        carry_in(x.at[2]).start()
                        start_x.start()
                        middle_x.start()
                    if key == 5:
                        load_weights(w_all, w, wsem, 0, (8,))
                        carry_in(x.at[2]).wait()
                        carry_out(x.at[2], joined).start()
                    if key == 6:
                        load_weights(w_all, w, wsem, 0, (4, 5))

            backward_layer(l, c.at[i], c.at[1 - i], x, w, prm, act, d_up, state, ready, have, spent, after)
            return carry

        lax.fori_loop(0, 2, gradient, 0)
        finish(c.at[0], c.at[1], grads)
        carry_out(x.at[2], joined).wait()

    @pl.when(stage != 0)
    def _():
        load_weights(w_all, w, wsem, 0, range(4))
        query_lanes, key_lanes = label_lanes(lens, parity, x.shape[1])
        lanes[0] = query_lanes
        lanes[1] = key_lanes
        copy = pltpu.make_async_copy(arrived_up, x.at[0], xsem.at[0])
        copy.start()
        copy.wait()
        carry_in(c.at[0]).start()
        carry_in(c.at[0]).wait()
        carry_out(c.at[0], grads).start()

        def layer(l, carry):
            forward_layer(
                l,
                lanes,
                x,
                w,
                prm,
                act,
                None,
                lambda place: wait_block(w, wsem, l, place),
                lambda point: load_ahead(w_all, w, wsem, l, point),
            )
            return carry

        lax.fori_loop(0, 2, layer, 0)
        finish(x.at[1], x.at[2], joined)
        carry_out(c.at[0], grads).wait()


def common_scratch(length, width, rows, extra):
    return (
        [
            pltpu.VMEM((3, length, width), BF),
            pltpu.VMEM((2, 12 * width, width), BF),
            pltpu.VMEM((2, PARAM_ROWS, width), F32),
            pltpu.VMEM((2, length, 128), BF),
            pltpu.VMEM((4, length, width), BF),
        ]
        + extra
        + [
            pltpu.SemaphoreType.DMA((3,)),
            pltpu.SemaphoreType.DMA((4,)),
            pltpu.SemaphoreType.DMA((8,)),
        ]
        + [pltpu.VMEM(dims, kind) for dims, kind in state_shapes(length, width)]
    )


def layers_cost(length, width, forwards, backwards):
    dense = 2 * length * width * width * 12
    heads = 2 * length * length * width
    return pl.CostEstimate(
        flops=2 * (forwards * (dense + 2 * heads) + backwards * (dense + 5 * heads)),
        bytes_accessed=2 * 12 * width * width * 2,
        transcendentals=0,
    )


def run_first(scal, lens, source, mine, theirs, pieces):
    _, length, width = source.shape
    shape = jax.ShapeDtypeStruct
    anywhere = pl.BlockSpec(memory_space=pl.ANY)
    smem = pl.BlockSpec(memory_space=pltpu.SMEM)
    vmem = pl.BlockSpec(memory_space=pltpu.VMEM)
    row = shape((length, width), BF)
    outs = [shape((2, 12 * width, width), BF), row, row]
    outs += [shape((2,) + dims, kind) for dims, kind in state_shapes(length, width)]
    scratch = common_scratch(
        length, width, 2, [pltpu.SemaphoreType.DMA((2, PLACES)), pltpu.SemaphoreType.DMA((2, PLACES))]
    )
    scratch[7] = pltpu.SemaphoreType.DMA
    return pl.pallas_call(
        first_kernel,
        out_shape=outs,
        in_specs=[smem, smem, anywhere, vmem, vmem] + [anywhere] * 32,
        out_specs=[anywhere] * len(outs),
        scratch_shapes=scratch,
        compiler_params=pltpu.CompilerParams(vmem_limit_bytes=VMEM_BYTES),
        cost_estimate=layers_cost(length, width, 1, 0),
        name="first",
    )(scal, lens, source, mine, theirs, *pieces)


def run_middle(scal, lens, source, arrived, cotangent, early_first, early_second, mine, theirs, w_all):
    _, length, width = source.shape
    shape = jax.ShapeDtypeStruct
    anywhere = pl.BlockSpec(memory_space=pl.ANY)
    smem = pl.BlockSpec(memory_space=pltpu.SMEM)
    vmem = pl.BlockSpec(memory_space=pltpu.VMEM)
    row, rows = shape((length, width), BF), shape((2, length, width), BF)
    outs = [row, row, rows, row, rows, row, shape((2, 16, width), F32)]
    outs += [shape((1,) + dims, kind) for dims, kind in state_shapes(length, width)]
    return pl.pallas_call(
        middle_kernel,
        out_shape=outs,
        in_specs=[smem, smem] + [anywhere] * 5 + [vmem, vmem, anywhere],
        out_specs=[anywhere] * 6 + [vmem] + [anywhere] * 6,
        scratch_shapes=common_scratch(
            length,
            width,
            2,
            [pltpu.VMEM((2, length, width), BF), pltpu.SemaphoreType.DMA((2, PLACES))],
        ),
        compiler_params=pltpu.CompilerParams(vmem_limit_bytes=VMEM_BYTES),
        cost_estimate=layers_cost(length, width, 1, 1),
        name="middle",
    )(scal, lens, source, arrived, cotangent, early_first, early_second, mine, theirs, w_all)


def run_last(scal, lens, source, arrived_up, arrived_down, early_first, second, mine, theirs, w_all, kept):
    _, length, width = source.shape
    shape = jax.ShapeDtypeStruct
    anywhere = pl.BlockSpec(memory_space=pl.ANY)
    smem = pl.BlockSpec(memory_space=pltpu.SMEM)
    vmem = pl.BlockSpec(memory_space=pltpu.VMEM)
    row, rows = shape((length, width), BF), shape((2, length, width), BF)
    return pl.pallas_call(
        last_kernel,
        out_shape=[rows, rows, row, shape((2, 16, width), F32)],
        in_specs=[smem, smem] + [anywhere] * 5 + [vmem, vmem] + [anywhere] * 7,
        out_specs=[anywhere] * 3 + [vmem],
        scratch_shapes=common_scratch(
            length,
            width,
            2,
            [pltpu.VMEM((2, length, width), BF), pltpu.SemaphoreType.DMA((2, PLACES))],
        ),
        compiler_params=pltpu.CompilerParams(vmem_limit_bytes=VMEM_BYTES),
        cost_estimate=layers_cost(length, width, 0, 1),
        name="last",
    )(scal, lens, source, arrived_up, arrived_down, early_first, second, mine, theirs, w_all, *kept)


def tables(sections, copies):
    group = copies // SHARDS
    out = np.zeros((sections * copies, 12), np.int32)
    for s in range(sections):
        for d in range(copies):
            shard = d // group
            place, side = RING.index(shard // 2), shard % 2
            row = out[s * copies + d]
            for step in range(4):
                node = RING[(place - step) % 4]
                row[2 * step], row[2 * step + 1] = 2 * node + side, 2 * node + 1 - side
            row[PARITY], row[STAGE], row[OWN_SHARD] = s % 2, s // 2, shard
    return out


def body(
    inputs,
    evaluation_input,
    output_cotangent,
    packed_segment_lengths,
    attention_in_weight,
    attention_out_weight,
    feedforward_in_weight,
    feedforward_out_weight,
    adapter_down_weight,
    adapter_up_weight,
    projection_biases,
    feedforward_bias,
    layer_norm_gain,
    layer_norm_shift,
):
    sections, copies = lax.axis_size("section"), lax.axis_size("dp")
    group = copies // SHARDS
    section, place = lax.axis_index("section"), lax.axis_index("dp")
    even = section % 2 == 0
    scal = lax.dynamic_index_in_dim(
        jnp.asarray(tables(sections, copies)), section * copies + place, 0, keepdims=False
    )

    def permuted(array, move):
        pairs = []
        for s in range(sections):
            for d in range(copies):
                target = move(s, d // group)
                if target is not None:
                    pairs.append((s * copies + d, target[0] * copies + target[1] * group + d % group))
        return lax.ppermute(array, AXES, pairs)

    ring_next = {RING[i]: RING[(i + 1) % 4] for i in range(4)}
    ring_last = {RING[i]: RING[i - 1] for i in range(4)}
    along = lambda s, q: (s, ring_next[q // 2] * 2 + q % 2)
    against = lambda s, q: (s, ring_last[q // 2] * 2 + q % 2)
    other_side = lambda s, q: (s, q ^ 1)
    partner = lambda s, q: (s ^ 1, q)
    upward = lambda s, q: (s + 2, q) if s < 2 else None
    downward = lambda s, q: (s - 2, q) if s >= 2 else None

    w_in, w_out, w_up, w_down = (
        attention_in_weight[0],
        attention_out_weight[0],
        feedforward_in_weight[0],
        feedforward_out_weight[0],
    )
    if group > 1:
        groups = [[q * group + i for i in range(group)] for q in range(SHARDS)]
        w_in, w_out, w_up, w_down = (
            lax.all_gather(piece, "dp", axis=0, tiled=True, axis_index_groups=groups)
            for piece in (w_in, w_out, w_up, w_down)
        )
    part_a, part_b, mine = pack(
        scal,
        w_in,
        w_out,
        w_up,
        w_down,
        adapter_down_weight[0].T,
        adapter_up_weight[0],
        projection_biases[0],
        feedforward_bias,
        layer_norm_gain[0],
        layer_norm_shift[0],
    )

    def held_back(array, until):
        return lax.optimization_barrier((array, until))[0]

    r0 = [part_a, part_b]
    x0, r1 = [None, None], [None, None]
    for half in range(2):
        x0[half] = permuted(r0[half], partner)
        r1[half] = permuted(r0[half], along)
    x1, r2 = [None, None], [None, None]
    for half in range(2):
        x1[half] = permuted(held_back(r1[half], x0[half]), partner)
        r2[half] = permuted(r1[half], along)
    z_first = permuted(held_back(jnp.where(even, r0[0], x0[1]), x1[0]), against)
    x2, z_second = [None, None], [None, None]
    for half in range(2):
        x2[half] = permuted(held_back(r2[half], x1[half]), partner)
        second_layer = jnp.where(even, x0[half], r0[half])
        z_second[half] = permuted(held_back(second_layer, z_first if half else r2[1]), against)
    x_first = permuted(held_back(z_first, x2[1]), partner)
    theirs = permuted(held_back(mine, x2[1]), partner)

    def swapped(halves):
        return halves + [permuted(half, other_side) for half in halves]

    pieces = []
    for halves in (r0, r1, r2, x0, x1, x2, [z_first], [x_first], z_second):
        pieces += swapped(halves)

    lens = packed_segment_lengths
    w_all, early_first, early_second, *kept = run_first(scal, lens, inputs, mine, theirs, pieces)
    arrived = permuted(early_second, upward)
    hop_up, hop_down, acts, acts_other, second, second_other, d_up_late, *_ = run_middle(
        scal,
        lens,
        evaluation_input,
        arrived,
        output_cotangent,
        early_first,
        early_second,
        mine,
        theirs,
        w_all,
    )
    arrived_down = permuted(hop_down, downward)
    arrived_up = permuted(hop_up, upward)
    acts_row = permuted(acts_other, partner)
    second_row = permuted(second_other, partner)
    joined, grads, last_other, d_up_early = run_last(
        scal, lens, inputs, arrived_up, arrived_down, early_first, second, mine, theirs, w_all, kept
    )
    last_other, d_up_early, acts_row, second_row = lax.optimization_barrier(
        (last_other, d_up_early, acts_row, second_row)
    )
    last_row = permuted(last_other, partner)
    early = section < 2
    row = 1 - section % 2

    def settled(rows, arrived_row):
        return lax.dynamic_update_slice(rows, arrived_row[None], (row, 0, 0))[None]

    activations = settled(acts, acts_row)
    joined = settled(joined, jnp.where(early, second_row, last_row))
    grads = settled(grads, jnp.where(early, last_row, second_row))

    total = jnp.where(early, d_up_early, d_up_late)
    total = jnp.where(even, total[0], total[1]) + permuted(jnp.where(even, total[1], total[0]), partner)
    for flips in ((1,), (2, 4, 6)):
        total = sum([permuted(total, lambda s, q, flip=flip: (s, q ^ flip)) for flip in flips], total)
    step = 1
    while step < group:
        total = total + lax.ppermute(total, "dp", [(d, d ^ step) for d in range(copies)])
        step *= 2
    total = total.reshape((1, 2, total.shape[0] // 2, total.shape[1]))
    return (activations, grads, total, joined)


def solution(mesh):
    in_specs = (
        P("dp", None, None),
        P("dp", None, None),
        P("dp", None, None),
        P("dp", None),
        P("section", "dp", None),
        P("section", "dp", None),
        P("section", "dp", None),
        P("section", "dp", None),
        P("section", None, None),
        P("section", None, None, None),
        P("section", None, None),
        P("section", None),
        P("section", None, None),
        P("section", None, None),
    )
    out_specs = (
        P("section", "dp", None, None),
        P("section", "dp", None, None),
        P("section", None, None, None),
        P("section", "dp", None, None),
    )
    return jax.shard_map(body, mesh=mesh, in_specs=in_specs, out_specs=out_specs, check_vma=False)
```

```python
import functools

import jax
import jax.numpy as jnp
import numpy as np
from jax import lax
from jax.experimental import pallas as pl
from jax.experimental.pallas import tpu as pltpu
from jax.sharding import PartitionSpec as P

HEADS = 12
norm_eps = 1e-05
masked_score = -1e30
BF = jnp.bfloat16
F32 = jnp.float32
AXES = ("section", "dp")
SHARDS = 8
RING = (0, 1, 3, 2)
PARAM_ROWS = 32
VMEM_BYTES = 62 << 20
PARTS = 3
PARITY, STAGE, OWN_SHARD = 8, 9, 10
RATE_FIRST, RATE_SECOND = 12, 13


def dot(left, right, left_dim=1, right_dim=0):
    return lax.dot_general(
        left, right, (((left_dim,), (right_dim,)), ((), ())), preferred_element_type=F32
    )


def centre_and_scale(value):
    centered = value - jnp.mean(value, axis=-1, keepdims=True)
    spread = jnp.mean(centered * centered, axis=-1, keepdims=True)
    rate = lax.rsqrt(spread + norm_eps)
    return centered * rate, rate


def norm_backward(normal, rate, gain, cotangent):
    q = gain * cotangent
    along = jnp.mean(q * normal, axis=-1, keepdims=True)
    return (q - jnp.mean(q, axis=-1, keepdims=True) - normal * along) * rate


def pack_kernel(
    scal, w_in, w_out, w_up, w_down, down_t, up, biases, inner_bias, gains, shifts, part_a, part_b, mine, rows
):
    depth, width = w_out.shape
    rank = up.shape[1]
    mine[0:4, :] = biases[...]
    for block in range(4):
        mine[4 + block : 5 + block, :] = inner_bias[:, block * width : (block + 1) * width]
    mine[8:10, :] = gains[...]
    mine[10:12, :] = shifts[...]
    down_t32 = down_t[...].astype(F32)
    mine[12:28, :] = down_t32
    mine[28:32, :] = jnp.zeros((4, width), F32)
    rows[:, 0 : 2 * rank] = down_t32.T
    a = rows[pl.ds(pl.multiple_of(scal[OWN_SHARD] * depth, 8), depth), 0 : 2 * rank]
    for block in range(3):
        piece = w_in[:, block * width : (block + 1) * width]
        if block != 1:
            side = block // 2
            extra = a[:, side * rank : side * rank + 1] * up[side, 0:1, :]
            for i in range(1, rank):
                extra = extra + a[:, side * rank + i : side * rank + i + 1] * up[side, i : i + 1, :]
            piece = (piece.astype(F32) + 2.0 * extra).astype(BF)
        part_a[block * depth : (block + 1) * depth, :] = piece
    part_a[3 * depth : 4 * depth, :] = w_out[...]
    for block in range(4):
        piece = w_up[:, block * width : (block + 1) * width]
        if block < 2:
            part_a[(4 + block) * depth : (5 + block) * depth, :] = piece
        else:
            part_b[(block - 2) * depth : (block - 1) * depth, :] = piece
    part_b[2 * depth : 6 * depth, :] = w_down[...]


def pack(scal, w_in, w_out, w_up, w_down, down_t, up, biases, inner_bias, gains, shifts):
    depth, width = w_out.shape
    shape = jax.ShapeDtypeStruct
    part = shape((6 * depth, width), BF)
    smem = pl.BlockSpec(memory_space=pltpu.SMEM)
    vmem = pl.BlockSpec(memory_space=pltpu.VMEM)
    return pl.pallas_call(
        pack_kernel,
        out_shape=(part, part, shape((PARAM_ROWS, width), F32)),
        in_specs=[smem] + [vmem] * 10,
        out_specs=(vmem, vmem, vmem),
        scratch_shapes=[pltpu.VMEM((width, 128), F32)],
        compiler_params=pltpu.CompilerParams(vmem_limit_bytes=VMEM_BYTES),
        name="pack",
    )(scal, w_in, w_out, w_up, w_down, down_t, up, biases, inner_bias, gains, shifts)


def piece_of(pieces, parity, l, step, side, half):
    if step < 3:
        base = 0 if parity == l else 12
        return pieces[base + (step * 2 + side) * 2 + half]
    if l == 0:
        return pieces[24 + (0 if half == parity else 2) + side]
    return pieces[28 + side * 2 + half]


def rows_of(w, l, block):
    depth = w.shape[2] // 12
    return jnp.concatenate([w[l, j, depth * block : depth * (block + 1), :] for j in range(SHARDS)], axis=0)


def down_of(w, l, block=None):
    depth = w.shape[2] // 12
    shards = range(SHARDS) if block is None else (2 * block, 2 * block + 1)
    return jnp.concatenate([w[l, j, 8 * depth :, :] for j in shards], axis=0)


def part_view(w, l, part):
    rows = w.shape[2] // PARTS
    return w.at[l, :, pl.ds(part * rows, rows)]


def start_part(scal, pieces, w, sem, l, part):
    half_rows = w.shape[2] // 2
    rows = w.shape[2] // PARTS
    begin, end = part * rows, (part + 1) * rows
    for parity in range(2):

        @pl.when(scal[PARITY] == parity)
        def _():
            for i in range(8):
                for half in range(2):
                    low, high = max(begin, half * half_rows), min(end, (half + 1) * half_rows)
                    if low < high:
                        source = piece_of(pieces, parity, l, i // 2, i % 2, half)
                        pltpu.make_async_copy(
                            source.at[pl.ds(low - half * half_rows, high - low)],
                            w.at[l, scal[i], pl.ds(low, high - low)],
                            sem.at[l, part],
                        ).start()


def wait_part(w, sem, l, part):
    view = part_view(w, l, part)
    pltpu.make_async_copy(view, view, sem.at[l, part]).wait()


def take_params(scal, mine, theirs, prm):
    prm[scal[PARITY]] = mine[...]
    prm[1 - scal[PARITY]] = theirs[...]


def label_lanes(lens, row, length):
    places = lax.broadcasted_iota(jnp.int32, (length, 1), 0)
    label = jnp.zeros((length, 1), jnp.int32)
    end = jnp.int32(0)
    segments = lens.shape[1]
    for j in range(segments):
        end = end + lens[row, j]
        label = label + (places >= end).astype(jnp.int32)
    lane = lax.broadcasted_iota(jnp.int32, (1, 128), 1) % 64
    same = label == lane
    used = lane <= segments
    query_lanes = jnp.where(same, 1.0, 0.0).astype(BF)
    key_lanes = jnp.where(same | ~used, 0.0, masked_score).astype(BF)
    return query_lanes, key_lanes


def forward_layer(l, lens_lanes, x, w, prm, act, state, ready, after):
    length, width = x.shape[1:]
    lane = lax.broadcasted_iota(jnp.int32, (1, 128), 1)
    low = lane < 64
    value = x[l]
    ready(0)
    after("begin")
    query = (dot(value, rows_of(w, l, 0)) + prm[l, 0:1, :]).astype(BF)
    keys = dot(value, rows_of(w, l, 1)).astype(BF)
    values = (dot(value, rows_of(w, l, 2)) + prm[l, 1:2, :]).astype(BF)
    if state is not None:
        qkv, shares, mixed_out, n, gp, r = state
        rates = jnp.zeros((length, 128), F32)
        qkv[0] = query
        qkv[1] = keys
        qkv[2] = values
    query_lanes, key_lanes = lens_lanes[0], lens_lanes[1]
    ones = jnp.ones((length, 128), BF)
    mixed = []
    for pair in range(width // 128):
        lanes = slice(128 * pair, 128 * pair + 128)
        scaled = query[:, lanes] * BF(0.125)
        upper = jnp.concatenate([jnp.where(low, scaled, BF(0)), query_lanes], axis=1)
        lower = jnp.concatenate([jnp.where(low, BF(0), scaled), query_lanes], axis=1)
        scores = dot(
            jnp.concatenate([upper, lower], axis=0), jnp.concatenate([keys[:, lanes], key_lanes], axis=1), 1, 1
        )
        top = jnp.max(scores, axis=1, keepdims=True)
        share = jnp.exp(scores - top).astype(BF)
        part = dot(share, jnp.concatenate([values[:, lanes], ones], axis=1))
        over = 1.0 / part[:, 128:129]
        part = part[:, 0:128] * over
        joined = jnp.where(low, part[:length], part[length:])
        if state is not None:
            shares[2 * pair] = share[:length]
            shares[2 * pair + 1] = share[length:]
            mixed_out[:, lanes] = joined
            rates = jnp.where(lane == 2 * pair, over[:length], rates)
            rates = jnp.where(lane == 2 * pair + 1, over[length:], rates)
        mixed.append(joined.astype(BF))
        if pair % 2:
            after(pair // 2)
    mixed = jnp.concatenate(mixed, axis=1)
    ready(1)
    ready(2)
    after("attended")
    halves = [slice(0, length // 2), slice(length // 2, length)]
    firsts, rates_first = [], []
    for rows in halves:
        attended = dot(mixed[rows], rows_of(w, l, 3))
        summed = value[rows].astype(F32) + (attended + prm[l, 2:3, :])
        normal, rate = centre_and_scale(summed)
        firsts.append((normal * prm[l, 8:9, :] + prm[l, 10:11, :]).astype(BF))
        rates_first.append(rate)
        if state is not None:
            n[0, rows] = normal.astype(BF)
    for block in range(4):
        for rows, first in zip(halves, firsts):
            inner = dot(first, rows_of(w, l, 4 + block))
            inner = inner + prm[l, 4 + block : 5 + block, :]
            below = 0.5 + 0.5 * lax.erf(inner * (2**-0.5))
            act[rows, block * width : (block + 1) * width] = (inner * below).astype(BF)
            if state is not None:
                bell = jnp.exp(-0.5 * inner * inner) * 0.3989422804014327
                gp[block, rows] = (below + inner * bell).astype(BF)
    after("inner")
    for rows, first, rate_first in zip(halves, firsts, rates_first):
        branch = dot(act[rows, :], down_of(w, l))
        closing = first.astype(F32) + (branch + prm[l, 3:4, :])
        normal, rate_second = centre_and_scale(closing)
        if state is not None:
            n[1, rows] = normal.astype(BF)
            own = jnp.where(lane == RATE_FIRST, rate_first, rates[rows])
            r[rows] = jnp.where(lane == RATE_SECOND, rate_second, own)
        x[l + 1, rows] = (normal * prm[l, 9:10, :] + prm[l, 11:12, :]).astype(BF)
    after("end")


def backward_layer(l, c_in, c_out, x, w, prm, d_qkv, d_up, state, ready, have, spent, after):
    qkv, shares, mixed, n, gp, r = state
    length, width = x.shape[1:]
    lane = lax.broadcasted_iota(jnp.int32, (1, 128), 1)
    for part in ("n", "r", "gp"):
        have(part)
    ready(2)
    rates = r[...]
    rate_first = rates[:, RATE_FIRST : RATE_FIRST + 1]
    rate_second = rates[:, RATE_SECOND : RATE_SECOND + 1]
    d_closing = norm_backward(n[1].astype(F32), rate_second, prm[l, 9:10, :], c_in[...].astype(F32))
    d_branch = d_closing.astype(BF)
    total = d_closing
    for block in range(4):
        d_active = dot(d_branch, down_of(w, l, block), 1, 1)
        d_inner = (d_active * gp[block].astype(F32)).astype(BF)
        if block == 0:
            ready(1)
        total = total + dot(d_inner, rows_of(w, l, 4 + block), 1, 1)
        after(("inner", block))
    spent("gp")
    d_summed = norm_backward(n[0].astype(F32), rate_first, prm[l, 8:9, :], total)
    spent("n")
    ready(0)
    d_mixed = dot(d_summed.astype(BF), rows_of(w, l, 3), 1, 1).astype(BF)
    have("mixed")
    have("qkv")
    low = lane < 64
    for pair in range(width // 128):
        if pair % 2 == 0:
            have(pair // 2)
        lanes = slice(128 * pair, 128 * pair + 128)
        query, keys, values = qkv[0, :, lanes], qkv[1, :, lanes], qkv[2, :, lanes]
        out_rows = d_mixed[:, lanes].astype(F32)
        upper = jnp.where(low, out_rows * rates[:, 2 * pair : 2 * pair + 1], 0.0)
        lower = jnp.where(low, 0.0, out_rows * rates[:, 2 * pair + 1 : 2 * pair + 2])
        scaled = jnp.concatenate([upper, lower], axis=0).astype(BF)
        mixed_rows = mixed[:, lanes]
        mixed_rows = jnp.concatenate([mixed_rows, mixed_rows], axis=0)
        row_sum = jnp.sum(scaled.astype(F32) * mixed_rows, axis=1, keepdims=True)
        share = jnp.concatenate([shares[2 * pair], shares[2 * pair + 1]], axis=0)
        d_score = (share.astype(F32) * (dot(scaled, values, 1, 1) - row_sum)).astype(BF)
        d_query = dot(d_score, keys)
        queries = jnp.concatenate([jnp.where(low, query, BF(0)), jnp.where(low, BF(0), query)], axis=0)
        d_keys = dot(queries.T, d_score)
        d_values = dot(scaled.T, share)
        d_query = jnp.where(low, d_query[:length], d_query[length:])
        d_qkv[:, lanes] = (d_query * 0.125).astype(BF)
        d_qkv[:, width + 128 * pair : width + 128 * pair + 128] = (d_keys * 0.125).astype(BF).T
        d_qkv[:, 2 * width + 128 * pair : 2 * width + 128 * pair + 128] = d_values.astype(BF).T
        if pair % 2:
            spent(pair // 2)
            after(pair // 2)
    for part in ("r", "mixed", "qkv"):
        spent(part)
    have("x")
    down = dot(x[l], prm[l, 12:28, :].astype(BF), 1, 1).astype(BF)
    rank = down.shape[1] // 2
    d_up[l, 0:rank, :] = 2.0 * dot(down, d_qkv[:, 0:width], 0, 0)[0:rank]
    d_up[l, rank : 2 * rank, :] = 2.0 * dot(down, d_qkv[:, 2 * width : 3 * width], 0, 0)[rank:]
    total = d_summed
    for kind in range(3):
        total = total + dot(d_qkv[:, kind * width : (kind + 1) * width], rows_of(w, l, kind), 1, 1)
    c_out[...] = total.astype(BF)


def state_shapes(length, width):
    return [
        ((3, length, width), BF),
        ((HEADS, length, length), BF),
        ((length, width), F32),
        ((2, length, width), BF),
        ((4, length, width), BF),
        ((length, 128), F32),
    ]


def state_copy(state, kept, sem, l, part, load):
    if isinstance(part, int):
        inside, outside = state[1].at[pl.ds(4 * part, 4)], kept[1].at[l, pl.ds(4 * part, 4)]
        which = 5 + part
    else:
        i = {"qkv": 0, "mixed": 2, "n": 3, "gp": 4, "r": 5}[part]
        inside, outside = state[i], kept[i].at[l]
        which = {0: 0, 2: 1, 3: 2, 4: 3, 5: 4}[i]
    ends = (outside, inside) if load else (inside, outside)
    return pltpu.make_async_copy(*ends, sem.at[which])


EARLY_PARTS = ("qkv", "mixed", 0, 1, 2)
INNER_PARTS = ("gp",)
END_PARTS = ("n", "r")
BATCHES = {0: ("qkv", 0), 1: (1,), 2: (2, "mixed"), "inner": INNER_PARTS, "end": END_PARTS}


def save_calls(state, kept, sem, l):
    def after(point):
        if point == "begin":

            @pl.when(l > 0)
            def _():
                for part in EARLY_PARTS:
                    state_copy(state, kept, sem, 0, part, False).wait()

        if point == "attended":

            @pl.when(l > 0)
            def _():
                for part in INNER_PARTS + END_PARTS:
                    state_copy(state, kept, sem, 0, part, False).wait()

    return after


def first_kernel(scal, lens, source, mine, theirs, *refs):
    pieces, refs = refs[:32], refs[32:]
    w_all, out_first, out_second = refs[:3]
    kept, refs = refs[3:9], refs[9:]
    x, w, prm, lanes, act, wsem, osem, xsem, hsem, ssem = refs[:10]
    state = refs[10:]
    parity, stage = scal[PARITY], scal[STAGE]

    def out_copy(l, place):
        return pltpu.make_async_copy(part_view(w, l, place), part_view(w_all, l, place), osem.at[l, place])

    start_part(scal, pieces, w, wsem, 0, 0)

    @pl.when(stage != 0)
    def _():
        for l in range(2):
            for place in range(PARTS):
                if l or place:
                    start_part(scal, pieces, w, wsem, l, place)
        for l in range(2):
            for place in range(PARTS):
                wait_part(w, wsem, l, place)
                out_copy(l, place).start()

    @pl.when(stage == 0)
    def _():
        fresh = pltpu.make_async_copy(source.at[parity], x.at[0], xsem)
        fresh.start()
        take_params(scal, mine, theirs, prm)
        query_lanes, key_lanes = label_lanes(lens, parity, x.shape[1])
        lanes[0] = query_lanes
        lanes[1] = key_lanes
        fresh.wait()

        def layer(l, carry):
            def ready(place):
                wait_part(w, wsem, l, place)

            waits = save_calls(state, kept, ssem, l)

            def ahead(places, own):
                for i in range(2):
                    if own or i == 0:

                        @pl.when(l == i)
                        def _():
                            for place in places:
                                start_part(scal, pieces, w, wsem, i if own else 1, place)

            def after(point):
                waits(point)
                if point in OWN_AHEAD:
                    ahead(OWN_AHEAD[point], True)
                if point in NEXT_AHEAD:
                    ahead(NEXT_AHEAD[point], False)
                for place in OUT_AT.get(point, ()):
                    out_copy(l, place).start()
                for part in BATCHES.get(point, ()):
                    state_copy(state, kept, ssem, l, part, False).start()

            forward_layer(l, lanes, x, w, prm, act, state, ready, after)
            return carry

        lax.fori_loop(0, 2, layer, 0)
        outs = [
            pltpu.make_async_copy(x.at[1], out_first, hsem.at[0]),
            pltpu.make_async_copy(x.at[2], out_second, hsem.at[1]),
        ]
        for copy in outs:
            copy.start()
        for part in EARLY_PARTS + INNER_PARTS + END_PARTS:
            state_copy(state, kept, ssem, 1, part, False).wait()
        for copy in outs:
            copy.wait()

    for l in range(2):
        for place in range(PARTS):
            out_copy(l, place).wait()


OWN_AHEAD = {"begin": (1,), 1: (2,)}
NEXT_AHEAD = {"attended": (0,)}
OUT_AT = {0: (0,), "attended": (1,), "inner": (2,)}


def load_weights(w_all, w, wsem, l, places):
    for place in places:
        pltpu.make_async_copy(part_view(w_all, l, place), part_view(w, l, place), wsem.at[l, place]).start()


def load_ahead(w_all, w, wsem, l, point):
    load_weights(w_all, w, wsem, l, OWN_AHEAD.get(point, ()))
    following = NEXT_AHEAD.get(point, ())
    if following:

        @pl.when(l == 0)
        def _():
            load_weights(w_all, w, wsem, 1, following)


def middle_kernel(scal, lens, source, arrived, cotangent, early_first, early_second, mine, theirs, w_all, *refs):
    hop_up, hop_down, acts, acts_other, second, second_other, d_up = refs[:7]
    kept, refs = refs[7:13], refs[13:]
    x, w, prm, lanes, act, c, wsem, xsem, hsem, ssem = refs[:10]
    state = refs[10:]
    parity, stage = scal[PARITY], scal[STAGE]
    load_weights(w_all, w, wsem, 0, (0,))
    d_up[...] = jnp.zeros(d_up.shape, F32)
    take_params(scal, mine, theirs, prm)
    query_lanes, key_lanes = label_lanes(lens, parity, x.shape[1])
    lanes[0] = query_lanes
    lanes[1] = key_lanes

    def placed(first, last, own, other, at):
        for p in range(2):

            @pl.when(parity == p)
            def _():
                ends = (first, last) if p == 0 else (last, first)
                pltpu.make_async_copy(ends[0], own.at[p], hsem.at[at]).start()
                pltpu.make_async_copy(ends[1], other, hsem.at[at + 1]).start()

    def placed_wait(own, other, at):
        pltpu.make_async_copy(own.at[0], own.at[0], hsem.at[at]).wait()
        pltpu.make_async_copy(other, other, hsem.at[at + 1]).wait()

    def both(copies):
        for copy in copies:
            copy.start()
        for copy in copies:
            copy.wait()

    @pl.when(stage == 0)
    def _():
        both(
            [
                pltpu.make_async_copy(source.at[parity], x.at[0], xsem.at[0]),
                pltpu.make_async_copy(early_first, c.at[0], xsem.at[1]),
                pltpu.make_async_copy(early_second, c.at[1], xsem.at[2]),
            ]
        )
        placed(c.at[0], c.at[1], acts, acts_other, 0)

    @pl.when(stage != 0)
    def _():
        both(
            [
                pltpu.make_async_copy(arrived, x.at[0], xsem.at[0]),
                pltpu.make_async_copy(cotangent.at[parity], c.at[0], xsem.at[1]),
            ]
        )

    def layer(l, carry):
        def ready(place):
            wait_part(w, wsem, l, place)

        waits = save_calls(state, kept, ssem, l)

        def after(point):
            waits(point)
            load_ahead(w_all, w, wsem, l, point)
            if point in BATCHES:

                @pl.when(l == 0)
                def _():
                    for part in BATCHES[point]:
                        state_copy(state, kept, ssem, 0, part, False).start()

        forward_layer(l, lanes, x, w, prm, act, state, ready, after)
        return carry

    lax.fori_loop(0, 2, layer, 0)

    @pl.when(stage == 0)
    def _():
        up = pltpu.make_async_copy(x.at[2], hop_up, xsem.at[0])
        up.start()
        placed(x.at[1], x.at[2], second, second_other, 2)
        up.wait()

    @pl.when(stage != 0)
    def _():
        placed(x.at[1], x.at[2], acts, acts_other, 0)

        def gradient(i, carry):
            l = 1 - i

            def have(part):
                if part != "x":

                    @pl.when(i > 0)
                    def _():
                        state_copy(state, kept, ssem, 0, part, True).wait()

            def spent(part):
                @pl.when(i == 0)
                def _():
                    state_copy(state, kept, ssem, 0, part, True).start()

            backward_layer(
                l, c.at[i], c.at[1 - i], x, w, prm, act, d_up, state, lambda place: None, have, spent, lambda point: None
            )
            return carry

        lax.fori_loop(0, 2, gradient, 0)
        down = pltpu.make_async_copy(c.at[0], hop_down, xsem.at[0])
        down.start()
        placed(c.at[0], c.at[1], second, second_other, 2)
        down.wait()

    placed_wait(acts, acts_other, 0)
    placed_wait(second, second_other, 2)


def last_kernel(scal, lens, source, arrived_up, arrived_down, early_first, second, mine, theirs, w_all, *refs):
    kept, refs = refs[:6], refs[6:]
    joined, grads, other, d_up = refs[:4]
    x, w, prm, lanes, act, c, wsem, xsem, hsem, ssem = refs[4:14]
    state = refs[14:]
    parity, stage = scal[PARITY], scal[STAGE]
    take_params(scal, mine, theirs, prm)
    d_up[...] = jnp.zeros(d_up.shape, F32)

    def carry_in(room):
        return pltpu.make_async_copy(second.at[parity], room, hsem.at[3])

    def carry_out(room, earlier):
        return pltpu.make_async_copy(room, earlier.at[parity], hsem.at[2])

    def finish(first, last, own):
        for p in range(2):

            @pl.when(parity == p)
            def _():
                ends = (first, last) if p == 0 else (last, first)
                copies = [
                    pltpu.make_async_copy(ends[1], other, hsem.at[1]),
                    pltpu.make_async_copy(ends[0], own.at[p], hsem.at[0]),
                ]
                for copy in copies:
                    copy.start()
                for copy in copies:
                    copy.wait()

    @pl.when(stage == 0)
    def _():
        def load(l, part):
            return state_copy(state, kept, ssem, l, part, True)

        cot = pltpu.make_async_copy(arrived_down, c.at[0], xsem.at[0])
        start_x = pltpu.make_async_copy(source.at[parity], x.at[0], xsem.at[1])
        middle_x = pltpu.make_async_copy(early_first, x.at[1], xsem.at[2])
        cot.start()
        for part in ("n", "r"):
            load(1, part).start()
        load_weights(w_all, w, wsem, 1, (2,))
        load(1, "gp").start()
        load_weights(w_all, w, wsem, 1, (1,))
        cot.wait()

        def gradient(i, carry):
            l = 1 - i

            def have(part):
                if part != "x":
                    load(0, part).wait()
                    return

                @pl.when(i == 0)
                def _():
                    start_x.wait()
                    middle_x.wait()

            def spent(part):
                @pl.when(i == 0)
                def _():
                    load(0, part).start()

            def ready(place):
                wait_part(w, wsem, l, place)

            def after(point):
                key = point[1] if isinstance(point, tuple) else point + 4
                load_weights(w_all, w, wsem, l, ((), (0,), (), (), (), (), ())[key])

                @pl.when(i == 0)
                def _():
                    for part in (("mixed",), ("qkv",), (0,), (1,), (2,), (), ())[key]:
                        load(1, part).start()
                    if key == 4:
                        carry_in(x.at[2]).start()
                        start_x.start()
                        middle_x.start()
                    if key == 5:
                        load_weights(w_all, w, wsem, 0, (2,))
                        carry_in(x.at[2]).wait()
                        carry_out(x.at[2], joined).start()
                    if key == 6:
                        load_weights(w_all, w, wsem, 0, (1,))

            backward_layer(l, c.at[i], c.at[1 - i], x, w, prm, act, d_up, state, ready, have, spent, after)
            return carry

        lax.fori_loop(0, 2, gradient, 0)
        finish(c.at[0], c.at[1], grads)
        carry_out(x.at[2], joined).wait()

    @pl.when(stage != 0)
    def _():
        load_weights(w_all, w, wsem, 0, (0,))
        query_lanes, key_lanes = label_lanes(lens, parity, x.shape[1])
        lanes[0] = query_lanes
        lanes[1] = key_lanes
        copy = pltpu.make_async_copy(arrived_up, x.at[0], xsem.at[0])
        copy.start()
        copy.wait()
        carry_in(c.at[0]).start()
        carry_in(c.at[0]).wait()
        carry_out(c.at[0], grads).start()

        def layer(l, carry):
            forward_layer(
                l,
                lanes,
                x,
                w,
                prm,
                act,
                None,
                lambda place: wait_part(w, wsem, l, place),
                lambda point: load_ahead(w_all, w, wsem, l, point),
            )
            return carry

        lax.fori_loop(0, 2, layer, 0)
        finish(x.at[1], x.at[2], joined)
        carry_out(c.at[0], grads).wait()


def common_scratch(length, width, rows, extra):
    return (
        [
            pltpu.VMEM((3, length, width), BF),
            pltpu.VMEM((2, SHARDS, 12 * width // SHARDS, width), BF),
            pltpu.VMEM((2, PARAM_ROWS, width), F32),
            pltpu.VMEM((2, length, 128), BF),
            pltpu.VMEM((length, 4 * width), BF),
        ]
        + extra
        + [
            pltpu.SemaphoreType.DMA((3,)),
            pltpu.SemaphoreType.DMA((4,)),
            pltpu.SemaphoreType.DMA((8,)),
        ]
        + [pltpu.VMEM(dims, kind) for dims, kind in state_shapes(length, width)]
    )


def layers_cost(length, width, forwards, backwards):
    dense = 2 * length * width * width * 12
    heads = 2 * length * length * width
    return pl.CostEstimate(
        flops=2 * (forwards * (dense + 2 * heads) + backwards * (dense + 5 * heads)),
        bytes_accessed=2 * 12 * width * width * 2,
        transcendentals=0,
    )


def run_first(scal, lens, source, mine, theirs, pieces):
    _, length, width = source.shape
    shape = jax.ShapeDtypeStruct
    anywhere = pl.BlockSpec(memory_space=pl.ANY)
    smem = pl.BlockSpec(memory_space=pltpu.SMEM)
    vmem = pl.BlockSpec(memory_space=pltpu.VMEM)
    row = shape((length, width), BF)
    outs = [shape((2, SHARDS, 12 * width // SHARDS, width), BF), row, row]
    outs += [shape((2,) + dims, kind) for dims, kind in state_shapes(length, width)]
    scratch = common_scratch(
        length, width, 2, [pltpu.SemaphoreType.DMA((2, PARTS)), pltpu.SemaphoreType.DMA((2, PARTS))]
    )
    scratch[7] = pltpu.SemaphoreType.DMA
    return pl.pallas_call(
        first_kernel,
        out_shape=outs,
        in_specs=[smem, smem, anywhere, vmem, vmem] + [anywhere] * 32,
        out_specs=[anywhere] * len(outs),
        scratch_shapes=scratch,
        compiler_params=pltpu.CompilerParams(vmem_limit_bytes=VMEM_BYTES),
        cost_estimate=layers_cost(length, width, 1, 0),
        name="first",
    )(scal, lens, source, mine, theirs, *pieces)


def run_middle(scal, lens, source, arrived, cotangent, early_first, early_second, mine, theirs, w_all):
    _, length, width = source.shape
    shape = jax.ShapeDtypeStruct
    anywhere = pl.BlockSpec(memory_space=pl.ANY)
    smem = pl.BlockSpec(memory_space=pltpu.SMEM)
    vmem = pl.BlockSpec(memory_space=pltpu.VMEM)
    row, rows = shape((length, width), BF), shape((2, length, width), BF)
    outs = [row, row, rows, row, rows, row, shape((2, 16, width), F32)]
    outs += [shape((1,) + dims, kind) for dims, kind in state_shapes(length, width)]
    return pl.pallas_call(
        middle_kernel,
        out_shape=outs,
        in_specs=[smem, smem] + [anywhere] * 5 + [vmem, vmem, anywhere],
        out_specs=[anywhere] * 6 + [vmem] + [anywhere] * 6,
        scratch_shapes=common_scratch(
            length,
            width,
            2,
            [pltpu.VMEM((2, length, width), BF), pltpu.SemaphoreType.DMA((2, PARTS))],
        ),
        compiler_params=pltpu.CompilerParams(vmem_limit_bytes=VMEM_BYTES),
        cost_estimate=layers_cost(length, width, 1, 1),
        name="middle",
    )(scal, lens, source, arrived, cotangent, early_first, early_second, mine, theirs, w_all)


def run_last(scal, lens, source, arrived_up, arrived_down, early_first, second, mine, theirs, w_all, kept):
    _, length, width = source.shape
    shape = jax.ShapeDtypeStruct
    anywhere = pl.BlockSpec(memory_space=pl.ANY)
    smem = pl.BlockSpec(memory_space=pltpu.SMEM)
    vmem = pl.BlockSpec(memory_space=pltpu.VMEM)
    row, rows = shape((length, width), BF), shape((2, length, width), BF)
    return pl.pallas_call(
        last_kernel,
        out_shape=[rows, rows, row, shape((2, 16, width), F32)],
        in_specs=[smem, smem] + [anywhere] * 5 + [vmem, vmem] + [anywhere] * 7,
        out_specs=[anywhere] * 3 + [vmem],
        scratch_shapes=common_scratch(
            length,
            width,
            2,
            [pltpu.VMEM((2, length, width), BF), pltpu.SemaphoreType.DMA((2, PARTS))],
        ),
        compiler_params=pltpu.CompilerParams(vmem_limit_bytes=VMEM_BYTES),
        cost_estimate=layers_cost(length, width, 0, 1),
        name="last",
    )(scal, lens, source, arrived_up, arrived_down, early_first, second, mine, theirs, w_all, *kept)


def tables(sections, copies):
    group = copies // SHARDS
    out = np.zeros((sections * copies, 12), np.int32)
    for s in range(sections):
        for d in range(copies):
            shard = d // group
            place, side = RING.index(shard // 2), shard % 2
            row = out[s * copies + d]
            for step in range(4):
                node = RING[(place - step) % 4]
                row[2 * step], row[2 * step + 1] = 2 * node + side, 2 * node + 1 - side
            row[PARITY], row[STAGE], row[OWN_SHARD] = s % 2, s // 2, shard
    return out


def body(
    inputs,
    evaluation_input,
    output_cotangent,
    packed_segment_lengths,
    attention_in_weight,
    attention_out_weight,
    feedforward_in_weight,
    feedforward_out_weight,
    adapter_down_weight,
    adapter_up_weight,
    projection_biases,
    feedforward_bias,
    layer_norm_gain,
    layer_norm_shift,
):
    sections, copies = lax.axis_size("section"), lax.axis_size("dp")
    group = copies // SHARDS
    section, place = lax.axis_index("section"), lax.axis_index("dp")
    even = section % 2 == 0
    scal = lax.dynamic_index_in_dim(
        jnp.asarray(tables(sections, copies)), section * copies + place, 0, keepdims=False
    )

    def permuted(array, move):
        pairs = []
        for s in range(sections):
            for d in range(copies):
                target = move(s, d // group)
                if target is not None:
                    pairs.append((s * copies + d, target[0] * copies + target[1] * group + d % group))
        return lax.ppermute(array, AXES, pairs)

    ring_next = {RING[i]: RING[(i + 1) % 4] for i in range(4)}
    ring_last = {RING[i]: RING[i - 1] for i in range(4)}
    along = lambda s, q: (s, ring_next[q // 2] * 2 + q % 2)
    against = lambda s, q: (s, ring_last[q // 2] * 2 + q % 2)
    other_side = lambda s, q: (s, q ^ 1)
    partner = lambda s, q: (s ^ 1, q)
    upward = lambda s, q: (s + 2, q) if s < 2 else None
    downward = lambda s, q: (s - 2, q) if s >= 2 else None

    w_in, w_out, w_up, w_down = (
        attention_in_weight[0],
        attention_out_weight[0],
        feedforward_in_weight[0],
        feedforward_out_weight[0],
    )
    if group > 1:
        groups = [[q * group + i for i in range(group)] for q in range(SHARDS)]
        w_in, w_out, w_up, w_down = (
            lax.all_gather(piece, "dp", axis=0, tiled=True, axis_index_groups=groups)
            for piece in (w_in, w_out, w_up, w_down)
        )
    part_a, part_b, mine = pack(
        scal,
        w_in,
        w_out,
        w_up,
        w_down,
        adapter_down_weight[0].T,
        adapter_up_weight[0],
        projection_biases[0],
        feedforward_bias,
        layer_norm_gain[0],
        layer_norm_shift[0],
    )

    def held_back(array, until):
        return lax.optimization_barrier((array, until))[0]

    r0 = [part_a, part_b]
    x0, r1 = [None, None], [None, None]
    for half in range(2):
        x0[half] = permuted(r0[half], partner)
        r1[half] = permuted(r0[half], along)
    x1, r2 = [None, None], [None, None]
    for half in range(2):
        x1[half] = permuted(held_back(r1[half], x0[half]), partner)
        r2[half] = permuted(r1[half], along)
    z_first = permuted(held_back(jnp.where(even, r0[0], x0[1]), x1[0]), against)
    x2, z_second = [None, None], [None, None]
    for half in range(2):
        x2[half] = permuted(held_back(r2[half], x1[half]), partner)
        second_layer = jnp.where(even, x0[half], r0[half])
        z_second[half] = permuted(held_back(second_layer, z_first if half else r2[1]), against)
    x_first = permuted(held_back(z_first, x2[1]), partner)
    theirs = permuted(held_back(mine, x2[1]), partner)

    def swapped(halves):
        return halves + [permuted(half, other_side) for half in halves]

    pieces = []
    for halves in (r0, r1, r2, x0, x1, x2, [z_first], [x_first], z_second):
        pieces += swapped(halves)

    lens = packed_segment_lengths
    w_all, early_first, early_second, *kept = run_first(scal, lens, inputs, mine, theirs, pieces)
    arrived = permuted(early_second, upward)
    hop_up, hop_down, acts, acts_other, second, second_other, d_up_late, *_ = run_middle(
        scal,
        lens,
        evaluation_input,
        arrived,
        output_cotangent,
        early_first,
        early_second,
        mine,
        theirs,
        w_all,
    )
    arrived_down = permuted(hop_down, downward)
    arrived_up = permuted(hop_up, upward)
    acts_row = permuted(acts_other, partner)
    second_row = permuted(second_other, partner)
    joined, grads, last_other, d_up_early = run_last(
        scal, lens, inputs, arrived_up, arrived_down, early_first, second, mine, theirs, w_all, kept
    )
    last_other, d_up_early, acts_row, second_row = lax.optimization_barrier(
        (last_other, d_up_early, acts_row, second_row)
    )
    last_row = permuted(last_other, partner)
    early = section < 2
    row = 1 - section % 2

    def settled(rows, arrived_row):
        return lax.dynamic_update_slice(rows, arrived_row[None], (row, 0, 0))[None]

    activations = settled(acts, acts_row)
    joined = settled(joined, jnp.where(early, second_row, last_row))
    grads = settled(grads, jnp.where(early, last_row, second_row))

    total = jnp.where(early, d_up_early, d_up_late)
    total = jnp.where(even, total[0], total[1]) + permuted(jnp.where(even, total[1], total[0]), partner)
    for flips in ((1,), (2, 4, 6)):
        total = sum([permuted(total, lambda s, q, flip=flip: (s, q ^ flip)) for flip in flips], total)
    step = 1
    while step < group:
        total = total + lax.ppermute(total, "dp", [(d, d ^ step) for d in range(copies)])
        step *= 2
    total = total.reshape((1, 2, total.shape[0] // 2, total.shape[1]))
    return (activations, grads, total, joined)


def solution(mesh):
    in_specs = (
        P("dp", None, None),
        P("dp", None, None),
        P("dp", None, None),
        P("dp", None),
        P("section", "dp", None),
        P("section", "dp", None),
        P("section", "dp", None),
        P("section", "dp", None),
        P("section", None, None),
        P("section", None, None, None),
        P("section", None, None),
        P("section", None),
        P("section", None, None),
        P("section", None, None),
    )
    out_specs = (
        P("section", "dp", None, None),
        P("section", "dp", None, None),
        P("section", None, None, None),
        P("section", "dp", None, None),
    )
    return jax.shard_map(body, mesh=mesh, in_specs=in_specs, out_specs=out_specs, check_vma=False)
```

```python
import functools

import jax
import jax.numpy as jnp
import numpy as np
from jax import lax
from jax.experimental import pallas as pl
from jax.experimental.pallas import tpu as pltpu
from jax.sharding import PartitionSpec as P

HEADS = 12
norm_eps = 1e-05
masked_score = -1e30
BF = jnp.bfloat16
F32 = jnp.float32
AXES = ("section", "dp")
SHARDS = 8
RING = (0, 1, 3, 2)
PARAM_ROWS = 32
VMEM_BYTES = 62 << 20
PARTS = 3
PARITY, STAGE, OWN_SHARD = 8, 9, 10
RATE_FIRST, RATE_SECOND = 12, 13


def dot(left, right, left_dim=1, right_dim=0):
    return lax.dot_general(
        left, right, (((left_dim,), (right_dim,)), ((), ())), preferred_element_type=F32
    )


def centre_and_scale(value):
    centered = value - jnp.mean(value, axis=-1, keepdims=True)
    spread = jnp.mean(centered * centered, axis=-1, keepdims=True)
    rate = lax.rsqrt(spread + norm_eps)
    return centered * rate, rate


def norm_backward(normal, rate, gain, cotangent):
    q = gain * cotangent
    along = jnp.mean(q * normal, axis=-1, keepdims=True)
    return (q - jnp.mean(q, axis=-1, keepdims=True) - normal * along) * rate


def pack_kernel(
    scal, w_in, w_out, w_up, w_down, down_t, up, biases, inner_bias, gains, shifts, part_a, part_b, mine, rows
):
    depth, width = w_out.shape
    rank = up.shape[1]
    mine[0:4, :] = biases[...]
    for block in range(4):
        mine[4 + block : 5 + block, :] = inner_bias[:, block * width : (block + 1) * width]
    mine[8:10, :] = gains[...]
    mine[10:12, :] = shifts[...]
    down_t32 = down_t[...].astype(F32)
    mine[12:28, :] = down_t32
    mine[28:32, :] = jnp.zeros((4, width), F32)
    rows[:, 0 : 2 * rank] = down_t32.T
    a = rows[pl.ds(pl.multiple_of(scal[OWN_SHARD] * depth, 8), depth), 0 : 2 * rank]
    for block in range(3):
        piece = w_in[:, block * width : (block + 1) * width]
        if block != 1:
            side = block // 2
            extra = a[:, side * rank : side * rank + 1] * up[side, 0:1, :]
            for i in range(1, rank):
                extra = extra + a[:, side * rank + i : side * rank + i + 1] * up[side, i : i + 1, :]
            piece = (piece.astype(F32) + 2.0 * extra).astype(BF)
        part_a[block * depth : (block + 1) * depth, :] = piece
    part_a[3 * depth : 4 * depth, :] = w_out[...]
    for block in range(4):
        piece = w_up[:, block * width : (block + 1) * width]
        if block < 2:
            part_a[(4 + block) * depth : (5 + block) * depth, :] = piece
        else:
            part_b[(block - 2) * depth : (block - 1) * depth, :] = piece
    part_b[2 * depth : 6 * depth, :] = w_down[...]


def pack(scal, w_in, w_out, w_up, w_down, down_t, up, biases, inner_bias, gains, shifts):
    depth, width = w_out.shape
    shape = jax.ShapeDtypeStruct
    part = shape((6 * depth, width), BF)
    smem = pl.BlockSpec(memory_space=pltpu.SMEM)
    vmem = pl.BlockSpec(memory_space=pltpu.VMEM)
    return pl.pallas_call(
        pack_kernel,
        out_shape=(part, part, shape((PARAM_ROWS, width), F32)),
        in_specs=[smem] + [vmem] * 10,
        out_specs=(vmem, vmem, vmem),
        scratch_shapes=[pltpu.VMEM((width, 128), F32)],
        compiler_params=pltpu.CompilerParams(vmem_limit_bytes=VMEM_BYTES),
        name="pack",
    )(scal, w_in, w_out, w_up, w_down, down_t, up, biases, inner_bias, gains, shifts)


def piece_of(pieces, parity, l, step, side, half):
    if step < 3:
        base = 0 if parity == l else 12
        return pieces[base + (step * 2 + side) * 2 + half]
    if l == 0:
        return pieces[24 + (0 if half == parity else 2) + side]
    return pieces[28 + side * 2 + half]


def rows_of(w, l, block):
    depth = w.shape[2] // 12
    return jnp.concatenate([w[l, j, depth * block : depth * (block + 1), :] for j in range(SHARDS)], axis=0)


def down_of(w, l, block=None):
    depth = w.shape[2] // 12
    shards = range(SHARDS) if block is None else (2 * block, 2 * block + 1)
    return jnp.concatenate([w[l, j, 8 * depth :, :] for j in shards], axis=0)


def part_view(w, l, part):
    rows = w.shape[2] // PARTS
    return w.at[l, :, pl.ds(part * rows, rows)]


def start_part(scal, pieces, w, sem, l, part):
    half_rows = w.shape[2] // 2
    rows = w.shape[2] // PARTS
    begin, end = part * rows, (part + 1) * rows
    for parity in range(2):

        @pl.when(scal[PARITY] == parity)
        def _():
            for i in range(8):
                for half in range(2):
                    low, high = max(begin, half * half_rows), min(end, (half + 1) * half_rows)
                    if low < high:
                        source = piece_of(pieces, parity, l, i // 2, i % 2, half)
                        pltpu.make_async_copy(
                            source.at[pl.ds(low - half * half_rows, high - low)],
                            w.at[l, scal[i], pl.ds(low, high - low)],
                            sem.at[l, part],
                        ).start()


def wait_part(w, sem, l, part):
    view = part_view(w, l, part)
    pltpu.make_async_copy(view, view, sem.at[l, part]).wait()


def take_params(scal, mine, theirs, prm):
    prm[scal[PARITY]] = mine[...]
    prm[1 - scal[PARITY]] = theirs[...]


def label_lanes(lens, row, length):
    places = lax.broadcasted_iota(jnp.int32, (length, 1), 0)
    label = jnp.zeros((length, 1), jnp.int32)
    end = jnp.int32(0)
    segments = lens.shape[1]
    for j in range(segments):
        end = end + lens[row, j]
        label = label + (places >= end).astype(jnp.int32)
    lane = lax.broadcasted_iota(jnp.int32, (1, 128), 1) % 64
    same = label == lane
    used = lane <= segments
    query_lanes = jnp.where(same, 1.0, 0.0).astype(BF)
    key_lanes = jnp.where(same | ~used, 0.0, masked_score).astype(BF)
    return query_lanes, key_lanes


def forward_layer(l, lens_lanes, x, w, prm, act, state, ready, after):
    length, width = x.shape[1:]
    lane = lax.broadcasted_iota(jnp.int32, (1, 128), 1)
    low = lane < 64
    value = x[l]
    ready(0)
    after("begin")
    query = (dot(value, rows_of(w, l, 0)) + prm[l, 0:1, :]).astype(BF)
    keys = dot(value, rows_of(w, l, 1)).astype(BF)
    values = (dot(value, rows_of(w, l, 2)) + prm[l, 1:2, :]).astype(BF)
    if state is not None:
        qkv, shares, mixed_out, n, gp, r = state
        rates = jnp.zeros((length, 128), F32)
        qkv[0] = query
        qkv[1] = keys
        qkv[2] = values
    query_lanes, key_lanes = lens_lanes[0], lens_lanes[1]
    ones = jnp.ones((length, 128), BF)
    mixed = []
    for pair in range(width // 128):
        lanes = slice(128 * pair, 128 * pair + 128)
        scaled = query[:, lanes] * BF(0.125)
        upper = jnp.concatenate([jnp.where(low, scaled, BF(0)), query_lanes], axis=1)
        lower = jnp.concatenate([jnp.where(low, BF(0), scaled), query_lanes], axis=1)
        scores = dot(
            jnp.concatenate([upper, lower], axis=0), jnp.concatenate([keys[:, lanes], key_lanes], axis=1), 1, 1
        )
        top = jnp.max(scores, axis=1, keepdims=True)
        share = jnp.exp(scores - top).astype(BF)
        part = dot(share, jnp.concatenate([values[:, lanes], ones], axis=1))
        over = 1.0 / part[:, 128:129]
        part = part[:, 0:128] * over
        joined = jnp.where(low, part[:length], part[length:])
        if state is not None:
            shares[2 * pair] = share[:length]
            shares[2 * pair + 1] = share[length:]
            mixed_out[:, lanes] = joined
            rates = jnp.where(lane == 2 * pair, over[:length], rates)
            rates = jnp.where(lane == 2 * pair + 1, over[length:], rates)
        mixed.append(joined.astype(BF))
        if pair % 2:
            after(pair // 2)
    mixed = jnp.concatenate(mixed, axis=1)
    ready(1)
    ready(2)
    after("attended")
    halves = [slice(0, length // 2), slice(length // 2, length)]
    firsts, rates_first = [], []
    for rows in halves:
        attended = dot(mixed[rows], rows_of(w, l, 3))
        summed = value[rows].astype(F32) + (attended + prm[l, 2:3, :])
        normal, rate = centre_and_scale(summed)
        firsts.append((normal * prm[l, 8:9, :] + prm[l, 10:11, :]).astype(BF))
        rates_first.append(rate)
        if state is not None:
            n[0, rows] = normal.astype(BF)
    for block in range(4):
        for rows, first in zip(halves, firsts):
            inner = dot(first, rows_of(w, l, 4 + block))
            inner = inner + prm[l, 4 + block : 5 + block, :]
            below = 0.5 + 0.5 * lax.erf(inner * (2**-0.5))
            act[rows, block * width : (block + 1) * width] = (inner * below).astype(BF)
            if state is not None:
                bell = jnp.exp(-0.5 * inner * inner) * 0.3989422804014327
                gp[block, rows] = (below + inner * bell).astype(BF)
    after("inner")
    for rows, first, rate_first in zip(halves, firsts, rates_first):
        branch = dot(act[rows, :], down_of(w, l))
        closing = first.astype(F32) + (branch + prm[l, 3:4, :])
        normal, rate_second = centre_and_scale(closing)
        if state is not None:
            n[1, rows] = normal.astype(BF)
            own = jnp.where(lane == RATE_FIRST, rate_first, rates[rows])
            r[rows] = jnp.where(lane == RATE_SECOND, rate_second, own)
        x[l + 1, rows] = (normal * prm[l, 9:10, :] + prm[l, 11:12, :]).astype(BF)
    after("end")


def backward_layer(l, c_in, c_out, x, w, prm, d_qkv, d_up, state, ready, have, spent, after, together=False):
    qkv, shares, mixed, n, gp, r = state
    length, width = x.shape[1:]
    lane = lax.broadcasted_iota(jnp.int32, (1, 128), 1)
    for part in ("n", "r", "gp"):
        have(part)
    ready(2)
    rates = r[...]
    rate_first = rates[:, RATE_FIRST : RATE_FIRST + 1]
    rate_second = rates[:, RATE_SECOND : RATE_SECOND + 1]
    d_closing = norm_backward(n[1].astype(F32), rate_second, prm[l, 9:10, :], c_in[...].astype(F32))
    d_branch = d_closing.astype(BF)
    total = d_closing
    for block in range(4):
        d_active = dot(d_branch, down_of(w, l, block), 1, 1)
        d_inner = (d_active * gp[block].astype(F32)).astype(BF)
        if block == 0:
            ready(1)
        total = total + dot(d_inner, rows_of(w, l, 4 + block), 1, 1)
        after(("inner", block))
    spent("gp")
    d_summed = norm_backward(n[0].astype(F32), rate_first, prm[l, 8:9, :], total)
    spent("n")
    ready(0)
    d_mixed = dot(d_summed.astype(BF), rows_of(w, l, 3), 1, 1).astype(BF)
    have("mixed")
    have("qkv")
    if together:
        for quad in range(3):
            have(quad)
    low = lane < 64
    for pair in range(width // 128):
        if pair % 2 == 0 and not together:
            have(pair // 2)
        lanes = slice(128 * pair, 128 * pair + 128)
        query, keys, values = qkv[0, :, lanes], qkv[1, :, lanes], qkv[2, :, lanes]
        out_rows = d_mixed[:, lanes].astype(F32)
        upper = jnp.where(low, out_rows * rates[:, 2 * pair : 2 * pair + 1], 0.0)
        lower = jnp.where(low, 0.0, out_rows * rates[:, 2 * pair + 1 : 2 * pair + 2])
        scaled = jnp.concatenate([upper, lower], axis=0).astype(BF)
        mixed_rows = mixed[:, lanes]
        mixed_rows = jnp.concatenate([mixed_rows, mixed_rows], axis=0)
        row_sum = jnp.sum(scaled.astype(F32) * mixed_rows, axis=1, keepdims=True)
        share = jnp.concatenate([shares[2 * pair], shares[2 * pair + 1]], axis=0)
        d_score = (share.astype(F32) * (dot(scaled, values, 1, 1) - row_sum)).astype(BF)
        d_query = dot(d_score, keys)
        queries = jnp.concatenate([jnp.where(low, query, BF(0)), jnp.where(low, BF(0), query)], axis=0)
        d_keys = dot(queries.T, d_score)
        d_values = dot(scaled.T, share)
        d_query = jnp.where(low, d_query[:length], d_query[length:])
        d_qkv[:, lanes] = (d_query * 0.125).astype(BF)
        d_qkv[:, width + 128 * pair : width + 128 * pair + 128] = (d_keys * 0.125).astype(BF).T
        d_qkv[:, 2 * width + 128 * pair : 2 * width + 128 * pair + 128] = d_values.astype(BF).T
        if pair % 2 and not together:
            spent(pair // 2)
            after(pair // 2)
    for part in ("r", "mixed", "qkv") + ((0, 1, 2) if together else ()):
        spent(part)
    have("x")
    down = dot(x[l], prm[l, 12:28, :].astype(BF), 1, 1).astype(BF)
    rank = down.shape[1] // 2
    d_up[l, 0:rank, :] = 2.0 * dot(down, d_qkv[:, 0:width], 0, 0)[0:rank]
    d_up[l, rank : 2 * rank, :] = 2.0 * dot(down, d_qkv[:, 2 * width : 3 * width], 0, 0)[rank:]
    total = d_summed
    for kind in range(3):
        total = total + dot(d_qkv[:, kind * width : (kind + 1) * width], rows_of(w, l, kind), 1, 1)
    c_out[...] = total.astype(BF)


def state_shapes(length, width):
    return [
        ((3, length, width), BF),
        ((HEADS, length, length), BF),
        ((length, width), F32),
        ((2, length, width), BF),
        ((4, length, width), BF),
        ((length, 128), F32),
    ]


def state_copy(state, kept, sem, l, part, load):
    if isinstance(part, int):
        inside, outside = state[1].at[pl.ds(4 * part, 4)], kept[1].at[l, pl.ds(4 * part, 4)]
        which = 5 + part
    else:
        i = {"qkv": 0, "mixed": 2, "n": 3, "gp": 4, "r": 5}[part]
        inside, outside = state[i], kept[i].at[l]
        which = {0: 0, 2: 1, 3: 2, 4: 3, 5: 4}[i]
    ends = (outside, inside) if load else (inside, outside)
    return pltpu.make_async_copy(*ends, sem.at[which])


EARLY_PARTS = ("qkv", "mixed", 0, 1, 2)
INNER_PARTS = ("gp",)
END_PARTS = ("n", "r")
BATCHES = {0: ("qkv", 0), 1: (1,), 2: (2, "mixed"), "inner": INNER_PARTS, "end": END_PARTS}


def save_calls(state, kept, sem, l):
    def after(point):
        if point == "begin":

            @pl.when(l > 0)
            def _():
                for part in EARLY_PARTS:
                    state_copy(state, kept, sem, 0, part, False).wait()

        if point == "attended":

            @pl.when(l > 0)
            def _():
                for part in INNER_PARTS + END_PARTS:
                    state_copy(state, kept, sem, 0, part, False).wait()

    return after


def first_kernel(scal, lens, source, mine, theirs, *refs):
    pieces, refs = refs[:32], refs[32:]
    w_all, out_first, out_second = refs[:3]
    kept, refs = refs[3:9], refs[9:]
    x, w, prm, lanes, act, wsem, osem, xsem, hsem, ssem = refs[:10]
    state = refs[10:]
    parity, stage = scal[PARITY], scal[STAGE]

    def out_copy(l, place):
        return pltpu.make_async_copy(part_view(w, l, place), part_view(w_all, l, place), osem.at[l, place])

    start_part(scal, pieces, w, wsem, 0, 0)

    @pl.when(stage != 0)
    def _():
        for l in range(2):
            for place in range(PARTS):
                if l or place:
                    start_part(scal, pieces, w, wsem, l, place)
        for l in range(2):
            for place in range(PARTS):
                wait_part(w, wsem, l, place)
                out_copy(l, place).start()

    @pl.when(stage == 0)
    def _():
        fresh = pltpu.make_async_copy(source.at[parity], x.at[0], xsem)
        fresh.start()
        take_params(scal, mine, theirs, prm)
        query_lanes, key_lanes = label_lanes(lens, parity, x.shape[1])
        lanes[0] = query_lanes
        lanes[1] = key_lanes
        fresh.wait()

        def layer(l, carry):
            def ready(place):
                wait_part(w, wsem, l, place)

            waits = save_calls(state, kept, ssem, l)

            def after(point):
                waits(point)
                for layer, loads, outs in ((0, FIRST_LOADS, FIRST_OUTS), (1, SECOND_LOADS, SECOND_OUTS)):
                    if point in loads or point in outs:

                        @pl.when(l == layer)
                        def _():
                            for to, part in loads.get(point, ()):
                                start_part(scal, pieces, w, wsem, to, part)
                            for part in outs.get(point, ()):
                                out_copy(layer, part).start()

                for part in BATCHES.get(point, ()):
                    state_copy(state, kept, ssem, l, part, False).start()

            forward_layer(l, lanes, x, w, prm, act, state, ready, after)
            return carry

        lax.fori_loop(0, 2, layer, 0)
        outs = [
            pltpu.make_async_copy(x.at[1], out_first, hsem.at[0]),
            pltpu.make_async_copy(x.at[2], out_second, hsem.at[1]),
        ]
        for copy in outs:
            copy.start()
        for part in EARLY_PARTS + INNER_PARTS + END_PARTS:
            state_copy(state, kept, ssem, 1, part, False).wait()
        for copy in outs:
            copy.wait()

    for l in range(2):
        for place in range(PARTS):
            out_copy(l, place).wait()


OWN_AHEAD = {"begin": (1,), 1: (2,)}
NEXT_AHEAD = {"attended": (0,)}
FIRST_LOADS = {"begin": ((0, 1),), 1: ((0, 2),), "attended": ((1, 0),), "inner": ((1, 1),)}
SECOND_LOADS = {"begin": ((1, 2),)}
FIRST_OUTS = {0: (0,), "attended": (1,), "inner": (2,)}
SECOND_OUTS = {0: (0,), 1: (1,), "attended": (2,)}


def load_weights(w_all, w, wsem, l, places):
    for place in places:
        pltpu.make_async_copy(part_view(w_all, l, place), part_view(w, l, place), wsem.at[l, place]).start()


def load_ahead(w_all, w, wsem, l, point):
    load_weights(w_all, w, wsem, l, OWN_AHEAD.get(point, ()))
    following = NEXT_AHEAD.get(point, ())
    if following:

        @pl.when(l == 0)
        def _():
            load_weights(w_all, w, wsem, 1, following)


def middle_kernel(scal, lens, source, arrived, cotangent, early_first, early_second, mine, theirs, w_all, *refs):
    hop, acts, acts_other, second, second_other, d_up = refs[:6]
    kept, refs = refs[6:12], refs[12:]
    x, w, prm, lanes, act, c, wsem, xsem, hsem, ssem = refs[:10]
    state = refs[10:]
    parity, stage = scal[PARITY], scal[STAGE]
    load_weights(w_all, w, wsem, 0, (0,))
    d_up[...] = jnp.zeros(d_up.shape, F32)
    take_params(scal, mine, theirs, prm)
    query_lanes, key_lanes = label_lanes(lens, parity, x.shape[1])
    lanes[0] = query_lanes
    lanes[1] = key_lanes

    def placed(first, last, own, other, at):
        for p in range(2):

            @pl.when(parity == p)
            def _():
                ends = (first, last) if p == 0 else (last, first)
                pltpu.make_async_copy(ends[0], own.at[p], hsem.at[at]).start()
                pltpu.make_async_copy(ends[1], other, hsem.at[at + 1]).start()

    def placed_wait(own, other, at):
        pltpu.make_async_copy(own.at[0], own.at[0], hsem.at[at]).wait()
        pltpu.make_async_copy(other, other, hsem.at[at + 1]).wait()

    def both(copies):
        for copy in copies:
            copy.start()
        for copy in copies:
            copy.wait()

    @pl.when(stage == 0)
    def _():
        both(
            [
                pltpu.make_async_copy(source.at[parity], x.at[0], xsem.at[0]),
                pltpu.make_async_copy(early_first, c.at[0], xsem.at[1]),
                pltpu.make_async_copy(early_second, c.at[1], xsem.at[2]),
            ]
        )
        placed(c.at[0], c.at[1], acts, acts_other, 0)

    @pl.when(stage != 0)
    def _():
        both(
            [
                pltpu.make_async_copy(arrived, x.at[0], xsem.at[0]),
                pltpu.make_async_copy(cotangent.at[parity], c.at[0], xsem.at[1]),
            ]
        )

    def layer(l, carry):
        def ready(place):
            wait_part(w, wsem, l, place)

        waits = save_calls(state, kept, ssem, l)

        def after(point):
            waits(point)
            load_ahead(w_all, w, wsem, l, point)
            if point in BATCHES:

                @pl.when(l == 0)
                def _():
                    for part in BATCHES[point]:
                        state_copy(state, kept, ssem, 0, part, False).start()

        forward_layer(l, lanes, x, w, prm, act, state, ready, after)
        return carry

    lax.fori_loop(0, 2, layer, 0)

    @pl.when(stage == 0)
    def _():
        up = pltpu.make_async_copy(x.at[2], hop, xsem.at[0])
        up.start()
        placed(x.at[1], x.at[2], second, second_other, 2)
        up.wait()

    @pl.when(stage != 0)
    def _():
        placed(x.at[1], x.at[2], acts, acts_other, 0)

        def gradient(i, carry):
            l = 1 - i

            def have(part):
                if part != "x":

                    @pl.when(i > 0)
                    def _():
                        state_copy(state, kept, ssem, 0, part, True).wait()

            def spent(part):
                @pl.when(i == 0)
                def _():
                    state_copy(state, kept, ssem, 0, part, True).start()

            backward_layer(
                l, c.at[i], c.at[1 - i], x, w, prm, act, d_up, state, lambda place: None, have, spent, lambda point: None, True
            )
            return carry

        lax.fori_loop(0, 2, gradient, 0)
        down = pltpu.make_async_copy(c.at[0], hop, xsem.at[0])
        down.start()
        placed(c.at[0], c.at[1], second, second_other, 2)
        down.wait()

    placed_wait(acts, acts_other, 0)
    placed_wait(second, second_other, 2)


def last_kernel(scal, lens, source, arrived, early_first, second, mine, theirs, w_all, *refs):
    kept, refs = refs[:6], refs[6:]
    joined, grads, other, d_up = refs[:4]
    x, w, prm, lanes, act, c, wsem, xsem, hsem, ssem = refs[4:14]
    state = refs[14:]
    parity, stage = scal[PARITY], scal[STAGE]
    take_params(scal, mine, theirs, prm)
    d_up[...] = jnp.zeros(d_up.shape, F32)

    def carry_in(room):
        return pltpu.make_async_copy(second.at[parity], room, hsem.at[3])

    def carry_out(room, earlier):
        return pltpu.make_async_copy(room, earlier.at[parity], hsem.at[2])

    def finish(first, last, own):
        for p in range(2):

            @pl.when(parity == p)
            def _():
                ends = (first, last) if p == 0 else (last, first)
                copies = [
                    pltpu.make_async_copy(ends[1], other, hsem.at[1]),
                    pltpu.make_async_copy(ends[0], own.at[p], hsem.at[0]),
                ]
                for copy in copies:
                    copy.start()
                for copy in copies:
                    copy.wait()

    @pl.when(stage == 0)
    def _():
        def load(l, part):
            return state_copy(state, kept, ssem, l, part, True)

        cot = pltpu.make_async_copy(arrived, c.at[0], xsem.at[0])
        start_x = pltpu.make_async_copy(source.at[parity], x.at[0], xsem.at[1])
        middle_x = pltpu.make_async_copy(early_first, x.at[1], xsem.at[2])
        cot.start()
        for part in ("n", "r"):
            load(1, part).start()
        load_weights(w_all, w, wsem, 1, (2,))
        load(1, "gp").start()
        load_weights(w_all, w, wsem, 1, (1,))
        cot.wait()

        def gradient(i, carry):
            l = 1 - i

            def have(part):
                if part != "x":
                    load(0, part).wait()
                    return

                @pl.when(i == 0)
                def _():
                    start_x.wait()
                    middle_x.wait()

            def spent(part):
                @pl.when(i == 0)
                def _():
                    load(0, part).start()

            def ready(place):
                wait_part(w, wsem, l, place)

            def after(point):
                key = point[1] if isinstance(point, tuple) else point + 4
                load_weights(w_all, w, wsem, l, ((), (0,), (), (), (), (), ())[key])

                @pl.when(i == 0)
                def _():
                    for part in (("mixed",), ("qkv",), (0,), (1,), (2,), (), ())[key]:
                        load(1, part).start()
                    if key == 4:
                        carry_in(x.at[2]).start()
                        start_x.start()
                        middle_x.start()
                    if key == 5:
                        load_weights(w_all, w, wsem, 0, (2,))
                        carry_in(x.at[2]).wait()
                        carry_out(x.at[2], joined).start()
                    if key == 6:
                        load_weights(w_all, w, wsem, 0, (1,))

            backward_layer(l, c.at[i], c.at[1 - i], x, w, prm, act, d_up, state, ready, have, spent, after)
            return carry

        lax.fori_loop(0, 2, gradient, 0)
        finish(c.at[0], c.at[1], grads)
        carry_out(x.at[2], joined).wait()

    @pl.when(stage != 0)
    def _():
        load_weights(w_all, w, wsem, 0, (0,))
        query_lanes, key_lanes = label_lanes(lens, parity, x.shape[1])
        lanes[0] = query_lanes
        lanes[1] = key_lanes
        copy = pltpu.make_async_copy(arrived, x.at[0], xsem.at[0])
        copy.start()
        copy.wait()
        carry_in(c.at[0]).start()
        carry_in(c.at[0]).wait()
        carry_out(c.at[0], grads).start()

        def layer(l, carry):
            forward_layer(
                l,
                lanes,
                x,
                w,
                prm,
                act,
                None,
                lambda place: wait_part(w, wsem, l, place),
                lambda point: load_ahead(w_all, w, wsem, l, point),
            )
            return carry

        lax.fori_loop(0, 2, layer, 0)
        finish(x.at[1], x.at[2], joined)
        carry_out(c.at[0], grads).wait()


def common_scratch(length, width, rows, extra):
    return (
        [
            pltpu.VMEM((3, length, width), BF),
            pltpu.VMEM((2, SHARDS, 12 * width // SHARDS, width), BF),
            pltpu.VMEM((2, PARAM_ROWS, width), F32),
            pltpu.VMEM((2, length, 128), BF),
            pltpu.VMEM((length, 4 * width), BF),
        ]
        + extra
        + [
            pltpu.SemaphoreType.DMA((3,)),
            pltpu.SemaphoreType.DMA((4,)),
            pltpu.SemaphoreType.DMA((8,)),
        ]
        + [pltpu.VMEM(dims, kind) for dims, kind in state_shapes(length, width)]
    )


def layers_cost(length, width, forwards, backwards):
    dense = 2 * length * width * width * 12
    heads = 2 * length * length * width
    return pl.CostEstimate(
        flops=2 * (forwards * (dense + 2 * heads) + backwards * (dense + 5 * heads)),
        bytes_accessed=2 * 12 * width * width * 2,
        transcendentals=0,
    )


def run_first(scal, lens, source, mine, theirs, pieces):
    _, length, width = source.shape
    shape = jax.ShapeDtypeStruct
    anywhere = pl.BlockSpec(memory_space=pl.ANY)
    smem = pl.BlockSpec(memory_space=pltpu.SMEM)
    vmem = pl.BlockSpec(memory_space=pltpu.VMEM)
    row = shape((length, width), BF)
    outs = [shape((2, SHARDS, 12 * width // SHARDS, width), BF), row, row]
    outs += [shape((2,) + dims, kind) for dims, kind in state_shapes(length, width)]
    scratch = common_scratch(
        length, width, 2, [pltpu.SemaphoreType.DMA((2, PARTS)), pltpu.SemaphoreType.DMA((2, PARTS))]
    )
    scratch[7] = pltpu.SemaphoreType.DMA
    return pl.pallas_call(
        first_kernel,
        out_shape=outs,
        in_specs=[smem, smem, anywhere, vmem, vmem] + [anywhere] * 32,
        out_specs=[anywhere] * len(outs),
        scratch_shapes=scratch,
        compiler_params=pltpu.CompilerParams(vmem_limit_bytes=VMEM_BYTES),
        cost_estimate=layers_cost(length, width, 1, 0),
        name="first",
    )(scal, lens, source, mine, theirs, *pieces)


def run_middle(scal, lens, source, arrived, cotangent, early_first, early_second, mine, theirs, w_all):
    _, length, width = source.shape
    shape = jax.ShapeDtypeStruct
    anywhere = pl.BlockSpec(memory_space=pl.ANY)
    smem = pl.BlockSpec(memory_space=pltpu.SMEM)
    vmem = pl.BlockSpec(memory_space=pltpu.VMEM)
    row, rows = shape((length, width), BF), shape((2, length, width), BF)
    outs = [row, rows, row, rows, row, shape((2, 16, width), F32)]
    outs += [shape((1,) + dims, kind) for dims, kind in state_shapes(length, width)]
    return pl.pallas_call(
        middle_kernel,
        out_shape=outs,
        in_specs=[smem, smem] + [anywhere] * 5 + [vmem, vmem, anywhere],
        out_specs=[anywhere] * 5 + [vmem] + [anywhere] * 6,
        scratch_shapes=common_scratch(
            length,
            width,
            2,
            [pltpu.VMEM((2, length, width), BF), pltpu.SemaphoreType.DMA((2, PARTS))],
        ),
        compiler_params=pltpu.CompilerParams(vmem_limit_bytes=VMEM_BYTES),
        cost_estimate=layers_cost(length, width, 1, 1),
        name="middle",
    )(scal, lens, source, arrived, cotangent, early_first, early_second, mine, theirs, w_all)


def run_last(scal, lens, source, arrived, early_first, second, mine, theirs, w_all, kept):
    _, length, width = source.shape
    shape = jax.ShapeDtypeStruct
    anywhere = pl.BlockSpec(memory_space=pl.ANY)
    smem = pl.BlockSpec(memory_space=pltpu.SMEM)
    vmem = pl.BlockSpec(memory_space=pltpu.VMEM)
    row, rows = shape((length, width), BF), shape((2, length, width), BF)
    return pl.pallas_call(
        last_kernel,
        out_shape=[rows, rows, row, shape((2, 16, width), F32)],
        in_specs=[smem, smem] + [anywhere] * 4 + [vmem, vmem] + [anywhere] * 7,
        out_specs=[anywhere] * 3 + [vmem],
        scratch_shapes=common_scratch(
            length,
            width,
            2,
            [pltpu.VMEM((2, length, width), BF), pltpu.SemaphoreType.DMA((2, PARTS))],
        ),
        compiler_params=pltpu.CompilerParams(vmem_limit_bytes=VMEM_BYTES),
        cost_estimate=layers_cost(length, width, 0, 1),
        name="last",
    )(scal, lens, source, arrived, early_first, second, mine, theirs, w_all, *kept)


def tables(sections, copies):
    group = copies // SHARDS
    out = np.zeros((sections * copies, 12), np.int32)
    for s in range(sections):
        for d in range(copies):
            shard = d // group
            place, side = RING.index(shard // 2), shard % 2
            row = out[s * copies + d]
            for step in range(4):
                node = RING[(place - step) % 4]
                row[2 * step], row[2 * step + 1] = 2 * node + side, 2 * node + 1 - side
            row[PARITY], row[STAGE], row[OWN_SHARD] = s % 2, s // 2, shard
    return out


def body(
    inputs,
    evaluation_input,
    output_cotangent,
    packed_segment_lengths,
    attention_in_weight,
    attention_out_weight,
    feedforward_in_weight,
    feedforward_out_weight,
    adapter_down_weight,
    adapter_up_weight,
    projection_biases,
    feedforward_bias,
    layer_norm_gain,
    layer_norm_shift,
):
    sections, copies = lax.axis_size("section"), lax.axis_size("dp")
    group = copies // SHARDS
    section, place = lax.axis_index("section"), lax.axis_index("dp")
    even = section % 2 == 0
    scal = lax.dynamic_index_in_dim(
        jnp.asarray(tables(sections, copies)), section * copies + place, 0, keepdims=False
    )

    def permuted(array, move):
        pairs = []
        for s in range(sections):
            for d in range(copies):
                target = move(s, d // group)
                if target is not None:
                    pairs.append((s * copies + d, target[0] * copies + target[1] * group + d % group))
        return lax.ppermute(array, AXES, pairs)

    ring_next = {RING[i]: RING[(i + 1) % 4] for i in range(4)}
    ring_last = {RING[i]: RING[i - 1] for i in range(4)}
    along = lambda s, q: (s, ring_next[q // 2] * 2 + q % 2)
    against = lambda s, q: (s, ring_last[q // 2] * 2 + q % 2)
    other_side = lambda s, q: (s, q ^ 1)
    partner = lambda s, q: (s ^ 1, q)
    upward = lambda s, q: (s + 2, q) if s < 2 else None
    across_y = lambda s, q: (s ^ 2, q)

    w_in, w_out, w_up, w_down = (
        attention_in_weight[0],
        attention_out_weight[0],
        feedforward_in_weight[0],
        feedforward_out_weight[0],
    )
    if group > 1:
        groups = [[q * group + i for i in range(group)] for q in range(SHARDS)]
        w_in, w_out, w_up, w_down = (
            lax.all_gather(piece, "dp", axis=0, tiled=True, axis_index_groups=groups)
            for piece in (w_in, w_out, w_up, w_down)
        )
    part_a, part_b, mine = pack(
        scal,
        w_in,
        w_out,
        w_up,
        w_down,
        adapter_down_weight[0].T,
        adapter_up_weight[0],
        projection_biases[0],
        feedforward_bias,
        layer_norm_gain[0],
        layer_norm_shift[0],
    )

    def held_back(array, until):
        return lax.optimization_barrier((array, until))[0]

    r0 = [part_a, part_b]
    x0, r1 = [None, None], [None, None]
    for half in range(2):
        x0[half] = permuted(r0[half], partner)
        r1[half] = permuted(r0[half], along)
    x1, r2 = [None, None], [None, None]
    for half in range(2):
        x1[half] = permuted(held_back(r1[half], x0[half]), partner)
        r2[half] = permuted(r1[half], along)
    z_first = permuted(held_back(jnp.where(even, r0[0], x0[1]), x1[0]), against)
    x2, z_second = [None, None], [None, None]
    for half in range(2):
        x2[half] = permuted(held_back(r2[half], x1[half]), partner)
        second_layer = jnp.where(even, x0[half], r0[half])
        z_second[half] = permuted(held_back(second_layer, z_first if half else r2[1]), against)
    x_first = permuted(held_back(z_first, x2[1]), partner)
    theirs = permuted(held_back(mine, x2[1]), partner)

    def swapped(halves):
        return halves + [permuted(half, other_side) for half in halves]

    pieces = []
    for halves in (r0, r1, r2, x0, x1, x2, [z_first], [x_first], z_second):
        pieces += swapped(halves)

    lens = packed_segment_lengths
    w_all, early_first, early_second, *kept = run_first(scal, lens, inputs, mine, theirs, pieces)
    arrived = permuted(early_second, upward)
    hop, acts, acts_other, second, second_other, d_up_late, *_ = run_middle(
        scal,
        lens,
        evaluation_input,
        arrived,
        output_cotangent,
        early_first,
        early_second,
        mine,
        theirs,
        w_all,
    )
    passed_on = permuted(hop, across_y)
    acts_row = permuted(acts_other, partner)
    second_row = permuted(second_other, partner)
    joined, grads, last_other, d_up_early = run_last(
        scal, lens, inputs, passed_on, early_first, second, mine, theirs, w_all, kept
    )
    last_other, d_up_early, acts_row, second_row = lax.optimization_barrier(
        (last_other, d_up_early, acts_row, second_row)
    )
    last_row = permuted(last_other, partner)
    early = section < 2
    row = 1 - section % 2

    def settled(rows, arrived_row):
        return lax.dynamic_update_slice(rows, arrived_row[None], (row, 0, 0))[None]

    activations = settled(acts, acts_row)
    joined = settled(joined, jnp.where(early, second_row, last_row))
    grads = settled(grads, jnp.where(early, last_row, second_row))

    total = jnp.where(early, d_up_early, d_up_late)
    total = jnp.where(even, total[0], total[1]) + permuted(jnp.where(even, total[1], total[0]), partner)
    for flips in ((1,), (2, 4, 6)):
        total = sum([permuted(total, lambda s, q, flip=flip: (s, q ^ flip)) for flip in flips], total)
    step = 1
    while step < group:
        total = total + lax.ppermute(total, "dp", [(d, d ^ step) for d in range(copies)])
        step *= 2
    total = total.reshape((1, 2, total.shape[0] // 2, total.shape[1]))
    return (activations, grads, total, joined)


def solution(mesh):
    in_specs = (
        P("dp", None, None),
        P("dp", None, None),
        P("dp", None, None),
        P("dp", None),
        P("section", "dp", None),
        P("section", "dp", None),
        P("section", "dp", None),
        P("section", "dp", None),
        P("section", None, None),
        P("section", None, None, None),
        P("section", None, None),
        P("section", None),
        P("section", None, None),
        P("section", None, None),
    )
    out_specs = (
        P("section", "dp", None, None),
        P("section", "dp", None, None),
        P("section", None, None, None),
        P("section", "dp", None, None),
    )
    return jax.shard_map(body, mesh=mesh, in_specs=in_specs, out_specs=out_specs, check_vma=False)
```

```python
import functools

import jax
import jax.numpy as jnp
import numpy as np
from jax import lax
from jax.experimental import pallas as pl
from jax.experimental.pallas import tpu as pltpu
from jax.sharding import PartitionSpec as P

HEADS = 12
norm_eps = 1e-05
masked_score = -1e30
BF = jnp.bfloat16
F32 = jnp.float32
AXES = ("section", "dp")
SHARDS = 8
RING = (0, 1, 3, 2)
PARAM_ROWS = 32
VMEM_BYTES = 62 << 20
PARTS = 3
PARITY, STAGE, OWN_SHARD = 8, 9, 10
RATE_FIRST, RATE_SECOND = 12, 13


def dot(left, right, left_dim=1, right_dim=0):
    return lax.dot_general(
        left, right, (((left_dim,), (right_dim,)), ((), ())), preferred_element_type=F32
    )


def centre_and_scale(value):
    centered = value - jnp.mean(value, axis=-1, keepdims=True)
    spread = jnp.mean(centered * centered, axis=-1, keepdims=True)
    rate = lax.rsqrt(spread + norm_eps)
    return centered * rate, rate


def norm_backward(normal, rate, gain, cotangent):
    q = gain * cotangent
    along = jnp.mean(q * normal, axis=-1, keepdims=True)
    return (q - jnp.mean(q, axis=-1, keepdims=True) - normal * along) * rate


def pack_kernel(
    scal, w_in, w_out, w_up, w_down, down_t, up, biases, inner_bias, gains, shifts, part_a, part_b, mine, rows
):
    depth, width = w_out.shape
    rank = up.shape[1]
    mine[0:4, :] = biases[...]
    for block in range(4):
        mine[4 + block : 5 + block, :] = inner_bias[:, block * width : (block + 1) * width]
    mine[8:10, :] = gains[...]
    mine[10:12, :] = shifts[...]
    down_t32 = down_t[...].astype(F32)
    mine[12:28, :] = down_t32
    mine[28:32, :] = jnp.zeros((4, width), F32)
    rows[:, 0 : 2 * rank] = down_t32.T
    a = rows[pl.ds(pl.multiple_of(scal[OWN_SHARD] * depth, 8), depth), 0 : 2 * rank]
    for block in range(3):
        piece = w_in[:, block * width : (block + 1) * width]
        if block != 1:
            side = block // 2
            extra = a[:, side * rank : side * rank + 1] * up[side, 0:1, :]
            for i in range(1, rank):
                extra = extra + a[:, side * rank + i : side * rank + i + 1] * up[side, i : i + 1, :]
            piece = (piece.astype(F32) + 2.0 * extra).astype(BF)
        part_a[block * depth : (block + 1) * depth, :] = piece
    part_a[3 * depth : 4 * depth, :] = w_out[...]
    for block in range(4):
        piece = w_up[:, block * width : (block + 1) * width]
        if block < 2:
            part_a[(4 + block) * depth : (5 + block) * depth, :] = piece
        else:
            part_b[(block - 2) * depth : (block - 1) * depth, :] = piece
    part_b[2 * depth : 6 * depth, :] = w_down[...]


def pack(scal, w_in, w_out, w_up, w_down, down_t, up, biases, inner_bias, gains, shifts):
    depth, width = w_out.shape
    shape = jax.ShapeDtypeStruct
    part = shape((6 * depth, width), BF)
    smem = pl.BlockSpec(memory_space=pltpu.SMEM)
    vmem = pl.BlockSpec(memory_space=pltpu.VMEM)
    return pl.pallas_call(
        pack_kernel,
        out_shape=(part, part, shape((PARAM_ROWS, width), F32)),
        in_specs=[smem] + [vmem] * 10,
        out_specs=(vmem, vmem, vmem),
        scratch_shapes=[pltpu.VMEM((width, 128), F32)],
        compiler_params=pltpu.CompilerParams(vmem_limit_bytes=VMEM_BYTES),
        name="pack",
    )(scal, w_in, w_out, w_up, w_down, down_t, up, biases, inner_bias, gains, shifts)


def piece_of(pieces, parity, l, step, side, half):
    if step < 3:
        base = 0 if parity == l else 12
        return pieces[base + (step * 2 + side) * 2 + half]
    if l == 0:
        return pieces[24 + (0 if half == parity else 2) + side]
    return pieces[28 + side * 2 + half]


def rows_of(w, l, block):
    depth = w.shape[2] // 12
    return jnp.concatenate([w[l, j, depth * block : depth * (block + 1), :] for j in range(SHARDS)], axis=0)


def down_of(w, l, block=None):
    depth = w.shape[2] // 12
    shards = range(SHARDS) if block is None else (2 * block, 2 * block + 1)
    return jnp.concatenate([w[l, j, 8 * depth :, :] for j in shards], axis=0)


def part_view(w, l, part):
    rows = w.shape[2] // PARTS
    return w.at[l, :, pl.ds(part * rows, rows)]


def start_part(scal, pieces, w, sem, l, part):
    half_rows = w.shape[2] // 2
    rows = w.shape[2] // PARTS
    begin, end = part * rows, (part + 1) * rows
    for parity in range(2):

        @pl.when(scal[PARITY] == parity)
        def _():
            for i in range(8):
                for half in range(2):
                    low, high = max(begin, half * half_rows), min(end, (half + 1) * half_rows)
                    if low < high:
                        source = piece_of(pieces, parity, l, i // 2, i % 2, half)
                        pltpu.make_async_copy(
                            source.at[pl.ds(low - half * half_rows, high - low)],
                            w.at[l, scal[i], pl.ds(low, high - low)],
                            sem.at[l, part],
                        ).start()


def wait_part(w, sem, l, part):
    view = part_view(w, l, part)
    pltpu.make_async_copy(view, view, sem.at[l, part]).wait()


def take_params(scal, mine, theirs, prm):
    prm[scal[PARITY]] = mine[...]
    prm[1 - scal[PARITY]] = theirs[...]


def label_lanes(lens, row, length):
    places = lax.broadcasted_iota(jnp.int32, (length, 1), 0)
    label = jnp.zeros((length, 1), jnp.int32)
    end = jnp.int32(0)
    segments = lens.shape[1]
    for j in range(segments):
        end = end + lens[row, j]
        label = label + (places >= end).astype(jnp.int32)
    lane = lax.broadcasted_iota(jnp.int32, (1, 128), 1) % 64
    same = label == lane
    used = lane <= segments
    query_lanes = jnp.where(same, 1.0, 0.0).astype(BF)
    key_lanes = jnp.where(same | ~used, 0.0, masked_score).astype(BF)
    return query_lanes, key_lanes


def forward_layer(l, lens_lanes, x, w, prm, act, state, ready, after):
    length, width = x.shape[1:]
    lane = lax.broadcasted_iota(jnp.int32, (1, 128), 1)
    low = lane < 64
    value = x[l]
    ready(0)
    after("begin")
    query = (dot(value, rows_of(w, l, 0)) + prm[l, 0:1, :]).astype(BF)
    keys = dot(value, rows_of(w, l, 1)).astype(BF)
    values = (dot(value, rows_of(w, l, 2)) + prm[l, 1:2, :]).astype(BF)
    if state is not None:
        qkv, shares, mixed_out, n, gp, r = state
        rates = jnp.zeros((length, 128), F32)
        qkv[0] = query
        qkv[1] = keys
        qkv[2] = values
    query_lanes, key_lanes = lens_lanes[0], lens_lanes[1]
    ones = jnp.ones((length, 128), BF)
    mixed = []
    for pair in range(width // 128):
        lanes = slice(128 * pair, 128 * pair + 128)
        scaled = query[:, lanes] * BF(0.125)
        upper = jnp.concatenate([jnp.where(low, scaled, BF(0)), query_lanes], axis=1)
        lower = jnp.concatenate([jnp.where(low, BF(0), scaled), query_lanes], axis=1)
        scores = dot(
            jnp.concatenate([upper, lower], axis=0), jnp.concatenate([keys[:, lanes], key_lanes], axis=1), 1, 1
        )
        top = jnp.max(scores, axis=1, keepdims=True)
        share = jnp.exp(scores - top).astype(BF)
        part = dot(share, jnp.concatenate([values[:, lanes], ones], axis=1))
        over = 1.0 / part[:, 128:129]
        part = part[:, 0:128] * over
        joined = jnp.where(low, part[:length], part[length:])
        if state is not None:
            shares[2 * pair] = share[:length]
            shares[2 * pair + 1] = share[length:]
            mixed_out[:, lanes] = joined
            rates = jnp.where(lane == 2 * pair, over[:length], rates)
            rates = jnp.where(lane == 2 * pair + 1, over[length:], rates)
        mixed.append(joined.astype(BF))
        if pair % 2:
            after(pair // 2)
    mixed = jnp.concatenate(mixed, axis=1)
    ready(1)
    ready(2)
    after("attended")
    halves = [slice(0, length // 2), slice(length // 2, length)]
    firsts, rates_first = [], []
    for rows in halves:
        attended = dot(mixed[rows], rows_of(w, l, 3))
        summed = value[rows].astype(F32) + (attended + prm[l, 2:3, :])
        normal, rate = centre_and_scale(summed)
        firsts.append((normal * prm[l, 8:9, :] + prm[l, 10:11, :]).astype(BF))
        rates_first.append(rate)
        if state is not None:
            n[0, rows] = normal.astype(BF)
    for block in range(4):
        for rows, first in zip(halves, firsts):
            inner = dot(first, rows_of(w, l, 4 + block))
            inner = inner + prm[l, 4 + block : 5 + block, :]
            below = 0.5 + 0.5 * lax.erf(inner * (2**-0.5))
            act[rows, block * width : (block + 1) * width] = (inner * below).astype(BF)
            if state is not None:
                bell = jnp.exp(-0.5 * inner * inner) * 0.3989422804014327
                gp[block, rows] = (below + inner * bell).astype(BF)
    after("inner")
    for rows, first, rate_first in zip(halves, firsts, rates_first):
        branch = dot(act[rows, :], down_of(w, l))
        closing = first.astype(F32) + (branch + prm[l, 3:4, :])
        normal, rate_second = centre_and_scale(closing)
        if state is not None:
            n[1, rows] = normal.astype(BF)
            own = jnp.where(lane == RATE_FIRST, rate_first, rates[rows])
            r[rows] = jnp.where(lane == RATE_SECOND, rate_second, own)
        x[l + 1, rows] = (normal * prm[l, 9:10, :] + prm[l, 11:12, :]).astype(BF)
    after("end")


def backward_layer(l, c_in, c_out, x, w, prm, d_qkv, d_up, state, ready, have, spent, after, together=False):
    qkv, shares, mixed, n, gp, r = state
    length, width = x.shape[1:]
    lane = lax.broadcasted_iota(jnp.int32, (1, 128), 1)
    for part in ("n", "r", "gp"):
        have(part)
    ready(2)
    rates = r[...]
    rate_first = rates[:, RATE_FIRST : RATE_FIRST + 1]
    rate_second = rates[:, RATE_SECOND : RATE_SECOND + 1]
    d_closing = norm_backward(n[1].astype(F32), rate_second, prm[l, 9:10, :], c_in[...].astype(F32))
    d_branch = d_closing.astype(BF)
    total = d_closing
    for block in range(4):
        d_active = dot(d_branch, down_of(w, l, block), 1, 1)
        d_inner = (d_active * gp[block].astype(F32)).astype(BF)
        if block == 0:
            ready(1)
        total = total + dot(d_inner, rows_of(w, l, 4 + block), 1, 1)
        after(("inner", block))
    spent("gp")
    d_summed = norm_backward(n[0].astype(F32), rate_first, prm[l, 8:9, :], total)
    spent("n")
    ready(0)
    d_mixed = dot(d_summed.astype(BF), rows_of(w, l, 3), 1, 1).astype(BF)
    have("mixed")
    have("qkv")
    if together:
        for quad in range(3):
            have(quad)
    low = lane < 64
    for pair in range(width // 128):
        if pair % 2 == 0 and not together:
            have(pair // 2)
        lanes = slice(128 * pair, 128 * pair + 128)
        query, keys, values = qkv[0, :, lanes], qkv[1, :, lanes], qkv[2, :, lanes]
        out_rows = d_mixed[:, lanes].astype(F32)
        upper = jnp.where(low, out_rows * rates[:, 2 * pair : 2 * pair + 1], 0.0)
        lower = jnp.where(low, 0.0, out_rows * rates[:, 2 * pair + 1 : 2 * pair + 2])
        scaled = jnp.concatenate([upper, lower], axis=0).astype(BF)
        mixed_rows = mixed[:, lanes]
        mixed_rows = jnp.concatenate([mixed_rows, mixed_rows], axis=0)
        row_sum = jnp.sum(scaled.astype(F32) * mixed_rows, axis=1, keepdims=True)
        share = jnp.concatenate([shares[2 * pair], shares[2 * pair + 1]], axis=0)
        d_score = (share.astype(F32) * (dot(scaled, values, 1, 1) - row_sum)).astype(BF)
        d_query = dot(d_score, keys)
        queries = jnp.concatenate([jnp.where(low, query, BF(0)), jnp.where(low, BF(0), query)], axis=0)
        d_keys = dot(queries.T, d_score)
        d_values = dot(scaled.T, share)
        d_query = jnp.where(low, d_query[:length], d_query[length:])
        d_qkv[:, lanes] = (d_query * 0.125).astype(BF)
        d_qkv[:, width + 128 * pair : width + 128 * pair + 128] = (d_keys * 0.125).astype(BF).T
        d_qkv[:, 2 * width + 128 * pair : 2 * width + 128 * pair + 128] = d_values.astype(BF).T
        if pair % 2 and not together:
            spent(pair // 2)
            after(pair // 2)
    for part in ("r", "mixed", "qkv") + ((0, 1, 2) if together else ()):
        spent(part)
    total = d_summed
    for kind in range(3):
        total = total + dot(d_qkv[:, kind * width : (kind + 1) * width], rows_of(w, l, kind), 1, 1)
    c_out[...] = total.astype(BF)
    have("x")
    down = dot(x[l], prm[l, 12:28, :].astype(BF), 1, 1).astype(BF)
    rank = down.shape[1] // 2
    d_up[l, 0:rank, :] = 2.0 * dot(down, d_qkv[:, 0:width], 0, 0)[0:rank]
    d_up[l, rank : 2 * rank, :] = 2.0 * dot(down, d_qkv[:, 2 * width : 3 * width], 0, 0)[rank:]


def state_shapes(length, width):
    return [
        ((3, length, width), BF),
        ((HEADS, length, length), BF),
        ((length, width), F32),
        ((2, length, width), BF),
        ((4, length, width), BF),
        ((length, 128), F32),
    ]


def state_copy(state, kept, sem, l, part, load):
    if isinstance(part, int):
        inside, outside = state[1].at[pl.ds(4 * part, 4)], kept[1].at[l, pl.ds(4 * part, 4)]
        which = 5 + part
    else:
        i = {"qkv": 0, "mixed": 2, "n": 3, "gp": 4, "r": 5}[part]
        inside, outside = state[i], kept[i].at[l]
        which = {0: 0, 2: 1, 3: 2, 4: 3, 5: 4}[i]
    ends = (outside, inside) if load else (inside, outside)
    return pltpu.make_async_copy(*ends, sem.at[which])


EARLY_PARTS = ("qkv", "mixed", 0, 1, 2)
INNER_PARTS = ("gp",)
END_PARTS = ("n", "r")
BATCHES = {0: ("qkv", 0), 1: (1,), 2: (2, "mixed"), "inner": INNER_PARTS, "end": END_PARTS}


def save_calls(state, kept, sem, l):
    def after(point):
        if point == "begin":

            @pl.when(l > 0)
            def _():
                for part in EARLY_PARTS:
                    state_copy(state, kept, sem, 0, part, False).wait()

        if point == "attended":

            @pl.when(l > 0)
            def _():
                for part in INNER_PARTS + END_PARTS:
                    state_copy(state, kept, sem, 0, part, False).wait()

    return after


def first_kernel(scal, lens, source, mine, theirs, *refs):
    pieces, refs = refs[:32], refs[32:]
    w_all, out_first, out_second = refs[:3]
    kept, refs = refs[3:9], refs[9:]
    x, w, prm, lanes, act, wsem, osem, xsem, hsem, ssem = refs[:10]
    state = refs[10:]
    parity, stage = scal[PARITY], scal[STAGE]

    def out_copy(l, place):
        return pltpu.make_async_copy(part_view(w, l, place), part_view(w_all, l, place), osem.at[l, place])

    start_part(scal, pieces, w, wsem, 0, 0)

    @pl.when(stage != 0)
    def _():
        for l in range(2):
            for place in range(PARTS):
                if l or place:
                    start_part(scal, pieces, w, wsem, l, place)
        for l in range(2):
            for place in range(PARTS):
                wait_part(w, wsem, l, place)
                out_copy(l, place).start()

    @pl.when(stage == 0)
    def _():
        fresh = pltpu.make_async_copy(source.at[parity], x.at[0], xsem)
        fresh.start()
        take_params(scal, mine, theirs, prm)
        query_lanes, key_lanes = label_lanes(lens, parity, x.shape[1])
        lanes[0] = query_lanes
        lanes[1] = key_lanes
        fresh.wait()

        def layer(l, carry):
            def ready(place):
                wait_part(w, wsem, l, place)

            waits = save_calls(state, kept, ssem, l)

            def after(point):
                waits(point)
                for layer, loads, outs in ((0, FIRST_LOADS, FIRST_OUTS), (1, SECOND_LOADS, SECOND_OUTS)):
                    if point in loads or point in outs:

                        @pl.when(l == layer)
                        def _():
                            for to, part in loads.get(point, ()):
                                start_part(scal, pieces, w, wsem, to, part)
                            for part in outs.get(point, ()):
                                out_copy(layer, part).start()

                for part in BATCHES.get(point, ()):
                    state_copy(state, kept, ssem, l, part, False).start()

            forward_layer(l, lanes, x, w, prm, act, state, ready, after)
            return carry

        lax.fori_loop(0, 2, layer, 0)
        outs = [
            pltpu.make_async_copy(x.at[1], out_first, hsem.at[0]),
            pltpu.make_async_copy(x.at[2], out_second, hsem.at[1]),
        ]
        for copy in outs:
            copy.start()
        for part in EARLY_PARTS + INNER_PARTS + END_PARTS:
            state_copy(state, kept, ssem, 1, part, False).wait()
        for copy in outs:
            copy.wait()

    for l in range(2):
        for place in range(PARTS):
            out_copy(l, place).wait()


OWN_AHEAD = {"begin": (1,), 1: (2,)}
NEXT_AHEAD = {"attended": (0,)}
FIRST_LOADS = {"begin": ((0, 1),), 1: ((0, 2),), "attended": ((1, 0),), "inner": ((1, 1),)}
SECOND_LOADS = {"begin": ((1, 2),)}
FIRST_OUTS = {0: (0,), "attended": (1,), "inner": (2,)}
SECOND_OUTS = {0: (0,), 1: (1,), "attended": (2,)}


def load_weights(w_all, w, wsem, l, places):
    for place in places:
        pltpu.make_async_copy(part_view(w_all, l, place), part_view(w, l, place), wsem.at[l, place]).start()


def load_ahead(w_all, w, wsem, l, point):
    load_weights(w_all, w, wsem, l, OWN_AHEAD.get(point, ()))
    following = NEXT_AHEAD.get(point, ())
    if following:

        @pl.when(l == 0)
        def _():
            load_weights(w_all, w, wsem, 1, following)


def middle_kernel(scal, lens, source, arrived, cotangent, early_first, early_second, mine, theirs, w_all, *refs):
    hop, acts, acts_other, second, second_other, d_up = refs[:6]
    kept, refs = refs[6:12], refs[12:]
    x, w, prm, lanes, act, c, wsem, xsem, hsem, ssem = refs[:10]
    state = refs[10:]
    parity, stage = scal[PARITY], scal[STAGE]
    load_weights(w_all, w, wsem, 0, (0,))
    d_up[...] = jnp.zeros(d_up.shape, F32)
    take_params(scal, mine, theirs, prm)
    query_lanes, key_lanes = label_lanes(lens, parity, x.shape[1])
    lanes[0] = query_lanes
    lanes[1] = key_lanes

    def placed(first, last, own, other, at):
        for p in range(2):

            @pl.when(parity == p)
            def _():
                ends = (first, last) if p == 0 else (last, first)
                pltpu.make_async_copy(ends[0], own.at[p], hsem.at[at]).start()
                pltpu.make_async_copy(ends[1], other, hsem.at[at + 1]).start()

    def placed_wait(own, other, at):
        pltpu.make_async_copy(own.at[0], own.at[0], hsem.at[at]).wait()
        pltpu.make_async_copy(other, other, hsem.at[at + 1]).wait()

    def both(copies):
        for copy in copies:
            copy.start()
        for copy in copies:
            copy.wait()

    @pl.when(stage == 0)
    def _():
        both(
            [
                pltpu.make_async_copy(source.at[parity], x.at[0], xsem.at[0]),
                pltpu.make_async_copy(early_first, c.at[0], xsem.at[1]),
                pltpu.make_async_copy(early_second, c.at[1], xsem.at[2]),
            ]
        )
        placed(c.at[0], c.at[1], acts, acts_other, 0)

    @pl.when(stage != 0)
    def _():
        both(
            [
                pltpu.make_async_copy(arrived, x.at[0], xsem.at[0]),
                pltpu.make_async_copy(cotangent.at[parity], c.at[0], xsem.at[1]),
            ]
        )

    def layer(l, carry):
        def ready(place):
            wait_part(w, wsem, l, place)

        waits = save_calls(state, kept, ssem, l)

        def after(point):
            waits(point)
            load_ahead(w_all, w, wsem, l, point)
            if point in BATCHES:

                @pl.when(l == 0)
                def _():
                    for part in BATCHES[point]:
                        state_copy(state, kept, ssem, 0, part, False).start()

        forward_layer(l, lanes, x, w, prm, act, state, ready, after)
        return carry

    lax.fori_loop(0, 2, layer, 0)

    @pl.when(stage == 0)
    def _():
        up = pltpu.make_async_copy(x.at[2], hop, xsem.at[0])
        up.start()
        placed(x.at[1], x.at[2], second, second_other, 2)
        up.wait()

    @pl.when(stage != 0)
    def _():
        placed(x.at[1], x.at[2], acts, acts_other, 0)

        def gradient(i, carry):
            l = 1 - i

            def have(part):
                if part != "x":

                    @pl.when(i > 0)
                    def _():
                        state_copy(state, kept, ssem, 0, part, True).wait()

            def spent(part):
                @pl.when(i == 0)
                def _():
                    state_copy(state, kept, ssem, 0, part, True).start()

            backward_layer(
                l, c.at[i], c.at[1 - i], x, w, prm, act, d_up, state, lambda place: None, have, spent, lambda point: None, True
            )
            return carry

        lax.fori_loop(0, 2, gradient, 0)
        down = pltpu.make_async_copy(c.at[0], hop, xsem.at[0])
        down.start()
        placed(c.at[0], c.at[1], second, second_other, 2)
        down.wait()

    placed_wait(acts, acts_other, 0)
    placed_wait(second, second_other, 2)


def last_kernel(scal, lens, source, arrived, early_first, second, mine, theirs, w_all, *refs):
    kept, refs = refs[:6], refs[6:]
    joined, grads, other, d_up = refs[:4]
    x, w, prm, lanes, act, c, wsem, xsem, hsem, ssem = refs[4:14]
    state = refs[14:]
    parity, stage = scal[PARITY], scal[STAGE]
    take_params(scal, mine, theirs, prm)
    d_up[...] = jnp.zeros(d_up.shape, F32)

    def carry_in(room):
        return pltpu.make_async_copy(second.at[parity], room, hsem.at[3])

    def carry_out(room, earlier):
        return pltpu.make_async_copy(room, earlier.at[parity], hsem.at[2])

    def finish(first, last, own):
        for p in range(2):

            @pl.when(parity == p)
            def _():
                ends = (first, last) if p == 0 else (last, first)
                copies = [
                    pltpu.make_async_copy(ends[1], other, hsem.at[1]),
                    pltpu.make_async_copy(ends[0], own.at[p], hsem.at[0]),
                ]
                for copy in copies:
                    copy.start()
                for copy in copies:
                    copy.wait()

    @pl.when(stage == 0)
    def _():
        def load(l, part):
            return state_copy(state, kept, ssem, l, part, True)

        cot = pltpu.make_async_copy(arrived, c.at[0], xsem.at[0])
        start_x = pltpu.make_async_copy(source.at[parity], x.at[0], xsem.at[1])
        middle_x = pltpu.make_async_copy(early_first, x.at[1], xsem.at[2])
        cot.start()
        for part in ("n", "r"):
            load(1, part).start()
        load_weights(w_all, w, wsem, 1, (2,))
        load(1, "gp").start()
        load_weights(w_all, w, wsem, 1, (1,))
        cot.wait()

        def gradient(i, carry):
            l = 1 - i

            def have(part):
                if part != "x":
                    load(0, part).wait()
                    return

                @pl.when(i == 0)
                def _():
                    start_x.wait()
                    middle_x.wait()

            def spent(part):
                @pl.when(i == 0)
                def _():
                    load(0, part).start()

            def ready(place):
                wait_part(w, wsem, l, place)

            def after(point):
                key = point[1] if isinstance(point, tuple) else point + 4
                load_weights(w_all, w, wsem, l, ((), (0,), (), (), (), (), ())[key])

                @pl.when(i == 0)
                def _():
                    for part in (("mixed",), ("qkv",), (0,), (1,), (2,), (), ())[key]:
                        load(1, part).start()
                    if key == 4:
                        carry_in(x.at[2]).start()
                        start_x.start()
                        middle_x.start()
                    if key == 5:
                        load_weights(w_all, w, wsem, 0, (2,))
                        carry_in(x.at[2]).wait()
                        carry_out(x.at[2], joined).start()
                    if key == 6:
                        load_weights(w_all, w, wsem, 0, (1,))

            backward_layer(l, c.at[i], c.at[1 - i], x, w, prm, act, d_up, state, ready, have, spent, after)
            return carry

        lax.fori_loop(0, 2, gradient, 0)
        finish(c.at[0], c.at[1], grads)
        carry_out(x.at[2], joined).wait()

    @pl.when(stage != 0)
    def _():
        load_weights(w_all, w, wsem, 0, (0,))
        query_lanes, key_lanes = label_lanes(lens, parity, x.shape[1])
        lanes[0] = query_lanes
        lanes[1] = key_lanes
        copy = pltpu.make_async_copy(arrived, x.at[0], xsem.at[0])
        copy.start()
        copy.wait()
        carry_in(c.at[0]).start()
        carry_in(c.at[0]).wait()
        carry_out(c.at[0], grads).start()

        def layer(l, carry):
            forward_layer(
                l,
                lanes,
                x,
                w,
                prm,
                act,
                None,
                lambda place: wait_part(w, wsem, l, place),
                lambda point: load_ahead(w_all, w, wsem, l, point),
            )
            return carry

        lax.fori_loop(0, 2, layer, 0)
        finish(x.at[1], x.at[2], joined)
        carry_out(c.at[0], grads).wait()


def common_scratch(length, width, rows, extra):
    return (
        [
            pltpu.VMEM((3, length, width), BF),
            pltpu.VMEM((2, SHARDS, 12 * width // SHARDS, width), BF),
            pltpu.VMEM((2, PARAM_ROWS, width), F32),
            pltpu.VMEM((2, length, 128), BF),
            pltpu.VMEM((length, 4 * width), BF),
        ]
        + extra
        + [
            pltpu.SemaphoreType.DMA((3,)),
            pltpu.SemaphoreType.DMA((4,)),
            pltpu.SemaphoreType.DMA((8,)),
        ]
        + [pltpu.VMEM(dims, kind) for dims, kind in state_shapes(length, width)]
    )


def layers_cost(length, width, forwards, backwards):
    dense = 2 * length * width * width * 12
    heads = 2 * length * length * width
    return pl.CostEstimate(
        flops=2 * (forwards * (dense + 2 * heads) + backwards * (dense + 5 * heads)),
        bytes_accessed=2 * 12 * width * width * 2,
        transcendentals=0,
    )


def run_first(scal, lens, source, mine, theirs, pieces):
    _, length, width = source.shape
    shape = jax.ShapeDtypeStruct
    anywhere = pl.BlockSpec(memory_space=pl.ANY)
    smem = pl.BlockSpec(memory_space=pltpu.SMEM)
    vmem = pl.BlockSpec(memory_space=pltpu.VMEM)
    row = shape((length, width), BF)
    outs = [shape((2, SHARDS, 12 * width // SHARDS, width), BF), row, row]
    outs += [shape((2,) + dims, kind) for dims, kind in state_shapes(length, width)]
    scratch = common_scratch(
        length, width, 2, [pltpu.SemaphoreType.DMA((2, PARTS)), pltpu.SemaphoreType.DMA((2, PARTS))]
    )
    scratch[7] = pltpu.SemaphoreType.DMA
    return pl.pallas_call(
        first_kernel,
        out_shape=outs,
        in_specs=[smem, smem, anywhere, vmem, vmem] + [anywhere] * 32,
        out_specs=[anywhere] * len(outs),
        scratch_shapes=scratch,
        compiler_params=pltpu.CompilerParams(vmem_limit_bytes=VMEM_BYTES),
        cost_estimate=layers_cost(length, width, 1, 0),
        name="first",
    )(scal, lens, source, mine, theirs, *pieces)


def run_middle(scal, lens, source, arrived, cotangent, early_first, early_second, mine, theirs, w_all):
    _, length, width = source.shape
    shape = jax.ShapeDtypeStruct
    anywhere = pl.BlockSpec(memory_space=pl.ANY)
    smem = pl.BlockSpec(memory_space=pltpu.SMEM)
    vmem = pl.BlockSpec(memory_space=pltpu.VMEM)
    row, rows = shape((length, width), BF), shape((2, length, width), BF)
    outs = [row, rows, row, rows, row, shape((2, 16, width), F32)]
    outs += [shape((1,) + dims, kind) for dims, kind in state_shapes(length, width)]
    return pl.pallas_call(
        middle_kernel,
        out_shape=outs,
        in_specs=[smem, smem] + [anywhere] * 5 + [vmem, vmem, anywhere],
        out_specs=[anywhere] * 5 + [vmem] + [anywhere] * 6,
        scratch_shapes=common_scratch(
            length,
            width,
            2,
            [pltpu.VMEM((2, length, width), BF), pltpu.SemaphoreType.DMA((2, PARTS))],
        ),
        compiler_params=pltpu.CompilerParams(vmem_limit_bytes=VMEM_BYTES),
        cost_estimate=layers_cost(length, width, 1, 1),
        name="middle",
    )(scal, lens, source, arrived, cotangent, early_first, early_second, mine, theirs, w_all)


def run_last(scal, lens, source, arrived, early_first, second, mine, theirs, w_all, kept):
    _, length, width = source.shape
    shape = jax.ShapeDtypeStruct
    anywhere = pl.BlockSpec(memory_space=pl.ANY)
    smem = pl.BlockSpec(memory_space=pltpu.SMEM)
    vmem = pl.BlockSpec(memory_space=pltpu.VMEM)
    row, rows = shape((length, width), BF), shape((2, length, width), BF)
    return pl.pallas_call(
        last_kernel,
        out_shape=[rows, rows, row, shape((2, 16, width), F32)],
        in_specs=[smem, smem] + [anywhere] * 4 + [vmem, vmem] + [anywhere] * 7,
        out_specs=[anywhere] * 3 + [vmem],
        scratch_shapes=common_scratch(
            length,
            width,
            2,
            [pltpu.VMEM((2, length, width), BF), pltpu.SemaphoreType.DMA((2, PARTS))],
        ),
        compiler_params=pltpu.CompilerParams(vmem_limit_bytes=VMEM_BYTES),
        cost_estimate=layers_cost(length, width, 0, 1),
        name="last",
    )(scal, lens, source, arrived, early_first, second, mine, theirs, w_all, *kept)


def tables(sections, copies):
    group = copies // SHARDS
    out = np.zeros((sections * copies, 12), np.int32)
    for s in range(sections):
        for d in range(copies):
            shard = d // group
            place, side = RING.index(shard // 2), shard % 2
            row = out[s * copies + d]
            for step in range(4):
                node = RING[(place - step) % 4]
                row[2 * step], row[2 * step + 1] = 2 * node + side, 2 * node + 1 - side
            row[PARITY], row[STAGE], row[OWN_SHARD] = s % 2, s // 2, shard
    return out


def body(
    inputs,
    evaluation_input,
    output_cotangent,
    packed_segment_lengths,
    attention_in_weight,
    attention_out_weight,
    feedforward_in_weight,
    feedforward_out_weight,
    adapter_down_weight,
    adapter_up_weight,
    projection_biases,
    feedforward_bias,
    layer_norm_gain,
    layer_norm_shift,
):
    sections, copies = lax.axis_size("section"), lax.axis_size("dp")
    group = copies // SHARDS
    section, place = lax.axis_index("section"), lax.axis_index("dp")
    even = section % 2 == 0
    scal = lax.dynamic_index_in_dim(
        jnp.asarray(tables(sections, copies)), section * copies + place, 0, keepdims=False
    )

    def permuted(array, move):
        pairs = []
        for s in range(sections):
            for d in range(copies):
                target = move(s, d // group)
                if target is not None:
                    pairs.append((s * copies + d, target[0] * copies + target[1] * group + d % group))
        return lax.ppermute(array, AXES, pairs)

    ring_next = {RING[i]: RING[(i + 1) % 4] for i in range(4)}
    ring_last = {RING[i]: RING[i - 1] for i in range(4)}
    along = lambda s, q: (s, ring_next[q // 2] * 2 + q % 2)
    against = lambda s, q: (s, ring_last[q // 2] * 2 + q % 2)
    other_side = lambda s, q: (s, q ^ 1)
    partner = lambda s, q: (s ^ 1, q)
    upward = lambda s, q: (s + 2, q) if s < 2 else None
    across_y = lambda s, q: (s ^ 2, q)

    w_in, w_out, w_up, w_down = (
        attention_in_weight[0],
        attention_out_weight[0],
        feedforward_in_weight[0],
        feedforward_out_weight[0],
    )
    if group > 1:
        groups = [[q * group + i for i in range(group)] for q in range(SHARDS)]
        w_in, w_out, w_up, w_down = (
            lax.all_gather(piece, "dp", axis=0, tiled=True, axis_index_groups=groups)
            for piece in (w_in, w_out, w_up, w_down)
        )
    part_a, part_b, mine = pack(
        scal,
        w_in,
        w_out,
        w_up,
        w_down,
        adapter_down_weight[0].T,
        adapter_up_weight[0],
        projection_biases[0],
        feedforward_bias,
        layer_norm_gain[0],
        layer_norm_shift[0],
    )

    def held_back(array, until):
        return lax.optimization_barrier((array, until))[0]

    r0 = [part_a, part_b]
    x0, r1 = [None, None], [None, None]
    for half in range(2):
        x0[half] = permuted(r0[half], partner)
        r1[half] = permuted(r0[half], along)
    x1, r2 = [None, None], [None, None]
    for half in range(2):
        x1[half] = permuted(held_back(r1[half], x0[half]), partner)
        r2[half] = permuted(r1[half], along)
    z_first = permuted(held_back(jnp.where(even, r0[0], x0[1]), x1[0]), against)
    x2, z_second = [None, None], [None, None]
    for half in range(2):
        x2[half] = permuted(held_back(r2[half], x1[half]), partner)
        second_layer = jnp.where(even, x0[half], r0[half])
        z_second[half] = permuted(held_back(second_layer, z_first if half else r2[1]), against)
    x_first = permuted(held_back(z_first, x2[1]), partner)
    theirs = permuted(held_back(mine, x2[1]), partner)

    def swapped(halves):
        return halves + [permuted(half, other_side) for half in halves]

    pieces = []
    for halves in (r0, r1, r2, x0, x1, x2, [z_first], [x_first], z_second):
        pieces += swapped(halves)

    lens = packed_segment_lengths
    w_all, early_first, early_second, *kept = run_first(scal, lens, inputs, mine, theirs, pieces)
    arrived = permuted(early_second, upward)
    hop, acts, acts_other, second, second_other, d_up_late, *_ = run_middle(
        scal,
        lens,
        evaluation_input,
        arrived,
        output_cotangent,
        early_first,
        early_second,
        mine,
        theirs,
        w_all,
    )
    passed_on = permuted(hop, across_y)
    acts_row = permuted(acts_other, partner)
    second_row = permuted(second_other, partner)
    joined, grads, last_other, d_up_early = run_last(
        scal, lens, inputs, passed_on, early_first, second, mine, theirs, w_all, kept
    )
    last_other, d_up_early, acts_row, second_row = lax.optimization_barrier(
        (last_other, d_up_early, acts_row, second_row)
    )
    last_row = permuted(last_other, partner)
    early = section < 2
    row = 1 - section % 2

    def settled(rows, arrived_row):
        return lax.dynamic_update_slice(rows, arrived_row[None], (row, 0, 0))[None]

    activations = settled(acts, acts_row)
    joined = settled(joined, jnp.where(early, second_row, last_row))
    grads = settled(grads, jnp.where(early, last_row, second_row))

    total = jnp.where(early, d_up_early, d_up_late)
    total = jnp.where(even, total[0], total[1]) + permuted(jnp.where(even, total[1], total[0]), partner)
    for flips in ((1,), (2, 4, 6)):
        total = sum([permuted(total, lambda s, q, flip=flip: (s, q ^ flip)) for flip in flips], total)
    step = 1
    while step < group:
        total = total + lax.ppermute(total, "dp", [(d, d ^ step) for d in range(copies)])
        step *= 2
    total = total.reshape((1, 2, total.shape[0] // 2, total.shape[1]))
    return (activations, grads, total, joined)


def solution(mesh):
    in_specs = (
        P("dp", None, None),
        P("dp", None, None),
        P("dp", None, None),
        P("dp", None),
        P("section", "dp", None),
        P("section", "dp", None),
        P("section", "dp", None),
        P("section", "dp", None),
        P("section", None, None),
        P("section", None, None, None),
        P("section", None, None),
        P("section", None),
        P("section", None, None),
        P("section", None, None),
    )
    out_specs = (
        P("section", "dp", None, None),
        P("section", "dp", None, None),
        P("section", None, None, None),
        P("section", "dp", None, None),
    )
    return jax.shard_map(body, mesh=mesh, in_specs=in_specs, out_specs=out_specs, check_vma=False)
```
